32 devices in a mesh: elem: 8 (over z, y), sub: 4 (over x, core).
Axes of the slice: x: 2, y: 2, z: 4, core: 2. Of those that a mesh axis runs over, the one named last changes fastest.
Arguments:
- gcm_state: float32 [8192, 576], P(('elem', 'sub')), may hold values from -6 to 6
- edge_part: float32 [2048, 4, 144], P(('elem', 'sub')), may hold values from -6 to 6
- neighbours: int32 [2048, 4], P(('elem', 'sub')), may hold values from 0 to 8191, as said below
- branch: int32 [8192], P(('elem', 'sub')), may hold values 0 or 1
- routes: int32 [8192, 1], P(('elem', 'sub')), may hold values from 0 to 31; in each aligned block of 256 rows (0 to 255, 256 to 511, ...) at most 16 rows name the same one
- crm_state: float32 [2, 48, 32, 16384], P(None, None, None, ('elem', 'sub')), may hold values from -6 to 6
Outputs:
- tendency: float32 [8192, 576], P(('elem', 'sub'))
- crm_out: float32 [2, 48, 32, 16384], P(None, None, None, ('elem', 'sub'))
- span_precip: float32 [32, 512], P(('elem', 'sub'))
The draws below stay inside these ranges and needn't reach their ends.
Inputs may be any that keep to these rules, and one draw needn't show every extreme that they name: `neighbours`: each edge names an edge of an element on the same device or on the device just before or after it in the order of elem+sub, wrapping around. `routes`: among the 256 columns of one device no owner is named more than 16 times, a bound that some block reaches.
All inputs are finite; a program needn't handle non-finite values. No bound on the sum of `branch` on one device may be relied on, other than what follows from the above.
Results may differ from the reference program's by a relative error of at most 0.0003.
Values sent between devices are 32-bit elements; how exact they have to be, the bound alone decides.
No kernel may reach another device: no remote copies, remote signals or barrier semaphores. Data moves between devices by JAX's collectives and lax.ppermute only.
A program may use at most 128 MiB of HBM per device.

```python
import math
import jax
import jax.numpy as jnp
import numpy as np
from jax import lax

E_DEV = 64
NV = 8
L = 72
CZ = 48
CX = 32
STEPS = 3
PEERS = 32
COL_DEV = 256
CAP = 16
ELEMENTS = 2048
COLUMNS = 8192
SLOTS_ALL = 16384


def draw_neighbours(key, part):
    key = jax.random.fold_in(key, 7)
    first, second, third = jax.random.split(key, 3)
    owner_dev = jnp.arange(ELEMENTS, dtype=jnp.int32) // E_DEV
    moved = jax.random.randint(first, (ELEMENTS, 4), -1, 2)
    device_of = (owner_dev[:, None] + moved + PEERS) % PEERS
    local_elem = jax.random.randint(second, (ELEMENTS, 4), 0, E_DEV)
    edge_of = jax.random.randint(third, (ELEMENTS, 4), 0, 4)
    return ((device_of * E_DEV + local_elem) * 4 + edge_of).astype(jnp.int32)


def place_ends(drawn, own_key, smallest, largest):
    dims = drawn.shape
    index_at = [jax.random.randint(jax.random.fold_in(own_key, axis), (), 0, dims[axis]) for axis in range(len(dims))]
    drawn = drawn.at[tuple(index_at)].set(smallest)
    longest = dims.index(max(dims))
    index_at[longest] = (index_at[longest] + 1) % dims[longest]
    return drawn.at[tuple(index_at)].set(largest)


def level_of(own_key, extent, cuts, low, largest):
    level, own = 1.0, jax.random.fold_in(own_key, 6)
    for dim, shards_of in cuts:
        heights = jnp.exp(jax.random.uniform(jax.random.fold_in(own, dim), (shards_of,), jnp.float32, low / len(cuts), largest / len(cuts)))
        level = level * jnp.repeat(heights, extent[dim] // shards_of).reshape([-1 if axis == dim else 1 for axis in range(len(extent))])
    return level


def routed_block(key, own, number, rows, count, top, most, lean):
    order = jax.random.permutation(key, count)
    packed, usual = load_shares(count, rows * top, most, lean, True), load_shares(count, rows * top, most, lean, False)
    places = jnp.arange(count)

    def named(sizes, turn):
        used = int((sizes > 0).sum())
        fixed = max(1, used // 4)
        passed = fixed + (places - fixed + turn * (used - fixed)) % max(1, count - fixed)
        return jnp.zeros((count,), jnp.int32).at[order[jnp.where(places < fixed, places, passed)]].set(jnp.asarray(sizes, jnp.int32))

    sizes = jnp.where(number % 4 == 0, named(packed, number // 4), named(usual, number - number // 4 - 1))
    mixed = jax.random.permutation(jax.random.fold_in(own, 3), count)
    giver, sink = mixed[0:count // 2 * 2:2], mixed[1:count // 2 * 2:2]
    slack = jnp.minimum(sizes[giver] - 1, most - sizes[sink]) // 2
    slack = jnp.where((giver == order[0]) | (sink == order[0]) | (sizes[sink] == 0), 0, jnp.maximum(slack, 0))
    passed = jax.random.randint(jax.random.fold_in(own, 4), (count // 2,), 0, 1 << 20) % (slack + 1)
    sizes = sizes.at[giver].add(-passed).at[sink].add(passed)
    members = jnp.searchsorted(jnp.cumsum(sizes), jnp.arange(rows * top), side="right").astype(jnp.int32)
    table = members.reshape(top, rows).T
    table = table[jax.random.permutation(jax.random.fold_in(own, 1), rows)]
    turn = jax.random.randint(jax.random.fold_in(own, 2), (rows, 1), 0, top)
    return jnp.take_along_axis(table, (jnp.arange(top)[None, :] + turn) % top, axis=1)


def load_shares(count, total, bound, lean, full):
    loads = [(1 << 20) // math.isqrt(rank ** lean) + 1 for rank in range(1, count + 1)]
    largest = bound if full else min(bound, max(-(-total // count), total * loads[0] // sum(loads)))
    least = 1 if total - largest >= count - 1 else 0
    holding, spare = [largest] + [least] * (count - 1), total - largest - least * (count - 1)
    while spare > 0:
        free = [i for i in range(1, count) if holding[i] < largest] or [i for i in range(1, count) if holding[i] < bound]
        pool, remaining = sum([loads[i] for i in free]), spare
        for i in free:
            extra = min(bound - holding[i], max(1, remaining * loads[i] // pool), spare)
            holding[i] = holding[i] + extra
            spare = spare - extra
    return np.array(holding)


def gaussian(key, shape, deviation, most, cuts=(), held_as=jnp.bfloat16):
    drawn = deviation * jax.random.normal(key, shape, jnp.float32)
    if cuts:
        drawn = drawn * level_of(key, shape, cuts, -0.22, 0.18)
    return jnp.clip(drawn, -most, most).astype(held_as)


def setup_inputs(seed: int = 0) -> dict:
    arg_keys = jax.random.split(jax.random.key(seed), 7)
    gcm_state = gaussian(arg_keys[0], (COLUMNS, NV * L), 1.0, 6.0, ((0, 32),), jnp.float32)
    edge_part = gaussian(arg_keys[1], (ELEMENTS, 4, 2 * L), 1.0, 6.0, ((0, 32),), jnp.float32)
    neighbours = draw_neighbours(jax.random.fold_in(arg_keys[6], 71), 0)
    branch = place_ends((jax.random.randint(arg_keys[3], (COLUMNS,), 0, 2) < 1).astype(jnp.int32), jax.random.fold_in(arg_keys[3], 1), 0, 1)
    routes_keys = jax.random.split(jax.random.fold_in(arg_keys[4], 1), COLUMNS // COL_DEV)
    routes_turns = jax.random.permutation(jax.random.fold_in(arg_keys[4], 3), COLUMNS // COL_DEV)
    routes = jax.vmap(lambda own, number: routed_block(jax.random.fold_in(arg_keys[4], 2), own, number, COL_DEV, PEERS, 1, CAP, 2))(routes_keys, routes_turns).reshape((COLUMNS, 1))
    crm_state = gaussian(arg_keys[5], (2, CZ, CX, SLOTS_ALL), 1.0, 6.0, ((3, 32),), jnp.float32)
    return dict(gcm_state=gcm_state, edge_part=edge_part, neighbours=neighbours, branch=branch, routes=routes, crm_state=crm_state)


viscosity = 0.2
timestep = 0.5

def tables(levels, crm_levels):
    position = jnp.arange(crm_levels, dtype=jnp.float32) * (levels - 1) / (crm_levels - 1)
    interp = jnp.maximum(0.0, 1.0 - jnp.abs(position[:, None] - jnp.arange(levels, dtype=jnp.float32)[None, :]))
    field_ids = jnp.arange(NV)
    parity = jnp.where((field_ids[None, :] + jnp.arange(2)[:, None]) % 2 == 0, 1.0, -1.0)
    mixing = ((0.8 + 0.05 * field_ids.astype(jnp.float32))[None, :] * parity / jnp.sqrt(jnp.float32(NV))).astype(jnp.float32)
    return (interp, mixing)

def laplace(values):
    upper = jnp.concatenate([values[1:], values[-1:]], axis=0)
    lower = jnp.concatenate([values[:1], values[:-1]], axis=0)
    return jnp.roll(values, 1, axis=1) + jnp.roll(values, -1, axis=1) + upper + lower - 4.0 * values

def respond(fields, slot_codes, crm_now):
    slot_count = fields.shape[0]
    levels = fields.shape[1] // NV
    crm_levels = crm_now.shape[1]
    interp, mixing = tables(levels, crm_levels)
    grouped = fields.reshape(slot_count, NV, levels)
    mixed_fields = jnp.einsum('vk,skl->vls', mixing, grouped, precision=lax.Precision.HIGHEST)
    force = jnp.einsum('zl,vls->vzs', interp, mixed_fields, precision=lax.Precision.HIGHEST)
    cond_rate = 0.15 + 0.25 * (slot_codes == 2).astype(jnp.float32)
    saturation = (1.0 - 2.0 * jnp.arange(crm_levels, dtype=jnp.float32) / (crm_levels - 1))[:, None, None]
    heat_field = crm_now[0]
    moist_field = crm_now[1]
    rainfall = jnp.zeros((slot_count,), jnp.float32)
    for substep in range(STEPS):
        heat_next = heat_field + viscosity * laplace(heat_field) + timestep * force[0][:, None, :]
        moist_next = moist_field + viscosity * laplace(moist_field) + timestep * force[1][:, None, :]
        condensed = cond_rate * jax.nn.softplus(moist_next - 0.3 * heat_next - saturation)
        heat_field = heat_next + 0.5 * condensed
        moist_field = moist_next - condensed
        rainfall = rainfall + lax.optimization_barrier(jnp.mean(condensed, axis=(0, 1)))
    updated = jnp.stack([heat_field, moist_field])
    change = lax.optimization_barrier(jnp.mean(updated - crm_now, axis=2))
    returned = jnp.einsum('zl,vzs->vls', interp, change, precision=lax.Precision.HIGHEST)
    slot_tendency = jnp.einsum('vk,vls->skl', mixing, returned, precision=lax.Precision.HIGHEST).reshape(slot_count, -1)
    occupied = slot_codes > 0
    updated = jnp.where(occupied[None, None, None, :], updated, crm_now)
    rainfall = jnp.where(occupied, rainfall, 0.0)
    return (updated, slot_tendency, rainfall)

def one_block(pieces):
    return respond(pieces[0], pieces[1], pieces[2])

def reference(gcm_state, edge_part, neighbours, branch, routes, crm_state):
    flattened = edge_part.reshape(ELEMENTS * 4, -1)
    summed = (flattened + flattened[neighbours.reshape(-1)]).reshape(ELEMENTS, 4, -1)
    paired = summed + jnp.roll(summed, -1, axis=1)
    edge_width = paired.shape[2]
    grouped = gcm_state.reshape(ELEMENTS, 4, -1)
    columns = jnp.concatenate([grouped[:, :, :edge_width] + 0.25 * paired, grouped[:, :, edge_width:]], axis=2).reshape(COLUMNS, -1)
    destination = routes[:, 0].reshape(PEERS, COL_DEV)
    onehot = (destination[:, :, None] == jnp.arange(PEERS, dtype=jnp.int32)[None, None, :]).astype(jnp.int32)
    before = jnp.cumsum(onehot, axis=1) - onehot
    slot_rank = lax.optimization_barrier(jnp.sum(before * onehot, axis=2))
    source = jnp.arange(PEERS, dtype=jnp.int32)[:, None]
    slot_index = (destination * (PEERS * CAP) + source * CAP + slot_rank).reshape(-1).astype(jnp.int32)
    fields_all = jnp.zeros((SLOTS_ALL, columns.shape[1]), jnp.float32).at[slot_index].set(columns)
    codes_all = jnp.zeros((SLOTS_ALL,), jnp.int32).at[slot_index].set(branch + 1)
    block_size = PEERS * CAP
    stacked = crm_state.reshape(2, CZ, CX, PEERS, block_size).transpose(3, 0, 1, 2, 4)
    updated, slot_tendency, rainfall = lax.map(one_block, (fields_all.reshape(PEERS, block_size, -1), codes_all.reshape(PEERS, block_size), stacked))
    crm_out = updated.transpose(1, 2, 3, 0, 4).reshape(2, CZ, CX, SLOTS_ALL)
    tendency = slot_tendency.reshape(SLOTS_ALL, -1)[slot_index]
    span_precip = rainfall.reshape(PEERS, PEERS * CAP)
    return (tendency, crm_out, span_precip)
```

```python
import functools

import jax
import jax.numpy as jnp
import numpy as np
from jax import lax
from jax.experimental import pallas as pl
from jax.experimental.pallas import tpu as pltpu
from jax.sharding import PartitionSpec as P

NV = 8
STEPS = 3
AXES = ("elem", "sub")
LANES = 128
HALF = 64
LOG2E = 1.4426950408889634
LN2 = 0.6931471805599453
F32 = jnp.float32
BF16 = jnp.bfloat16
HIGHEST = lax.Precision.HIGHEST
SMALL_RAIN = 1e-3


def tables(levels, crm_levels):
    position = np.arange(crm_levels, dtype=np.float64) * (levels - 1) / (crm_levels - 1)
    interp = np.maximum(0.0, 1.0 - np.abs(position[:, None] - np.arange(levels)[None, :]))
    field_ids = np.arange(NV)
    parity = np.where(field_ids % 2 == 0, 1.0, -1.0)
    return interp, (0.8 + 0.05 * field_ids) * parity / np.sqrt(float(NV))


def dot(a, b, contract, precision=None):
    return lax.dot_general(
        a, b, ((contract[0:1], contract[1:2]), ((), ())),
        precision=precision, preferred_element_type=F32,
    )


def split(x):
    high = x.astype(BF16)
    return high, (x - high.astype(F32)).astype(BF16)


def pick(onehot, x, contract):
    high, low = split(x)
    return dot(onehot, high, contract) + dot(onehot, low, contract)


def iota(shape, dim):
    return lax.broadcasted_iota(jnp.int32, shape, dim)


def full(shape):
    return pl.BlockSpec(shape, lambda *_: (0,) * len(shape))


def edges_kernel(edge_ref, weight_ref, out_ref):
    parts = [
        dot(weight_ref[...], edge_ref[:, j, :], (1, 1), HIGHEST) for j in range(4)
    ]
    out_ref[...] = jnp.concatenate(parts, axis=1)


def route_kernel(peers, capacity, me_ref, routes_ref, branch_ref, neigh_ref, gcm_ref, weight_ref,
                 own_ref, pos_ref, base_ref, halo_map_ref):
    columns = routes_ref.shape[1]
    elems = columns // 4
    crm_levels = own_ref.shape[0]
    slots = peers * capacity
    half = capacity // 2
    me = me_ref[0]
    destination = routes_ref[...]
    named = iota((peers, columns), 0) == destination
    earlier = (iota((columns, columns), 0) < iota((columns, columns), 1)).astype(BF16)
    before = dot(named.astype(BF16), earlier, (1, 0))
    rank = jnp.sum(jnp.where(named, before, 0.0), axis=0, keepdims=True).astype(jnp.int32)
    upper = (rank >= half).astype(jnp.int32)
    position = upper * (slots // 2) + destination * half + rank - upper * half
    pos_ref[...] = position
    place = (iota((slots, columns), 0) == position).astype(BF16)

    target = jnp.concatenate([neigh_ref[j : j + 1, :] for j in range(4)], axis=1)
    owner = target // columns
    edge = target - owner * columns
    block = jnp.where(owner == me, 0, jnp.where(owner == (me ^ 1), 1, 2))
    source = block * columns + (edge % 4) * elems + edge // 4
    window = iota((3 * columns, columns), 0)
    chosen = (window == source).astype(F32) + (window == iota((3 * columns, columns), 1)).astype(F32)
    column = iota((columns, columns), 0)
    row = iota((columns, columns), 1)
    first = (column % 4) * elems + column // 4
    second = ((column + 1) % 4) * elems + column // 4
    pair = ((row == first) | (row == second)).astype(BF16)
    mapped = dot(pair, chosen.astype(BF16), (1, 1)).astype(BF16)
    halo_map_ref[...] = dot(place, mapped[:, columns:], (1, 0)).astype(BF16)

    own_high, own_low = split(own_ref[...])
    local = mapped[:, :columns]
    force = dot(weight_ref[...], gcm_ref[...], (1, 0), HIGHEST)
    force += 0.25 * (dot(own_high, local, (1, 1)) + dot(own_low, local, (1, 1)))
    code = (branch_ref[...] + 1).astype(F32)
    fields = jnp.concatenate(
        [force, code, jnp.zeros((HALF - crm_levels - 1, columns), F32)], axis=0
    )
    both = pick(place, fields, (1, 1))
    base_ref[...] = jnp.concatenate([both[: slots // 2], both[slots // 2 :]], axis=1)


def outgoing_kernel(base_ref, map_ref, pair_ref, other_ref, out_ref):
    crm_levels = pair_ref.shape[0]
    window = jnp.concatenate([pair_ref[...], other_ref[...]], axis=1)
    window = jnp.concatenate([window, jnp.zeros((HALF - crm_levels, window.shape[1]), F32)], axis=0)
    both = 0.25 * pick(map_ref[...], window, (1, 1))
    rows = out_ref.shape[0]
    out_ref[...] = base_ref[...] + jnp.concatenate([both[:rows], both[rows:]], axis=1)


def neighbours_sum(row, up, down, count):
    sums = []
    for k in range(count):
        left = row[k - 1] if k else pltpu.roll(row[count - 1], 1, 0)
        right = row[k + 1] if k + 1 < count else pltpu.roll(row[0], 7, 0)
        sums.append((row[k] + left) + (right + (up[k] + down[k])))
    return sums


def sweep(ref, z, crm_levels, count):
    low = jnp.maximum(z - 1, 0)
    high = jnp.minimum(z + 1, crm_levels - 1)
    rows = [[ref[at, k] for k in range(count)] for at in (z, low, high)]
    return neighbours_sum(*rows, count)


def add_up(values):
    while len(values) > 1:
        values = [a + b for a, b in zip(values[::2], values[1::2])]
    return values[0]


def rows_of_sums(ref, crm_levels):
    return add_up([ref[pl.ds(s, crm_levels, stride=8), :] for s in range(8)])


def saturation_at(z, crm_levels):
    return 1.0 - z.astype(F32) * (2.0 / (crm_levels - 1))


def before_kernel(state_ref, first_ref, sums_ref, g_ref, part_ref):
    _, crm_levels, width, _ = state_ref.shape
    count = width // 8

    def load(z, _):
        fixed = LOG2E * saturation_at(z, crm_levels)
        heat = [state_ref[0, z, pl.ds(k, 8, stride=count), :] for k in range(count)]
        moist = [state_ref[1, z, pl.ds(k, 8, stride=count), :] for k in range(count)]
        for k in range(count):
            g_ref[z, k] = LOG2E * moist[k] - (0.3 * LOG2E) * heat[k] - fixed
        at = pl.multiple_of(z * 8, 8)
        part_ref[0, pl.ds(at, 8), :] = add_up(heat)
        part_ref[1, pl.ds(at, 8), :] = add_up(moist)
        return 0

    lax.fori_loop(0, crm_levels, load, 0, unroll=8)

    def step(z, _):
        for k, total in enumerate(sweep(g_ref, z, crm_levels, count)):
            first_ref[z, k] = 0.2 * total
        return 0

    lax.fori_loop(0, crm_levels, step, 0, unroll=8)
    heat = rows_of_sums(part_ref.at[0], crm_levels) * (1.0 / width)
    moist = rows_of_sums(part_ref.at[1], crm_levels) * (1.0 / width)
    level = saturation_at(iota((crm_levels, LANES), 0), crm_levels)
    sums_ref[0] = LOG2E * (moist - 0.3 * heat - level)
    sums_ref[1] = 2.0 * heat + moist


def lane_maps(rows, capacity):
    half = capacity // 2
    row = iota((rows, LANES), 0)
    slot = iota((rows, LANES), 1)
    rank = slot % capacity
    low = (row == (slot // capacity) * half + rank) & (rank < half)
    high = (row == (slot // capacity) * half + rank - half) & (rank >= half)
    return low.astype(BF16), high.astype(BF16)


def received(arrived, capacity):
    low, high = lane_maps(arrived.shape[0], capacity)
    first, second = split(arrived)
    lower = dot(first, low, (0, 0)) + dot(second, low, (0, 0))
    upper = dot(first, high, (0, 0)) + dot(second, high, (0, 0))
    return lower[:HALF] + upper[HALF:]


def rates(code):
    return 0.15 + 0.25 * (code == 2.0).astype(F32)


def cloud_kernel(capacity, arrived_ref, first_ref, sums_ref, last_ref, reply_ref, rain_ref,
                 a_ref, b_ref, push_ref, part_ref):
    crm_levels, count = first_ref.shape[:2]
    cells = crm_levels * count * 8
    got = received(arrived_ref[...], capacity)
    force = got[:crm_levels]
    code = got[crm_levels : crm_levels + 1]
    level = iota((crm_levels, LANES), 0)
    edge = (0.4 / (crm_levels - 1)) * LOG2E
    bound = jnp.where(level == 0, -edge, 0.0) + jnp.where(level == crm_levels - 1, edge, 0.0)
    push_ref[...] = (-0.65 * LOG2E) * force + bound
    rate = rates(code)
    lowered = jnp.broadcast_to(1.15 * rate, (8, LANES))

    def run(exact):
        def condense(y):
            e = jnp.exp2(y)
            u = 1.0 + e
            amount = jnp.log2(u)
            if exact:
                amount = jnp.where(e < 2.0**-8, (LOG2E * e) * (1.0 - 0.5 * e), amount)
            return amount, y - lowered * amount

        def first(z, acc):
            push = jnp.broadcast_to(push_ref[pl.ds(z, 1), :], (8, LANES))
            new = []
            for k in range(count):
                amount, g = condense(first_ref[z, k] + push)
                a_ref[z, k] = g
                new.append(acc[k] + amount)
            return tuple(new)

        def later(src, dst, last):
            def body(z, acc):
                push = jnp.broadcast_to(push_ref[pl.ds(z, 1), :], (8, LANES))
                new, out = [], []
                for k, total in enumerate(sweep(src, z, crm_levels, count)):
                    amount, g = condense(0.2 * total + push)
                    dst[z, k] = g
                    out.append(g)
                    new.append(acc[k] + amount)
                if last:
                    part_ref[pl.ds(pl.multiple_of(z * 8, 8), 8), :] = add_up(out)
                return tuple(new)
            return body

        acc = tuple(jnp.zeros((8, LANES), F32) for _ in range(count))
        acc = lax.fori_loop(0, crm_levels, first, acc, unroll=8)
        acc = lax.fori_loop(0, crm_levels, later(a_ref, b_ref, False), acc, unroll=8)
        acc = lax.fori_loop(0, crm_levels, later(b_ref, last_ref, True), acc, unroll=8)
        mean = jnp.sum(add_up(list(acc)), axis=0, keepdims=True) * (1.0 / cells)
        rain_ref[...] = jnp.where(code > 0.0, (rate * LN2) * mean, 0.0)
        return mean

    mean = run(False)

    @pl.when(jnp.min(mean) < SMALL_RAIN)
    def _():
        run(True)

    dg = rows_of_sums(part_ref, crm_levels) * (1.0 / (count * 8)) - sums_ref[0]
    start = sums_ref[1]
    q = start
    for _ in range(STEPS):
        up = jnp.concatenate([q[:1], q[:-1]], axis=0)
        down = jnp.concatenate([q[1:], q[-1:]], axis=0)
        q = 0.6 * q + 0.2 * (up + down) + 0.5 * force
    answer = (0.7 / 2.3) * (q - start) - (3.0 / (2.3 * LOG2E)) * dg
    answer = jnp.concatenate([answer, jnp.zeros((HALF - crm_levels, LANES), F32)], axis=0)
    low, high = lane_maps(arrived_ref.shape[0], capacity)
    reply_ref[...] = jnp.concatenate([pick(low, answer, (1, 1)), pick(high, answer, (1, 1))], axis=1)


def after_kernel(capacity, arrived_ref, last_ref, state_ref, out_ref, a_ref, b_ref, push_ref):
    _, crm_levels, width, _ = state_ref.shape
    count = width // 8
    got = received(arrived_ref[...], capacity)
    occupied = jnp.broadcast_to(got[crm_levels : crm_levels + 1], (8, LANES)) > 0.0
    push_ref[...] = 2.5 * got[:crm_levels]

    def load(z, _):
        for k in range(count):
            at = pl.ds(k, 8, stride=count)
            a_ref[z, k] = 2.0 * state_ref[0, z, at, :] + state_ref[1, z, at, :]
        return 0

    def step(src, dst, scale):
        def body(z, _):
            push = jnp.broadcast_to(scale * push_ref[pl.ds(z, 1), :], (8, LANES))
            for k, total in enumerate(sweep(src, z, crm_levels, count)):
                dst[z, k] = total + push
            return 0
        return body

    def finish(z, _):
        push = jnp.broadcast_to(25.0 * push_ref[pl.ds(z, 1), :], (8, LANES))
        fixed = saturation_at(z, crm_levels)
        for k, total in enumerate(sweep(a_ref, z, crm_levels, count)):
            at = pl.ds(k, 8, stride=count)
            dry = (1.0 / LOG2E) * last_ref[z, k] + fixed
            heat = (1.0 / (125.0 * 2.3)) * (total + push) - (1.0 / 2.3) * dry
            moist = dry + 0.3 * heat
            out_ref[0, z, at, :] = jnp.where(occupied, heat, state_ref[0, z, at, :])
            out_ref[1, z, at, :] = jnp.where(occupied, moist, state_ref[1, z, at, :])
        return 0

    lax.fori_loop(0, crm_levels, load, 0, unroll=8)
    lax.fori_loop(0, crm_levels, step(a_ref, b_ref, 1.0), 0, unroll=8)
    lax.fori_loop(0, crm_levels, step(b_ref, a_ref, 5.0), 0, unroll=8)
    lax.fori_loop(0, crm_levels, finish, 0, unroll=8)


def tendency_kernel(pos_ref, returned_ref, weight_ref, out_ref):
    rows = returned_ref.shape[0]
    columns = pos_ref.shape[1]
    place = (iota((2 * rows, columns), 0) == pos_ref[...]).astype(BF16)
    high, low = split(returned_ref[...])
    lower = dot(high, place[:rows], (0, 0)) + dot(low, place[:rows], (0, 0))
    upper = dot(high, place[rows:], (0, 0)) + dot(low, place[rows:], (0, 0))
    out_ref[...] = dot(weight_ref[...], lower[:HALF] + upper[HALF:], (1, 0), HIGHEST)


def call(kernel, out, grid=None, in_specs=None, out_specs=None, scratch=(), cost=(0, 0, 0), vmem=32):
    extra = {} if grid is None else dict(grid=grid, in_specs=in_specs, out_specs=out_specs)
    return pl.pallas_call(
        kernel, out_shape=out, scratch_shapes=list(scratch),
        cost_estimate=pl.CostEstimate(flops=int(cost[0]), bytes_accessed=int(cost[1]), transcendentals=int(cost[2])),
        compiler_params=pltpu.CompilerParams(vmem_limit_bytes=vmem * 2**20), **extra,
    )


def on_device(gcm_state, edge_part, neighbours, branch, routes, crm_state):
    peers = lax.axis_size(AXES)
    me = lax.axis_index(AXES)
    columns, features = gcm_state.shape
    levels = features // NV
    _, crm_levels, width, slots = crm_state.shape
    capacity = slots // peers
    count = width // 8
    blocks = slots // LANES
    rows = slots // 2
    part = rows // blocks
    interp, mixing = tables(levels, crm_levels)
    weight = np.concatenate([mixing[k] * interp for k in range(NV)], axis=1).astype(np.float32)
    edge_weight = weight[:, : edge_part.shape[2]]
    back = np.zeros((features, HALF), np.float32)
    back[:, :crm_levels] = weight.T
    shape = jax.ShapeDtypeStruct

    own = call(edges_kernel, shape((crm_levels, columns), F32), cost=(1e7, 4e5, 0))(
        edge_part, jnp.asarray(edge_weight)
    )
    pair = lax.ppermute(own, AXES, [(i, i ^ 1) for i in range(peers)])
    other = lax.ppermute(own, AXES, [(i, (((i + 1) ^ 1) - 1) % peers) for i in range(peers)])
    smem = pl.BlockSpec(memory_space=pltpu.SMEM)
    vmem = pl.BlockSpec(memory_space=pltpu.VMEM)
    position, base, halo_map = pl.pallas_call(
        functools.partial(route_kernel, peers, capacity),
        out_shape=(
            shape((1, columns), jnp.int32),
            shape((rows, LANES), F32),
            shape((slots, 2 * columns), BF16),
        ),
        in_specs=[smem] + [vmem] * 6,
        out_specs=[vmem] * 3,
        cost_estimate=pl.CostEstimate(flops=int(2e9), bytes_accessed=int(2e6), transcendentals=0),
        compiler_params=pltpu.CompilerParams(vmem_limit_bytes=32 * 2**20),
    )(me.reshape(1), routes.T, branch.reshape(1, -1), neighbours.T, gcm_state.T, jnp.asarray(weight), own)
    outgoing = call(outgoing_kernel, shape((rows, LANES), F32), cost=(2e8, 1e6, 0))(base, halo_map, pair, other)

    field = (crm_levels, count, 8, LANES)
    state_spec = pl.BlockSpec((2, crm_levels, width, LANES), lambda j: (0, 0, 0, j))
    field_spec = pl.BlockSpec(field, lambda j: (0, 0, 0, j))
    sums_spec = pl.BlockSpec((2, crm_levels, LANES), lambda j: (0, 0, j))
    rows_spec = pl.BlockSpec((part, LANES), lambda j: (j, 0))
    whole_field = shape((crm_levels, count, 8, slots), F32)
    cells = crm_levels * width * slots
    first, sums = call(
        before_kernel, (whole_field, shape((2, crm_levels, slots), F32)), (blocks,),
        [state_spec], [field_spec, sums_spec],
        [pltpu.VMEM(field, F32), pltpu.VMEM((2, crm_levels * 8, LANES), F32)],
        (cells * 10, cells * 12, 0),
    )(crm_state)

    arrived = lax.all_to_all(outgoing.reshape(peers, capacity // 2, LANES), AXES, 0, 0, tiled=True)
    arrived = arrived.reshape(rows, LANES)
    last, reply, rain = call(
        functools.partial(cloud_kernel, capacity),
        (whole_field, shape((rows, LANES), F32), shape((1, slots), F32)), (blocks,),
        [rows_spec, field_spec, sums_spec],
        [field_spec, rows_spec, pl.BlockSpec((1, LANES), lambda j: (0, j))],
        [pltpu.VMEM(field, F32), pltpu.VMEM(field, F32), pltpu.VMEM((crm_levels, LANES), F32),
         pltpu.VMEM((crm_levels * 8, LANES), F32)],
        (cells * 30, cells * 8, cells * 6),
    )(arrived, first, sums)
    returned = lax.all_to_all(reply.reshape(peers, capacity // 2, LANES), AXES, 0, 0, tiled=True)
    updated = call(
        functools.partial(after_kernel, capacity), shape(crm_state.shape, F32), (blocks,),
        [rows_spec, field_spec, state_spec], state_spec,
        [pltpu.VMEM(field, F32), pltpu.VMEM(field, F32), pltpu.VMEM((crm_levels, LANES), F32)],
        (cells * 30, cells * 20, 0),
    )(arrived, last, crm_state)
    tendency = call(tendency_kernel, shape((features, columns), F32), cost=(1e8, 1e6, 0))(
        position, returned.reshape(rows, LANES), jnp.asarray(back)
    )
    return (tendency.T, updated, rain)


def solution(mesh):
    in_specs = (
        P(AXES, None),
        P(AXES, None, None),
        P(AXES, None),
        P(AXES),
        P(AXES, None),
        P(None, None, None, AXES),
    )
    out_specs = (
        P(AXES, None),
        P(None, None, None, AXES),
        P(AXES, None),
    )
    return jax.shard_map(
        on_device, mesh=mesh, in_specs=in_specs, out_specs=out_specs, check_vma=False
    )
```

```python
import functools

import jax
import jax.numpy as jnp
import numpy as np
from jax import lax
from jax.experimental import pallas as pl
from jax.experimental.pallas import tpu as pltpu
from jax.sharding import PartitionSpec as P

NV = 8
STEPS = 3
AXES = ("elem", "sub")
LANES = 128
HALF = 64
LOG2E = 1.4426950408889634
F32 = jnp.float32
BF16 = jnp.bfloat16
HIGHEST = lax.Precision.HIGHEST
SMALL_RAIN = 1e-3


def tables(levels, crm_levels):
    position = np.arange(crm_levels, dtype=np.float64) * (levels - 1) / (crm_levels - 1)
    interp = np.maximum(0.0, 1.0 - np.abs(position[:, None] - np.arange(levels)[None, :]))
    field_ids = np.arange(NV)
    parity = np.where(field_ids % 2 == 0, 1.0, -1.0)
    return interp, (0.8 + 0.05 * field_ids) * parity / np.sqrt(float(NV))


def dot(a, b, contract, precision=None):
    return lax.dot_general(
        a, b, ((contract[0:1], contract[1:2]), ((), ())),
        precision=precision, preferred_element_type=F32,
    )


def split(x):
    high = x.astype(BF16)
    return high, (x - high.astype(F32)).astype(BF16)


def pick(onehot, x, contract):
    high, low = split(x)
    return dot(onehot, high, contract) + dot(onehot, low, contract)


def iota(shape, dim):
    return lax.broadcasted_iota(jnp.int32, shape, dim)


def full(shape):
    return pl.BlockSpec(shape, lambda *_: (0,) * len(shape))


def edges_kernel(edge_ref, weight_ref, out_ref):
    parts = [
        dot(weight_ref[...], edge_ref[:, j, :], (1, 1), HIGHEST) for j in range(4)
    ]
    out_ref[...] = jnp.concatenate(parts, axis=1)


def route_kernel(peers, capacity, me_ref, routes_ref, branch_ref, neigh_ref, gcm_ref, weight_ref,
                 own_ref, pos_ref, base_ref, halo_map_ref):
    columns = routes_ref.shape[1]
    elems = columns // 4
    crm_levels = own_ref.shape[0]
    slots = peers * capacity
    half = capacity // 2
    me = me_ref[0]
    destination = routes_ref[...]
    named = iota((peers, columns), 0) == destination
    earlier = (iota((columns, columns), 0) < iota((columns, columns), 1)).astype(BF16)
    before = dot(named.astype(BF16), earlier, (1, 0))
    rank = jnp.sum(jnp.where(named, before, 0.0), axis=0, keepdims=True).astype(jnp.int32)
    upper = (rank >= half).astype(jnp.int32)
    position = upper * (slots // 2) + destination * half + rank - upper * half
    pos_ref[...] = position
    place = (iota((slots, columns), 0) == position).astype(BF16)

    target = jnp.concatenate([neigh_ref[j : j + 1, :] for j in range(4)], axis=1)
    owner = target // columns
    edge = target - owner * columns
    block = jnp.where(owner == me, 0, jnp.where(owner == (me ^ 1), 1, 2))
    source = block * columns + (edge % 4) * elems + edge // 4
    window = iota((3 * columns, columns), 0)
    chosen = (window == source).astype(F32) + (window == iota((3 * columns, columns), 1)).astype(F32)
    column = iota((columns, columns), 0)
    row = iota((columns, columns), 1)
    first = (column % 4) * elems + column // 4
    second = ((column + 1) % 4) * elems + column // 4
    pair = ((row == first) | (row == second)).astype(BF16)
    mapped = dot(pair, chosen.astype(BF16), (1, 1)).astype(BF16)
    halo_map_ref[...] = dot(place, mapped[:, columns:], (1, 0)).astype(BF16)

    own_high, own_low = split(own_ref[...])
    local = mapped[:, :columns]
    force = dot(weight_ref[...], gcm_ref[...], (1, 0), HIGHEST)
    force += 0.25 * (dot(own_high, local, (1, 1)) + dot(own_low, local, (1, 1)))
    code = (branch_ref[...] + 1).astype(F32)
    fields = jnp.concatenate(
        [force, code, jnp.zeros((HALF - crm_levels - 1, columns), F32)], axis=0
    )
    both = pick(place, fields, (1, 1))
    base_ref[...] = jnp.concatenate([both[: slots // 2], both[slots // 2 :]], axis=1)


def outgoing_kernel(base_ref, map_ref, pair_ref, other_ref, out_ref):
    crm_levels = pair_ref.shape[0]
    window = jnp.concatenate([pair_ref[...], other_ref[...]], axis=1)
    window = jnp.concatenate([window, jnp.zeros((HALF - crm_levels, window.shape[1]), F32)], axis=0)
    both = 0.25 * pick(map_ref[...], window, (1, 1))
    rows = out_ref.shape[0]
    out_ref[...] = base_ref[...] + jnp.concatenate([both[:rows], both[rows:]], axis=1)


def five_points(rows, z):
    row, up, down = rows[z], rows[max(z - 1, 0)], rows[min(z + 1, len(rows) - 1)]
    count = len(row)
    ring = [pltpu.roll(row[-1], 1, 0)] + row + [pltpu.roll(row[0], 7, 0)]
    pairs = [row[k] + row[k + 1] for k in range(0, count, 2)]
    return [
        (pairs[k // 2] + ring[k if k % 2 == 0 else k + 2]) + (up[k] + down[k]) for k in range(count)
    ]


def add_up(values):
    while len(values) > 1:
        values = [a + b for a, b in zip(values[::2], values[1::2])]
    return values[0]


def rows_of_sums(ref, crm_levels):
    return add_up([ref[pl.ds(s, crm_levels, stride=8), :] for s in range(8)])


def saturation(z, crm_levels):
    return 1.0 - z * (2.0 / (crm_levels - 1))


def levels_of(crm_levels):
    return iota((crm_levels, LANES), 0)


def shifted(x):
    return jnp.concatenate([x[:1], x[:-1]], axis=0) + jnp.concatenate([x[1:], x[-1:]], axis=0)


def before_kernel(state_ref, kept_ref, first_ref, linear_ref, sums_ref, part_ref, sems):
    blocks, _, crm_levels, width, _ = kept_ref.shape
    count = width // 8

    def copy(j):
        lanes = pl.ds(pl.multiple_of(j * LANES, LANES), LANES)
        return pltpu.make_async_copy(state_ref.at[:, :, :, lanes], kept_ref.at[j], sems.at[j])

    for j in range(blocks):
        copy(j).start()

    def block(j, _):
        copy(j).wait()
        dry = []
        fields = [[] for _ in range(STEPS + 1)]
        for i in range(crm_levels + STEPS):
            if i < crm_levels:
                heat = [kept_ref[j, 0, i, pl.ds(k, 8, stride=count), :] for k in range(count)]
                moist = [kept_ref[j, 1, i, pl.ds(k, 8, stride=count), :] for k in range(count)]
                dry.append([m - 0.3 * h for h, m in zip(heat, moist)])
                fields[0].append([(h + h) + m for h, m in zip(heat, moist)])
                part_ref[0, pl.ds(8 * i, 8), :] = add_up(dry[i])
                part_ref[1, pl.ds(8 * i, 8), :] = add_up(fields[0][i])
            z = i - 1
            if 0 <= z < crm_levels:
                for k, total in enumerate(five_points(dry, z)):
                    first_ref[j, z, k] = (0.2 * LOG2E) * total
            for t in range(1, STEPS + 1):
                z = i - t
                if 0 <= z < crm_levels:
                    fields[t].append(five_points(fields[t - 1], z))
            if 0 <= z < crm_levels:
                for k, total in enumerate(fields[STEPS][z]):
                    linear_ref[j, z, k] = (1.0 / 125.0) * total
        level = saturation(levels_of(crm_levels).astype(F32), crm_levels)
        dry_mean = rows_of_sums(part_ref.at[0], crm_levels) * (1.0 / width)
        sums_ref[j, 0] = LOG2E * (dry_mean - level)
        sums_ref[j, 1] = rows_of_sums(part_ref.at[1], crm_levels) * (1.0 / width)
        return 0

    lax.fori_loop(0, blocks, block, 0)


def lane_maps(rows, capacity):
    half = capacity // 2
    row = iota((rows, LANES), 0)
    slot = iota((rows, LANES), 1)
    rank = slot % capacity
    low = (row == (slot // capacity) * half + rank) & (rank < half)
    high = (row == (slot // capacity) * half + rank - half) & (rank >= half)
    return low.astype(BF16), high.astype(BF16)


def received(arrived, low, high):
    first, second = split(arrived)
    lower = dot(first, low, (0, 0)) + dot(second, low, (0, 0))
    upper = dot(first, high, (0, 0)) + dot(second, high, (0, 0))
    return lower[:HALF] + upper[HALF:]


def cloud_kernel(capacity, arrived_ref, first_ref, sums_ref, last_ref, row_ref, occupied_ref,
                 reply_ref, rain_ref, got_ref, push_ref, part_ref, field_ref):
    blocks, crm_levels, count = first_ref.shape[:3]
    cells = crm_levels * count * 8
    part = arrived_ref.shape[0] // blocks
    low, high = lane_maps(part, capacity)
    for j in range(blocks):
        got_ref[j] = received(arrived_ref[pl.ds(j * part, part), :], low, high)
    level = levels_of(crm_levels)
    edge = (0.4 / (crm_levels - 1)) * LOG2E
    bound = jnp.where(level == 0, -edge, 0.0) + jnp.where(level == crm_levels - 1, edge, 0.0)
    dried = LOG2E * saturation(level.astype(F32), crm_levels)

    def block(j, _):
        force = got_ref[j, :crm_levels, :]
        code = got_ref[j, crm_levels : crm_levels + 1, :]
        rate = 0.15 + 0.25 * (code == 2.0).astype(F32)
        lowered = jnp.broadcast_to((1.15 * LOG2E) * rate, (8, LANES))
        push = (-0.65 * LOG2E) * force
        push_ref[0] = push - dried
        push_ref[1] = push + bound

        def finish(acc):
            mean = jnp.sum(add_up(list(acc)), axis=0, keepdims=True) * (1.0 / cells)
            rain_ref[j] = jnp.where(code > 0.0, rate * mean, 0.0)
            return mean

        def pushed(step, z):
            return jnp.broadcast_to(push_ref[min(step, 1), pl.ds(z, 1), :], (8, LANES))

        fields = [[] for _ in range(STEPS)]
        acc = [jnp.zeros((8, LANES), F32) for _ in range(count)]
        for i in range(crm_levels + STEPS - 1):
            for t in range(STEPS):
                z = i - t
                if not 0 <= z < crm_levels:
                    continue
                push = pushed(t, z)
                if t == 0:
                    values = [first_ref[j, z, k] + push for k in range(count)]
                else:
                    values = [0.2 * total + push for total in five_points(fields[t - 1], z)]
                amounts = [jnp.log(1.0 + jnp.exp2(y)) for y in values]
                acc = [a + amount for a, amount in zip(acc, amounts)]
                values = [y - lowered * amount for y, amount in zip(values, amounts)]
                fields[t].append(values)
                if t == STEPS - 1:
                    for k in range(count):
                        last_ref[j, z, k] = values[k]
                    part_ref[pl.ds(8 * z, 8), :] = add_up(values)
        mean = finish(acc)

        @pl.when(jnp.min(mean) < SMALL_RAIN)
        def _():
            def condense(z, k, y, acc, store):
                e = jnp.exp2(y)
                amount = jnp.where(e < 2.0**-8, e * (1.0 - 0.5 * e), jnp.log(1.0 + e))
                store[z, k] = y - lowered * amount
                return acc + amount

            def first(z, acc):
                push = pushed(0, z)
                return tuple(
                    condense(z, k, first_ref[j, z, k] + push, acc[k], field_ref.at[0]) for k in range(count)
                )

            def later(source, target):
                def body(z, acc):
                    push = pushed(1, z)
                    at = (z, jnp.maximum(z - 1, 0), jnp.minimum(z + 1, crm_levels - 1))
                    row, up, down = [[source[y, k] for k in range(count)] for y in at]
                    totals = five_points([up, row, down], 1)
                    return tuple(
                        condense(z, k, 0.2 * totals[k] + push, acc[k], target) for k in range(count)
                    )
                return body

            acc = tuple(jnp.zeros((8, LANES), F32) for _ in range(count))
            acc = lax.fori_loop(0, crm_levels, first, acc)
            acc = lax.fori_loop(0, crm_levels, later(field_ref.at[0], field_ref.at[1]), acc)
            acc = lax.fori_loop(0, crm_levels, later(field_ref.at[1], last_ref.at[j]), acc)

            def totals(z, _):
                at = pl.ds(pl.multiple_of(8 * z, 8), 8)
                part_ref[at, :] = add_up([last_ref[j, z, k] for k in range(count)])
                return 0

            lax.fori_loop(0, crm_levels, totals, 0)
            finish(acc)

        dg = rows_of_sums(part_ref, crm_levels) * (1.0 / (count * 8)) - sums_ref[j, 0]
        start = sums_ref[j, 1]
        q, response = start, jnp.zeros_like(start)
        for _ in range(STEPS):
            q = 0.6 * q + 0.2 * shifted(q) + 0.5 * force
            response = 0.6 * response + 0.2 * shifted(response) + 0.5 * force
        row_ref[j] = response
        occupied_ref[j] = code
        answer = (0.7 / 2.3) * (q - start) - (3.0 / (2.3 * LOG2E)) * dg
        answer = jnp.concatenate([answer, jnp.zeros((HALF - crm_levels, LANES), F32)], axis=0)
        reply = jnp.concatenate([pick(low, answer, (1, 1)), pick(high, answer, (1, 1))], axis=1)
        reply_ref[pl.ds(pl.multiple_of(j * part, part), part), :] = reply
        return 0

    lax.fori_loop(0, blocks, block, 0)


def after_kernel(kept_ref, last_ref, linear_ref, row_ref, occupied_ref, out_ref, new_ref, sems):
    blocks, _, crm_levels, width, _ = kept_ref.shape
    count = width // 8

    def copy(j):
        lanes = pl.ds(pl.multiple_of(j * LANES, LANES), LANES)
        return pltpu.make_async_copy(new_ref.at[j], out_ref.at[:, :, :, lanes], sems.at[j])

    def block(j, _):
        occupied = jnp.broadcast_to(occupied_ref[j], (8, LANES)) > 0.0
        for z in range(crm_levels):
            row = jnp.broadcast_to(row_ref[j, pl.ds(z, 1), :], (8, LANES))
            for k in range(count):
                at = pl.ds(k, 8, stride=count)
                linear = linear_ref[j, z, k] + row
                dry = (1.0 / LOG2E) * last_ref[j, z, k] + saturation(z, crm_levels)
                heat = (1.0 / 2.3) * (linear - dry)
                moist = dry + 0.3 * heat
                new_ref[j, 0, z, at, :] = jnp.where(occupied, heat, kept_ref[j, 0, z, at, :])
                new_ref[j, 1, z, at, :] = jnp.where(occupied, moist, kept_ref[j, 1, z, at, :])
        copy(j).start()
        return 0

    lax.fori_loop(0, blocks, block, 0)
    for j in range(blocks):
        copy(j).wait()


def tendency_kernel(pos_ref, returned_ref, weight_ref, out_ref):
    rows = returned_ref.shape[0]
    columns = pos_ref.shape[1]
    place = (iota((2 * rows, columns), 0) == pos_ref[...]).astype(BF16)
    high, low = split(returned_ref[...])
    lower = dot(high, place[:rows], (0, 0)) + dot(low, place[:rows], (0, 0))
    upper = dot(high, place[rows:], (0, 0)) + dot(low, place[rows:], (0, 0))
    out_ref[...] = dot(weight_ref[...], lower[:HALF] + upper[HALF:], (1, 0), HIGHEST)


def call(kernel, out, scratch=(), cost=(0, 0, 0), vmem=32, **specs):
    return pl.pallas_call(
        kernel, out_shape=out, scratch_shapes=list(scratch),
        cost_estimate=pl.CostEstimate(flops=int(cost[0]), bytes_accessed=int(cost[1]), transcendentals=int(cost[2])),
        compiler_params=pltpu.CompilerParams(vmem_limit_bytes=vmem * 2**20), **specs,
    )


def from_hbm(*arrays):
    return [pltpu.with_memory_space_constraint(x, pltpu.HBM) for x in arrays]


def cloud_before(crm_state):
    _, crm_levels, width, slots = crm_state.shape
    blocks = slots // LANES
    cells = crm_levels * width * slots
    field = (blocks, crm_levels, width // 8, 8, LANES)
    return call(
        before_kernel,
        (
            pltpu.VMEM((blocks, 2, crm_levels, width, LANES), F32),
            pltpu.VMEM(field, F32),
            pltpu.VMEM(field, F32),
            pltpu.VMEM((blocks, 2, crm_levels, LANES), F32),
        ),
        [pltpu.VMEM((2, crm_levels * 8, LANES), F32), pltpu.SemaphoreType.DMA((blocks,))],
        (cells * 25, cells * 8, 0),
        in_specs=[pl.BlockSpec(memory_space=pltpu.HBM)],
        out_specs=[pl.BlockSpec(memory_space=pltpu.VMEM)] * 4,
    )(*from_hbm(crm_state))


def cloud_steps(capacity, arrived, first, sums):
    blocks, crm_levels, count = first.shape[:3]
    slots = blocks * LANES
    cells = crm_levels * count * 8 * slots
    return call(
        functools.partial(cloud_kernel, capacity),
        (
            pltpu.VMEM(first.shape, F32),
            pltpu.VMEM((blocks, crm_levels, LANES), F32),
            pltpu.VMEM((blocks, 1, LANES), F32),
            jax.ShapeDtypeStruct(arrived.shape, F32),
            jax.ShapeDtypeStruct((blocks, 1, LANES), F32),
        ),
        [
            pltpu.VMEM((blocks, HALF, LANES), F32),
            pltpu.VMEM((2, crm_levels, LANES), F32),
            pltpu.VMEM((crm_levels * 8, LANES), F32),
            pltpu.VMEM((2,) + first.shape[1:], F32),
        ],
        (cells * 30, cells * 8, cells * 6),
        in_specs=[pl.BlockSpec(memory_space=pltpu.VMEM)] * 3,
        out_specs=[pl.BlockSpec(memory_space=pltpu.VMEM)] * 5,
    )(arrived, first, sums)


def cloud_after(kept, last, linear, row, occupied):
    blocks, _, crm_levels, width, _ = kept.shape
    slots = blocks * LANES
    cells = crm_levels * width * slots
    return call(
        after_kernel,
        jax.ShapeDtypeStruct((2, crm_levels, width, slots), F32),
        [pltpu.VMEM(kept.shape, F32), pltpu.SemaphoreType.DMA((blocks,))],
        (cells * 10, cells * 8, 0),
        in_specs=[pl.BlockSpec(memory_space=pltpu.VMEM)] * 5,
        out_specs=pl.BlockSpec(memory_space=pltpu.HBM),
    )(kept, last, linear, row, occupied)


def on_device(gcm_state, edge_part, neighbours, branch, routes, crm_state):
    peers = lax.axis_size(AXES)
    me = lax.axis_index(AXES)
    columns, features = gcm_state.shape
    levels = features // NV
    _, crm_levels, width, slots = crm_state.shape
    capacity = slots // peers
    rows = slots // 2
    interp, mixing = tables(levels, crm_levels)
    weight = np.concatenate([mixing[k] * interp for k in range(NV)], axis=1).astype(np.float32)
    edge_weight = weight[:, : edge_part.shape[2]]
    back = np.zeros((features, HALF), np.float32)
    back[:, :crm_levels] = weight.T
    shape = jax.ShapeDtypeStruct

    own = call(edges_kernel, shape((crm_levels, columns), F32), cost=(1e7, 4e5, 0))(
        *from_hbm(edge_part, jnp.asarray(edge_weight))
    )
    pair = lax.ppermute(own, AXES, [(i, i ^ 1) for i in range(peers)])
    other = lax.ppermute(own, AXES, [(i, (((i + 1) ^ 1) - 1) % peers) for i in range(peers)])
    smem = pl.BlockSpec(memory_space=pltpu.SMEM)
    vmem = pl.BlockSpec(memory_space=pltpu.VMEM)
    position, base, halo_map = call(
        functools.partial(route_kernel, peers, capacity),
        (
            shape((1, columns), jnp.int32),
            shape((rows, LANES), F32),
            shape((slots, 2 * columns), BF16),
        ),
        cost=(2e9, 2e6, 0),
        in_specs=[smem] + [vmem] * 6,
        out_specs=[vmem] * 3,
    )(
        me.reshape(1),
        *from_hbm(routes.T, branch.reshape(1, -1), neighbours.T, gcm_state.T, jnp.asarray(weight)),
        own,
    )
    outgoing = call(outgoing_kernel, shape((rows, LANES), F32), cost=(2e8, 1e6, 0))(base, halo_map, pair, other)
    kept, first, linear, sums = cloud_before(crm_state)
    arrived = lax.all_to_all(outgoing.reshape(peers, capacity // 2, LANES), AXES, 0, 0, tiled=True)
    last, row, occupied, reply, rain = cloud_steps(capacity, arrived.reshape(rows, LANES), first, sums)
    returned = lax.all_to_all(reply.reshape(peers, capacity // 2, LANES), AXES, 0, 0, tiled=True)
    updated = cloud_after(kept, last, linear, row, occupied)
    tendency = call(tendency_kernel, shape((features, columns), F32), cost=(1e8, 1e6, 0))(
        position, returned.reshape(rows, LANES), *from_hbm(jnp.asarray(back))
    )
    return (tendency.T, updated, rain.reshape(1, slots))


def solution(mesh):
    in_specs = (
        P(AXES, None),
        P(AXES, None, None),
        P(AXES, None),
        P(AXES),
        P(AXES, None),
        P(None, None, None, AXES),
    )
    out_specs = (
        P(AXES, None),
        P(None, None, None, AXES),
        P(AXES, None),
    )
    return jax.shard_map(
        on_device, mesh=mesh, in_specs=in_specs, out_specs=out_specs, check_vma=False
    )
```

```python
import functools

import jax
import jax.numpy as jnp
import numpy as np
from jax import lax
from jax.experimental import pallas as pl
from jax.experimental.pallas import tpu as pltpu
from jax.sharding import PartitionSpec as P

NV = 8
STEPS = 3
AXES = ("elem", "sub")
LANES = 128
HALF = 64
LOG2E = 1.4426950408889634
F32 = jnp.float32
BF16 = jnp.bfloat16
HIGHEST = lax.Precision.HIGHEST
SMALL_RAIN = 0.2


def mixing(k):
    return (0.8 + 0.05 * k) * (1.0 if k % 2 == 0 else -1.0) / float(np.sqrt(float(NV)))


def interp(z, level, crm_levels, levels):
    position = z.astype(F32) * ((levels - 1) / (crm_levels - 1))
    return jnp.maximum(0.0, 1.0 - jnp.abs(position - level.astype(F32)))


def dot(a, b, contract, precision=None):
    return lax.dot_general(
        a, b, ((contract[0:1], contract[1:2]), ((), ())),
        precision=precision, preferred_element_type=F32,
    )


def split(x):
    high = x.astype(BF16)
    return high, (x - high.astype(F32)).astype(BF16)


def both_halves(x):
    high, low = split(x)
    return jnp.concatenate([high, low], axis=0)


def slot_rows(onehot, fields):
    product = dot(onehot, both_halves(fields), (1, 1))
    product = product + pltpu.roll(product, HALF, 1)
    rows = product.shape[0] // 2
    return jnp.where(iota((rows, 2 * HALF), 1) < HALF, product[:rows], product[rows:])


def padded(fields):
    return jnp.concatenate([fields, jnp.zeros((HALF - fields.shape[0], fields.shape[1]), F32)], axis=0)


def iota(shape, dim):
    return lax.broadcasted_iota(jnp.int32, shape, dim)


def edges_kernel(edge_ref, out_ref):
    crm_levels = out_ref.shape[0]
    shape = (crm_levels, edge_ref.shape[2])
    levels = shape[1] // 2
    lane = iota(shape, 1)
    weight = jnp.where(
        lane < levels,
        mixing(0) * interp(iota(shape, 0), lane, crm_levels, levels),
        mixing(1) * interp(iota(shape, 0), lane - levels, crm_levels, levels),
    )
    parts = [dot(weight, edge_ref[:, j, :], (1, 1), HIGHEST) for j in range(4)]
    out_ref[...] = jnp.concatenate(parts, axis=1)


def route_kernel(peers, capacity, me_ref, routes_ref, branch_ref, neigh_ref, gcm_ref, own_ref,
                 pos_ref, base_ref, halo_map_ref):
    columns = routes_ref.shape[1]
    elems = columns // 4
    crm_levels = own_ref.shape[0]
    slots = peers * capacity
    half = capacity // 2
    me = me_ref[0]
    destination = routes_ref[...]
    named = iota((peers, columns), 0) == destination
    earlier = (iota((columns, columns), 0) < iota((columns, columns), 1)).astype(BF16)
    before = dot(named.astype(BF16), earlier, (1, 0))
    rank = jnp.sum(jnp.where(named, before, 0.0), axis=0, keepdims=True).astype(jnp.int32)
    upper = (rank >= half).astype(jnp.int32)
    position = upper * (slots // 2) + destination * half + rank - upper * half
    pos_ref[...] = position
    place = (iota((slots, columns), 0) == position).astype(BF16)

    target = jnp.concatenate([neigh_ref[j : j + 1, :] for j in range(4)], axis=1)
    owner = target // columns
    edge = target - owner * columns
    block = jnp.where(owner == me, 0, jnp.where(owner == (me ^ 1), 1, 2))
    source = block * columns + (edge % 4) * elems + edge // 4
    window = iota((3 * columns, columns), 0)
    chosen = (window == source).astype(F32) + (window == iota((3 * columns, columns), 1)).astype(F32)
    column = iota((columns, columns), 0)
    row = iota((columns, columns), 1)
    first = (column % 4) * elems + column // 4
    second = ((column + 1) % 4) * elems + column // 4
    pair = ((row == first) | (row == second)).astype(BF16)
    mapped = dot(pair, chosen.astype(BF16), (1, 1)).astype(BF16)
    halo_map_ref[...] = dot(place, mapped[:, columns:], (1, 0)).astype(BF16)

    own_high, own_low = split(own_ref[...])
    local = mapped[:, :columns]
    levels = gcm_ref.shape[0] // NV
    mixed = mixing(0) * gcm_ref[:levels, :]
    for k in range(1, NV):
        mixed += mixing(k) * gcm_ref[pl.ds(k * levels, levels), :]
    shape = (crm_levels, levels)
    force = dot(interp(iota(shape, 0), iota(shape, 1), crm_levels, levels), mixed, (1, 0), HIGHEST)
    force += 0.25 * (dot(own_high, local, (1, 1)) + dot(own_low, local, (1, 1)))
    code = (branch_ref[...] + 1).astype(F32)
    base_ref[...] = slot_rows(place, padded(jnp.concatenate([force, code], axis=0)))


def outgoing_kernel(base_ref, map_ref, pair_ref, other_ref, out_ref):
    window = jnp.concatenate([pair_ref[...], other_ref[...]], axis=1)
    out_ref[...] = base_ref[...] + 0.25 * slot_rows(map_ref[...], padded(window))


def five_points(rows, z):
    row, up, down = rows[z], rows[max(z - 1, 0)], rows[min(z + 1, len(rows) - 1)]
    count = len(row)
    ring = [pltpu.roll(row[-1], 1, 0)] + row + [pltpu.roll(row[0], 7, 0)]
    pairs = [row[k] + row[k + 1] for k in range(0, count, 2)]
    return [
        (pairs[k // 2] + ring[k if k % 2 == 0 else k + 2]) + (up[k] + down[k]) for k in range(count)
    ]


def add_up(values):
    while len(values) > 1:
        values = [a + b for a, b in zip(values[::2], values[1::2])]
    return values[0]


def rows_of_sums(ref, crm_levels):
    return add_up([ref[pl.ds(s, crm_levels, stride=8), :] for s in range(8)])


def saturation(z, crm_levels):
    return 1.0 - z * (2.0 / (crm_levels - 1))


def levels_of(crm_levels):
    return iota((crm_levels, LANES), 0)


def shifted(x):
    return jnp.concatenate([x[:1], x[:-1]], axis=0) + jnp.concatenate([x[1:], x[-1:]], axis=0)


def before_kernel(state_ref, first_ref, sums_ref, kept_ref, part_ref, sems):
    blocks, _, crm_levels, width, _ = kept_ref.shape
    count = width // 8

    def copy(j):
        lanes = pl.ds(pl.multiple_of(j * LANES, LANES), LANES)
        return pltpu.make_async_copy(state_ref.at[:, :, :, lanes], kept_ref.at[j], sems.at[j])

    for j in range(blocks):
        copy(j).start()

    def block(j, _):
        copy(j).wait()
        dry = []
        for i in range(crm_levels + 1):
            if i < crm_levels:
                heat = [kept_ref[j, 0, i, pl.ds(k, 8, stride=count), :] for k in range(count)]
                moist = [kept_ref[j, 1, i, pl.ds(k, 8, stride=count), :] for k in range(count)]
                dry.append([m - 0.3 * h for h, m in zip(heat, moist)])
                part_ref[0, pl.ds(8 * i, 8), :] = add_up(dry[i])
                part_ref[1, pl.ds(8 * i, 8), :] = add_up(heat)
            if i:
                for k, total in enumerate(five_points(dry, i - 1)):
                    first_ref[j, i - 1, k] = (0.2 * LOG2E) * total
        level = saturation(levels_of(crm_levels).astype(F32), crm_levels)
        dry_mean = rows_of_sums(part_ref.at[0], crm_levels) * (1.0 / width)
        start = dry_mean + rows_of_sums(part_ref.at[1], crm_levels) * (2.3 / width)
        q = start
        for _ in range(STEPS):
            q = 0.6 * q + 0.2 * shifted(q)
        sums_ref[j, 0] = LOG2E * (dry_mean - level)
        sums_ref[j, 1] = q - start
        return 0

    lax.fori_loop(0, blocks, block, 0)


def lane_maps(rows, capacity):
    half = capacity // 2
    row = iota((rows, LANES), 0)
    slot = iota((rows, LANES), 1)
    rank = slot % capacity
    low = (row == (slot // capacity) * half + rank) & (rank < half)
    high = (row == (slot // capacity) * half + rank - half) & (rank >= half)
    return low.astype(BF16), high.astype(BF16)


def cloud_kernel(capacity, arrived_ref, first_ref, sums_ref, last_ref, row_ref, occupied_ref,
                 reply_ref, rain_ref, push_ref, part_ref, field_ref):
    blocks, crm_levels, count = first_ref.shape[:3]
    width = count * 8
    part = arrived_ref.shape[0] // blocks
    low, high = lane_maps(part, capacity)
    level = levels_of(crm_levels)
    edge = (0.4 / (crm_levels - 1)) * LOG2E
    bound = jnp.where(level == 0, -edge, 0.0) + jnp.where(level == crm_levels - 1, edge, 0.0)
    dried = LOG2E * saturation(level.astype(F32), crm_levels)
    maps = jnp.concatenate([low, high], axis=1)
    maps = jnp.concatenate([maps, maps], axis=0)
    for j in range(blocks):
        got = dot(both_halves(arrived_ref[pl.ds(j * part, part), :]), maps, (0, 0))
        got = got[:HALF, :LANES] + got[HALF:, LANES:]
        push = (-0.65 * LOG2E) * got[:crm_levels]
        push_ref[j, 0] = push - dried
        push_ref[j, 1] = push + bound
        occupied_ref[j] = got[crm_levels : crm_levels + 1]
        response = jnp.zeros((crm_levels, LANES), F32)
        for _ in range(STEPS):
            response = 0.6 * response + 0.2 * shifted(response) + 0.5 * got[:crm_levels]
        row_ref[j] = response

    def rate_of(j):
        return 0.15 + 0.25 * (occupied_ref[j] == 2.0).astype(F32)

    def lowering(j):
        return jnp.broadcast_to((1.15 * LOG2E) * rate_of(j), (8, LANES))

    def pushed(j, step, z):
        return jnp.broadcast_to(push_ref[j, min(step, 1), pl.ds(z, 1), :], (8, LANES))

    def block(j, _):
        lowered = lowering(j)
        fields = [[] for _ in range(STEPS)]
        for i in range(crm_levels + STEPS - 1):
            for t in range(STEPS):
                z = i - t
                if not 0 <= z < crm_levels:
                    continue
                push = pushed(j, t, z)
                if t == 0:
                    values = [first_ref[j, z, k] + push for k in range(count)]
                else:
                    values = [0.2 * total + push for total in five_points(fields[t - 1], z)]
                values = [y - lowered * jnp.log(1.0 + jnp.exp2(y)) for y in values]
                fields[t].append(values)
                if t == STEPS - 1:
                    for k in range(count):
                        last_ref[j, z, k] = values[k]
                    part_ref[j, pl.ds(8 * z, 8), :] = add_up(values)
        return 0

    lax.fori_loop(0, blocks, block, 0)

    def again(j):
        lowered = lowering(j)

        def condense(z, k, y, acc, store):
            e = jnp.exp2(y)
            amount = jnp.where(e < 2.0**-8, e * (1.0 - 0.5 * e), jnp.log(1.0 + e))
            store[z, k] = y - lowered * amount
            return acc + amount

        def first(z, acc):
            push = pushed(j, 0, z)
            return tuple(
                condense(z, k, first_ref[j, z, k] + push, acc[k], field_ref.at[0]) for k in range(count)
            )

        def later(source, target):
            def body(z, acc):
                push = pushed(j, 1, z)
                at = (jnp.maximum(z - 1, 0), z, jnp.minimum(z + 1, crm_levels - 1))
                totals = five_points([[source[y, k] for k in range(count)] for y in at], 1)
                return tuple(
                    condense(z, k, 0.2 * totals[k] + push, acc[k], target) for k in range(count)
                )
            return body

        def totals(z, _):
            at = pl.ds(pl.multiple_of(8 * z, 8), 8)
            part_ref[j, at, :] = add_up([last_ref[j, z, k] for k in range(count)])
            return 0

        acc = tuple(jnp.zeros((8, LANES), F32) for _ in range(count))
        acc = lax.fori_loop(0, crm_levels, first, acc)
        acc = lax.fori_loop(0, crm_levels, later(field_ref.at[0], field_ref.at[1]), acc)
        acc = lax.fori_loop(0, crm_levels, later(field_ref.at[1], last_ref.at[j]), acc)
        lax.fori_loop(0, crm_levels, totals, 0)
        mean = jnp.sum(add_up(list(acc)), axis=0, keepdims=True) * (1.0 / (crm_levels * width))
        rain_ref[j] = jnp.where(occupied_ref[j] > 0.0, rate_of(j) * mean, 0.0)

    def change(j):
        return rows_of_sums(part_ref.at[j], crm_levels) * (1.0 / width) - sums_ref[j, 0]

    for j in range(blocks):
        budget = STEPS * (push_ref[j, 1] - bound) - change(j)
        rain = jnp.sum(budget, axis=0, keepdims=True) * (1.0 / (1.15 * LOG2E * crm_levels))
        occupied = occupied_ref[j] > 0.0
        rain_ref[j] = jnp.where(occupied, rain, 0.0)
        wettest = jnp.max(jnp.where(occupied, rain / rate_of(j), -2.0))

        @pl.when((wettest > -1.0) & (wettest < SMALL_RAIN))
        def _():
            again(j)

    turned = jnp.concatenate([low, high], axis=0)
    for j in range(blocks):
        answer = (0.7 / 2.3) * (sums_ref[j, 1] + row_ref[j]) - (3.0 / (2.3 * LOG2E)) * change(j)
        reply_ref[pl.ds(j * part, part), :] = slot_rows(turned, padded(answer))


def after_kernel(state_ref, last_ref, row_ref, occupied_ref, out_ref, kept_ref, new_ref, sems, done_sems):
    blocks, _, crm_levels, width, _ = kept_ref.shape
    count = width // 8

    def lanes(j):
        return pl.ds(pl.multiple_of(j * LANES, LANES), LANES)

    def load(j):
        return pltpu.make_async_copy(state_ref.at[:, :, :, lanes(j)], kept_ref.at[j], sems.at[j])

    def store(j):
        return pltpu.make_async_copy(new_ref.at[j], out_ref.at[:, :, :, lanes(j)], done_sems.at[j])

    for j in range(blocks):
        load(j).start()

    def block(j, _):
        occupied = jnp.broadcast_to(occupied_ref[j], (8, LANES)) > 0.0
        load(j).wait()
        fields = [[] for _ in range(STEPS + 1)]
        for i in range(crm_levels + STEPS):
            if i < crm_levels:
                heat = [kept_ref[j, 0, i, pl.ds(k, 8, stride=count), :] for k in range(count)]
                moist = [kept_ref[j, 1, i, pl.ds(k, 8, stride=count), :] for k in range(count)]
                fields[0].append([(h + h) + m for h, m in zip(heat, moist)])
            for t in range(1, STEPS + 1):
                z = i - t
                if 0 <= z < crm_levels:
                    fields[t].append(five_points(fields[t - 1], z))
            if not 0 <= z < crm_levels:
                continue
            row = jnp.broadcast_to(row_ref[j, pl.ds(z, 1), :], (8, LANES))
            for k, total in enumerate(fields[STEPS][z]):
                at = pl.ds(k, 8, stride=count)
                linear = (1.0 / 125.0) * total + row
                dry = (1.0 / LOG2E) * last_ref[j, z, k] + saturation(z, crm_levels)
                heat = (1.0 / 2.3) * (linear - dry)
                moist = dry + 0.3 * heat
                new_ref[j, 0, z, at, :] = jnp.where(occupied, heat, kept_ref[j, 0, z, at, :])
                new_ref[j, 1, z, at, :] = jnp.where(occupied, moist, kept_ref[j, 1, z, at, :])
        store(j).start()
        return 0

    lax.fori_loop(0, blocks, block, 0)
    for j in range(blocks):
        store(j).wait()


def tendency_kernel(crm_levels, pos_ref, returned_ref, out_ref):
    levels = out_ref.shape[0] // NV
    rows = returned_ref.shape[0]
    columns = pos_ref.shape[1]
    place = (iota((2 * rows, columns), 0) == pos_ref[...]).astype(BF16)
    high, low = split(returned_ref[...])
    lower = dot(high, place[:rows], (0, 0)) + dot(low, place[:rows], (0, 0))
    upper = dot(high, place[rows:], (0, 0)) + dot(low, place[rows:], (0, 0))
    answer = lower[:crm_levels] + upper[HALF : HALF + crm_levels]
    shape = (levels, crm_levels)
    spread = dot(interp(iota(shape, 1), iota(shape, 0), crm_levels, levels), answer, (1, 0), HIGHEST)
    for k in range(NV):
        out_ref[pl.ds(k * levels, levels), :] = mixing(k) * spread


def call(kernel, out, scratch=(), cost=(0, 0, 0), vmem=32, **specs):
    return pl.pallas_call(
        kernel, out_shape=out, scratch_shapes=list(scratch),
        cost_estimate=pl.CostEstimate(flops=int(cost[0]), bytes_accessed=int(cost[1]), transcendentals=int(cost[2])),
        compiler_params=pltpu.CompilerParams(vmem_limit_bytes=vmem * 2**20), **specs,
    )


def from_hbm(*arrays):
    return [pltpu.with_memory_space_constraint(x, pltpu.HBM) for x in arrays]


HBM = pl.BlockSpec(memory_space=pltpu.HBM)
VMEM = pl.BlockSpec(memory_space=pltpu.VMEM)


def cloud_before(crm_state):
    _, crm_levels, width, slots = crm_state.shape
    blocks = slots // LANES
    cells = crm_levels * width * slots
    return call(
        before_kernel,
        (
            pltpu.VMEM((blocks, crm_levels, width // 8, 8, LANES), F32),
            pltpu.VMEM((blocks, 2, crm_levels, LANES), F32),
        ),
        [
            pltpu.VMEM((blocks, 2, crm_levels, width, LANES), F32),
            pltpu.VMEM((2, crm_levels * 8, LANES), F32),
            pltpu.SemaphoreType.DMA((blocks,)),
        ],
        (cells * 25, cells * 8, 0),
        in_specs=[HBM],
        out_specs=[VMEM] * 2,
    )(*from_hbm(crm_state))


def cloud_steps(capacity, arrived, first, sums):
    blocks, crm_levels, count = first.shape[:3]
    slots = blocks * LANES
    cells = crm_levels * count * 8 * slots
    return call(
        functools.partial(cloud_kernel, capacity),
        (
            pltpu.VMEM(first.shape, F32),
            pltpu.VMEM((blocks, crm_levels, LANES), F32),
            pltpu.VMEM((blocks, 1, LANES), F32),
            jax.ShapeDtypeStruct(arrived.shape, F32),
            jax.ShapeDtypeStruct((blocks, 1, LANES), F32),
        ),
        [
            pltpu.VMEM((blocks, 2, crm_levels, LANES), F32),
            pltpu.VMEM((blocks, crm_levels * 8, LANES), F32),
            pltpu.VMEM((2,) + first.shape[1:], F32),
        ],
        (cells * 30, cells * 8, cells * 6),
        in_specs=[VMEM] * 3,
        out_specs=[VMEM] * 5,
    )(arrived, first, sums)


def cloud_after(crm_state, last, row, occupied):
    _, crm_levels, width, slots = crm_state.shape
    blocks = slots // LANES
    cells = crm_levels * width * slots
    return call(
        after_kernel,
        jax.ShapeDtypeStruct(crm_state.shape, F32),
        [pltpu.VMEM((blocks, 2, crm_levels, width, LANES), F32)] * 2
        + [pltpu.SemaphoreType.DMA((blocks,))] * 2,
        (cells * 10, cells * 8, 0),
        in_specs=[HBM] + [VMEM] * 3,
        out_specs=HBM,
    )(*from_hbm(crm_state), last, row, occupied)


def on_device(gcm_state, edge_part, neighbours, branch, routes, crm_state):
    peers = lax.axis_size(AXES)
    me = lax.axis_index(AXES)
    columns, features = gcm_state.shape
    _, crm_levels, _, slots = crm_state.shape
    capacity = slots // peers
    rows = slots // 2
    shape = jax.ShapeDtypeStruct

    own = call(edges_kernel, shape((crm_levels, columns), F32), cost=(1e7, 4e5, 0))(
        *from_hbm(edge_part)
    )
    pair = lax.ppermute(own, AXES, [(i, i ^ 1) for i in range(peers)])
    other = lax.ppermute(own, AXES, [(i, (((i + 1) ^ 1) - 1) % peers) for i in range(peers)])
    position, base, halo_map = call(
        functools.partial(route_kernel, peers, capacity),
        (
            shape((1, columns), jnp.int32),
            shape((rows, LANES), F32),
            shape((slots, 2 * columns), BF16),
        ),
        cost=(2e9, 2e6, 0),
        in_specs=[pl.BlockSpec(memory_space=pltpu.SMEM)] + [VMEM] * 5,
        out_specs=[VMEM] * 3,
    )(
        me.reshape(1),
        *from_hbm(routes.T, branch.reshape(1, -1), neighbours.T, gcm_state.T),
        own,
    )
    outgoing = call(outgoing_kernel, shape((rows, LANES), F32), cost=(2e8, 1e6, 0))(base, halo_map, pair, other)
    first, sums = cloud_before(crm_state)
    arrived = lax.all_to_all(outgoing.reshape(peers, capacity // 2, LANES), AXES, 0, 0, tiled=True)
    last, row, occupied, reply, rain = cloud_steps(capacity, arrived.reshape(rows, LANES), first, sums)
    returned = lax.all_to_all(reply.reshape(peers, capacity // 2, LANES), AXES, 0, 0, tiled=True)
    updated = cloud_after(crm_state, last, row, occupied)
    tendency = call(functools.partial(tendency_kernel, crm_levels), shape((features, columns), F32), cost=(1e8, 1e6, 0))(
        position, returned.reshape(rows, LANES)
    )
    return (tendency.T, updated, rain.reshape(1, slots))


def solution(mesh):
    in_specs = (
        P(AXES, None),
        P(AXES, None, None),
        P(AXES, None),
        P(AXES),
        P(AXES, None),
        P(None, None, None, AXES),
    )
    out_specs = (
        P(AXES, None),
        P(None, None, None, AXES),
        P(AXES, None),
    )
    return jax.shard_map(
        on_device, mesh=mesh, in_specs=in_specs, out_specs=out_specs, check_vma=False
    )
```

```python
import functools

import jax
import jax.numpy as jnp
import numpy as np
from jax import lax
from jax.experimental import pallas as pl
from jax.experimental.pallas import tpu as pltpu
from jax.sharding import PartitionSpec as P

NV = 8
STEPS = 3
AXES = ("elem", "sub")
LANES = 128
HALF = 64
LOG2E = 1.4426950408889634
F32 = jnp.float32
BF16 = jnp.bfloat16
HIGHEST = lax.Precision.HIGHEST
SMALL_RAIN = 0.2


def mixing(k):
    return (0.8 + 0.05 * k) * (1.0 if k % 2 == 0 else -1.0) / float(np.sqrt(float(NV)))


def interp(z, level, crm_levels, levels):
    position = z.astype(F32) * ((levels - 1) / (crm_levels - 1))
    return jnp.maximum(0.0, 1.0 - jnp.abs(position - level.astype(F32)))


def dot(a, b, contract, precision=None):
    return lax.dot_general(
        a, b, ((contract[0:1], contract[1:2]), ((), ())),
        precision=precision, preferred_element_type=F32,
    )


def split(x):
    high = x.astype(BF16)
    return high, (x - high.astype(F32)).astype(BF16)


def both_halves(x):
    high, low = split(x)
    return jnp.concatenate([high, low], axis=0)


def slot_rows(onehot, fields):
    product = dot(onehot, both_halves(fields), (1, 1))
    product = product + pltpu.roll(product, HALF, 1)
    rows = product.shape[0] // 2
    return jnp.where(iota((rows, 2 * HALF), 1) < HALF, product[:rows], product[rows:])


def padded(fields):
    return jnp.concatenate([fields, jnp.zeros((HALF - fields.shape[0], fields.shape[1]), F32)], axis=0)


def iota(shape, dim):
    return lax.broadcasted_iota(jnp.int32, shape, dim)


def edges_kernel(edge_ref, out_ref):
    crm_levels = out_ref.shape[0]
    shape = (crm_levels, edge_ref.shape[2])
    levels = shape[1] // 2
    lane = iota(shape, 1)
    weight = jnp.where(
        lane < levels,
        mixing(0) * interp(iota(shape, 0), lane, crm_levels, levels),
        mixing(1) * interp(iota(shape, 0), lane - levels, crm_levels, levels),
    )
    out_ref[...] = dot(weight, edge_ref[...].reshape(-1, shape[1]), (1, 1), HIGHEST)


def route_kernel(peers, capacity, me_ref, routes_ref, branch_ref, neigh_ref, gcm_ref, own_ref, pair_ref,
                 pos_ref, base_ref, halo_map_ref):
    columns = routes_ref.shape[1]
    elems = columns // 4
    crm_levels = own_ref.shape[0]
    slots = peers * capacity
    half = capacity // 2
    me = me_ref[0]
    destination = routes_ref[...]
    named = iota((peers, columns), 0) == destination
    earlier = (iota((columns, columns), 0) < iota((columns, columns), 1)).astype(BF16)
    before = dot(named.astype(BF16), earlier, (1, 0))
    rank = jnp.sum(jnp.where(named, before, 0.0), axis=0, keepdims=True).astype(jnp.int32)
    upper = (rank >= half).astype(jnp.int32)
    position = upper * (slots // 2) + destination * half + rank - upper * half
    pos_ref[...] = position
    place = (iota((slots, columns), 0) == position).astype(BF16)

    target = jnp.concatenate([neigh_ref[j : j + 1, :] for j in range(4)], axis=1)
    owner = target // columns
    edge = target - owner * columns
    block = jnp.where(owner == me, 0, jnp.where(owner == (me ^ 1), 1, 2))
    source = block * columns + edge
    window = iota((3 * columns, columns), 0)
    local = iota((1, columns), 1)
    local = 4 * (local % elems) + local // elems
    chosen = (window == source).astype(F32) + (window == local).astype(F32)
    column = iota((columns, columns), 0)
    row = iota((columns, columns), 1)
    first = (column % 4) * elems + column // 4
    second = ((column + 1) % 4) * elems + column // 4
    pair = ((row == first) | (row == second)).astype(BF16)
    mapped = dot(pair, chosen.astype(BF16), (1, 1)).astype(BF16)
    halo_map_ref[...] = dot(place, mapped[:, 2 * columns :], (1, 0)).astype(BF16)

    near = jnp.concatenate([own_ref[...], pair_ref[...]], axis=1)
    levels = gcm_ref.shape[0] // NV
    mixed = mixing(0) * gcm_ref[:levels, :]
    for k in range(1, NV):
        mixed += mixing(k) * gcm_ref[pl.ds(k * levels, levels), :]
    shape = (crm_levels, levels)
    force = dot(interp(iota(shape, 0), iota(shape, 1), crm_levels, levels), mixed, (1, 0), HIGHEST)
    for part in split(near):
        force += 0.25 * dot(part, mapped[:, : 2 * columns], (1, 1))
    code = (branch_ref[...] + 1).astype(F32)
    base_ref[...] = slot_rows(place, padded(jnp.concatenate([force, code], axis=0)))


def outgoing_kernel(base_ref, map_ref, other_ref, out_ref):
    out_ref[...] = base_ref[...] + 0.25 * slot_rows(map_ref[...], padded(other_ref[...]))


class Field:
    def __init__(self, total):
        self.total, self.rows, self.diagonals = total, [], []

    def five(self, z):
        while len(self.diagonals) < z + 2:
            at = len(self.diagonals)
            below, here = self.rows[max(at - 1, 0)], self.rows[min(at, self.total - 1)]
            right = here[1:] + [pltpu.roll(here[0], 7, 0)]
            self.diagonals.append([a + b for a, b in zip(below, right)])
        low, high = self.diagonals[z], self.diagonals[z + 1]
        high = [pltpu.roll(high[-1], 1, 0)] + high[:-1]
        return [row + (a + b) for row, a, b in zip(self.rows[z], low, high)]


def five_points(row, up, down):
    left = [pltpu.roll(row[-1], 1, 0)] + row[:-1]
    right = row[1:] + [pltpu.roll(row[0], 7, 0)]
    return [(a + b + c) + (d + e) for a, b, c, d, e in zip(row, left, right, up, down)]


def add_up(values):
    while len(values) > 1:
        values = [a + b for a, b in zip(values[::2], values[1::2])]
    return values[0]


def rows_of_sums(ref, crm_levels):
    return add_up([ref[pl.ds(s, crm_levels, stride=8), :] for s in range(8)])


def saturation(z, crm_levels):
    return 1.0 - z * (2.0 / (crm_levels - 1))


def levels_of(crm_levels):
    return iota((crm_levels, LANES), 0)


def shifted(x):
    return jnp.concatenate([x[:1], x[:-1]], axis=0) + jnp.concatenate([x[1:], x[-1:]], axis=0)


def before_kernel(state_ref, first_ref, sums_ref, kept_ref, part_ref, kept_sums_ref, new_ref, sems, done_sems):
    blocks, _, crm_levels, width, _ = kept_ref.shape
    count = width // 8

    def copy(j):
        lanes = pl.ds(pl.multiple_of(j * LANES, LANES), LANES)
        return pltpu.make_async_copy(state_ref.at[:, :, :, lanes], kept_ref.at[j], sems.at[j])

    def done(j):
        return pltpu.make_async_copy(new_ref.at[j], first_ref.at[j], done_sems.at[j])

    for j in range(blocks):
        copy(j).start()

    def block(j, _):
        copy(j).wait()
        dry = Field(crm_levels)
        for i in range(crm_levels + 1):
            if i < crm_levels:
                heat = [kept_ref[j, 0, i, pl.ds(k, 8, stride=count), :] for k in range(count)]
                moist = [kept_ref[j, 1, i, pl.ds(k, 8, stride=count), :] for k in range(count)]
                dry.rows.append([m - 0.3 * h for h, m in zip(heat, moist)])
                part_ref[0, pl.ds(8 * i, 8), :] = add_up(dry.rows[i])
                part_ref[1, pl.ds(8 * i, 8), :] = add_up(heat)
            if i:
                for k, total in enumerate(dry.five(i - 1)):
                    new_ref[j, i - 1, k] = (0.2 * LOG2E) * total
        done(j).start()
        level = saturation(levels_of(crm_levels).astype(F32), crm_levels)
        dry_mean = rows_of_sums(part_ref.at[0], crm_levels) * (1.0 / width)
        start = dry_mean + rows_of_sums(part_ref.at[1], crm_levels) * (2.3 / width)
        q = start
        for _ in range(STEPS):
            q = 0.6 * q + 0.2 * shifted(q)
        kept_sums_ref[j, 0] = LOG2E * (dry_mean - level)
        kept_sums_ref[j, 1] = q - start
        return 0

    lax.fori_loop(0, blocks, block, 0)
    sums = pltpu.make_async_copy(kept_sums_ref, sums_ref, done_sems.at[blocks])
    sums.start()
    for j in range(blocks):
        done(j).wait()
    sums.wait()


def lane_maps(rows, capacity):
    half = capacity // 2
    row = iota((rows, LANES), 0)
    slot = iota((rows, LANES), 1)
    rank = slot % capacity
    low = (row == (slot // capacity) * half + rank) & (rank < half)
    high = (row == (slot // capacity) * half + rank - half) & (rank >= half)
    return low.astype(BF16), high.astype(BF16)


def bounds(crm_levels):
    level = levels_of(crm_levels)
    edge = (0.4 / (crm_levels - 1)) * LOG2E
    return jnp.where(level == 0, -edge, 0.0) + jnp.where(level == crm_levels - 1, edge, 0.0)


def dried(crm_levels):
    return LOG2E * saturation(levels_of(crm_levels).astype(F32), crm_levels)


def respond(force):
    q = jnp.zeros_like(force)
    for _ in range(STEPS):
        q = 0.6 * q + 0.2 * shifted(q) + 0.5 * force
    return q


def rate_of(code):
    return 0.15 + 0.25 * (code == 2.0).astype(F32)


def cloud_kernel(capacity, arrived_ref, far_ref, far_sums_ref, last_ref, force_ref, code_ref, rain_ref,
                 reply_ref, push_ref, part_ref, sums_ref, first_ref, sems):
    blocks, crm_levels, count = last_ref.shape[:3]
    width = count * 8
    part = arrived_ref.shape[0] // blocks

    def load(j):
        return pltpu.make_async_copy(far_ref.at[j], first_ref.at[j], sems.at[j])

    load_sums = pltpu.make_async_copy(far_sums_ref, sums_ref, sems.at[blocks])
    for j in range(blocks):
        load(j).start()
    load_sums.start()
    low, high = lane_maps(part, capacity)
    maps = jnp.concatenate([low, high], axis=1)
    maps = jnp.concatenate([maps, maps], axis=0)
    for j in range(blocks):
        got = dot(both_halves(arrived_ref[pl.ds(j * part, part), :]), maps, (0, 0))
        got = got[:HALF, :LANES] + got[HALF:, LANES:]
        push = (-0.65 * LOG2E) * got[:crm_levels]
        push_ref[j, 0] = push - dried(crm_levels)
        push_ref[j, 1] = push + bounds(crm_levels)
        force_ref[j] = got[:crm_levels]
        code_ref[j] = got[crm_levels : crm_levels + 1]

    def block(j, _):
        load(j).wait()
        lowered = jnp.broadcast_to((1.15 * LOG2E) * rate_of(code_ref[j]), (8, LANES))
        fields = [Field(crm_levels) for _ in range(STEPS)]
        for i in range(crm_levels + STEPS - 1):
            for t in range(STEPS):
                z = i - t
                if not 0 <= z < crm_levels:
                    continue
                push = jnp.broadcast_to(push_ref[j, min(t, 1), pl.ds(z, 1), :], (8, LANES))
                if t == 0:
                    values = [first_ref[j, z, k] + push for k in range(count)]
                else:
                    values = [0.2 * total + push for total in fields[t - 1].five(z)]
                values = [y - lowered * jnp.log(1.0 + jnp.exp2(y)) for y in values]
                fields[t].rows.append(values)
                if t == STEPS - 1:
                    for k in range(count):
                        last_ref[j, z, k] = values[k]
                    part_ref[j, pl.ds(8 * z, 8), :] = add_up(values)
        return 0

    lax.fori_loop(0, blocks, block, 0)
    load_sums.wait()
    turned = jnp.concatenate([low, high], axis=0)
    for j in range(blocks):
        dg = rows_of_sums(part_ref.at[j], crm_levels) * (1.0 / width) - sums_ref[j, 0]
        answer = (0.7 / 2.3) * (sums_ref[j, 1] + respond(force_ref[j])) - (3.0 / (2.3 * LOG2E)) * dg
        reply_ref[pl.ds(j * part, part), :] = slot_rows(turned, padded(answer))
        budget = (-0.65 * LOG2E * STEPS) * force_ref[j] - dg
        rain = jnp.sum(budget, axis=0, keepdims=True) * (1.0 / (1.15 * LOG2E * crm_levels))
        rain_ref[j] = jnp.where(code_ref[j] > 0.0, rain, 0.0)


def after_kernel(state_ref, last_ref, force_ref, code_ref, guess_ref, out_ref, rain_ref,
                 kept_ref, new_ref, row_ref, push_ref, field_ref, sems, done_sems):
    blocks, _, crm_levels, width, _ = kept_ref.shape
    count = width // 8
    pieces = sems.shape[1]
    piece = crm_levels // pieces

    def lanes(j):
        return pl.ds(pl.multiple_of(j * LANES, LANES), LANES)

    def load(j, p):
        at = pl.ds(p * piece, piece)
        return pltpu.make_async_copy(
            state_ref.at[:, at, :, lanes(j)], kept_ref.at[j, :, at, :, :], sems.at[j, p]
        )

    def store(j, p):
        at = pl.ds(p * piece, piece)
        return pltpu.make_async_copy(
            new_ref.at[j, :, at, :, :], out_ref.at[:, at, :, lanes(j)], done_sems.at[j, p]
        )

    for j in range(blocks):
        for p in range(pieces):
            load(j, p).start()
    rain_ref[...] = guess_ref[...]
    for j in range(blocks):
        row_ref[j] = respond(force_ref[j])
    rows = [guess_ref[j] / rate_of(code_ref[j]) for j in range(blocks)]
    marks = [jnp.where(code_ref[j] > 0.0, row, -2.0) for j, row in enumerate(rows)]
    wettest = [jnp.max(mark, axis=1, keepdims=True) for mark in marks]
    dry = [((w > -1.0) & (w < SMALL_RAIN)).astype(jnp.int32) for w in wettest]
    some_dry = jnp.max(functools.reduce(jnp.maximum, dry)) > 0

    def block(j, _):
        occupied = jnp.broadcast_to(code_ref[j], (8, LANES)) > 0.0
        fields = [Field(crm_levels) for _ in range(STEPS + 1)]
        for i in range(crm_levels + STEPS):
            if i < crm_levels:
                if i % piece == 0:
                    load(j, i // piece).wait()
                heat = [kept_ref[j, 0, i, pl.ds(k, 8, stride=count), :] for k in range(count)]
                moist = [kept_ref[j, 1, i, pl.ds(k, 8, stride=count), :] for k in range(count)]
                fields[0].rows.append([(h + h) + m for h, m in zip(heat, moist)])
            for t in range(1, STEPS + 1):
                z = i - t
                if 0 <= z < crm_levels:
                    fields[t].rows.append(fields[t - 1].five(z))
            if not 0 <= z < crm_levels:
                continue
            row = jnp.broadcast_to(row_ref[j, pl.ds(z, 1), :], (8, LANES))
            for k, total in enumerate(fields[STEPS].rows[z]):
                at = pl.ds(k, 8, stride=count)
                linear = (1.0 / 125.0) * total + row
                dry = (1.0 / LOG2E) * last_ref[j, z, k] + saturation(z, crm_levels)
                heat = (1.0 / 2.3) * (linear - dry)
                moist = dry + 0.3 * heat
                new_ref[j, 0, z, at, :] = jnp.where(occupied, heat, kept_ref[j, 0, z, at, :])
                new_ref[j, 1, z, at, :] = jnp.where(occupied, moist, kept_ref[j, 1, z, at, :])
            if z % piece == piece - 1:
                store(j, z // piece).start()
        return 0

    lax.fori_loop(0, blocks, block, 0)

    def again(j, _):
        rate = rate_of(code_ref[j])
        lowered = jnp.broadcast_to((1.15 * LOG2E) * rate, (8, LANES))
        push = (-0.65 * LOG2E) * force_ref[j]
        push_ref[0] = push - dried(crm_levels)
        push_ref[1] = push + bounds(crm_levels)

        def condense(y, acc):
            e = jnp.exp2(y)
            amount = jnp.where(e < 2.0**-8, e * (1.0 - 0.5 * e), jnp.log(1.0 + e))
            return y - lowered * amount, acc + amount

        def start(z, _):
            for k in range(count):
                at = pl.ds(k, 8, stride=count)
                field_ref[0, z, k] = LOG2E * (kept_ref[j, 1, z, at, :] - 0.3 * kept_ref[j, 0, z, at, :])
            return 0

        def step(source, target, which):
            def body(z, acc):
                push = jnp.broadcast_to(push_ref[which, pl.ds(z, 1), :], (8, LANES))
                at = (z, jnp.maximum(z - 1, 0), jnp.minimum(z + 1, crm_levels - 1))
                totals = five_points(*[[field_ref[source, y, k] for k in range(count)] for y in at])
                new = []
                for k in range(count):
                    field_ref[target, z, k], total = condense(0.2 * totals[k] + push, acc[k])
                    new.append(total)
                return tuple(new)
            return body

        acc = tuple(jnp.zeros((8, LANES), F32) for _ in range(count))
        lax.fori_loop(0, crm_levels, start, 0)
        for t in range(STEPS):
            acc = lax.fori_loop(0, crm_levels, step(t % 2, (t + 1) % 2, min(t, 1)), acc)
        mean = jnp.sum(add_up(list(acc)), axis=0, keepdims=True) * (1.0 / (crm_levels * width))
        rain_ref[j] = jnp.where(code_ref[j] > 0.0, rate * mean, 0.0)
        return 0

    @pl.when(some_dry)
    def _():
        lax.fori_loop(0, blocks, again, 0)

    for j in range(blocks):
        for p in range(pieces):
            store(j, p).wait()


def tendency_kernel(crm_levels, pos_ref, returned_ref, out_ref, new_ref, sems):
    levels = out_ref.shape[0] // NV
    rows = returned_ref.shape[0]
    columns = pos_ref.shape[1]
    place = (iota((2 * rows, columns), 0) == pos_ref[...]).astype(BF16)
    high, low = split(returned_ref[...])
    lower = dot(high, place[:rows], (0, 0)) + dot(low, place[:rows], (0, 0))
    upper = dot(high, place[rows:], (0, 0)) + dot(low, place[rows:], (0, 0))
    answer = lower[:crm_levels] + upper[HALF : HALF + crm_levels]
    shape = (levels, crm_levels)
    spread = dot(interp(iota(shape, 1), iota(shape, 0), crm_levels, levels), answer, (1, 0), HIGHEST)
    copies = []
    for k in range(NV):
        new_ref[k] = mixing(k) * spread
        copies.append(
            pltpu.make_async_copy(new_ref.at[k], out_ref.at[pl.ds(k * levels, levels), :], sems.at[k])
        )
        copies[k].start()
    for copy in copies:
        copy.wait()


def call(kernel, out, scratch=(), cost=(0, 0, 0), vmem=32, **specs):
    return pl.pallas_call(
        kernel, out_shape=out, scratch_shapes=list(scratch),
        cost_estimate=pl.CostEstimate(flops=int(cost[0]), bytes_accessed=int(cost[1]), transcendentals=int(cost[2])),
        compiler_params=pltpu.CompilerParams(vmem_limit_bytes=vmem * 2**20), **specs,
    )


def from_hbm(*arrays):
    return [pltpu.with_memory_space_constraint(x, pltpu.HBM) for x in arrays]


HBM = pl.BlockSpec(memory_space=pltpu.HBM)
VMEM = pl.BlockSpec(memory_space=pltpu.VMEM)


def cloud_before(crm_state):
    _, crm_levels, width, slots = crm_state.shape
    blocks = slots // LANES
    cells = crm_levels * width * slots
    field = (blocks, crm_levels, width // 8, 8, LANES)
    sums = (blocks, 2, crm_levels, LANES)
    return call(
        before_kernel,
        (pltpu.HBM(field, F32), pltpu.HBM(sums, F32)),
        [
            pltpu.VMEM((blocks, 2, crm_levels, width, LANES), F32),
            pltpu.VMEM((2, crm_levels * 8, LANES), F32),
            pltpu.VMEM(sums, F32),
            pltpu.VMEM(field, F32),
            pltpu.SemaphoreType.DMA((blocks,)),
            pltpu.SemaphoreType.DMA((blocks + 1,)),
        ],
        (cells * 25, cells * 8, 0),
        in_specs=[HBM],
        out_specs=[HBM] * 2,
    )(*from_hbm(crm_state))


def cloud_steps(capacity, arrived, first, sums):
    blocks, _, crm_levels, _ = sums.shape
    slots = blocks * LANES
    cells = crm_levels * first.shape[2] * 8 * slots
    return call(
        functools.partial(cloud_kernel, capacity),
        (
            pltpu.VMEM(first.shape, F32),
            pltpu.VMEM((blocks, crm_levels, LANES), F32),
            pltpu.VMEM((blocks, 1, LANES), F32),
            pltpu.VMEM((blocks, 1, LANES), F32),
            jax.ShapeDtypeStruct(arrived.shape, F32),
        ),
        [
            pltpu.VMEM(sums.shape, F32),
            pltpu.VMEM((blocks, crm_levels * 8, LANES), F32),
            pltpu.VMEM(sums.shape, F32),
            pltpu.VMEM(first.shape, F32),
            pltpu.SemaphoreType.DMA((blocks + 1,)),
        ],
        (cells * 30, cells * 8, cells * 6),
        in_specs=[VMEM, HBM, HBM],
        out_specs=[VMEM] * 5,
    )(arrived, *from_hbm(first, sums))


def cloud_after(crm_state, last, force, code, rain):
    _, crm_levels, width, slots = crm_state.shape
    blocks = slots // LANES
    pieces = 1
    cells = crm_levels * width * slots
    return call(
        after_kernel,
        (jax.ShapeDtypeStruct(crm_state.shape, F32), jax.ShapeDtypeStruct((blocks, 1, LANES), F32)),
        [pltpu.VMEM((blocks, 2, crm_levels, width, LANES), F32)] * 2
        + [
            pltpu.VMEM((blocks, crm_levels, LANES), F32),
            pltpu.VMEM((2, crm_levels, LANES), F32),
            pltpu.VMEM((2,) + last.shape[1:], F32),
        ]
        + [pltpu.SemaphoreType.DMA((blocks, pieces))] * 2,
        (cells * 10, cells * 8, 0),
        in_specs=[HBM] + [VMEM] * 4,
        out_specs=[HBM, VMEM],
    )(*from_hbm(crm_state), last, force, code, rain)


def on_device(gcm_state, edge_part, neighbours, branch, routes, crm_state):
    peers = lax.axis_size(AXES)
    me = lax.axis_index(AXES)
    columns, features = gcm_state.shape
    _, crm_levels, _, slots = crm_state.shape
    capacity = slots // peers
    rows = slots // 2
    shape = jax.ShapeDtypeStruct

    own = call(edges_kernel, shape((crm_levels, columns), F32), cost=(1e7, 4e5, 0))(
        *from_hbm(edge_part)
    )
    other = lax.ppermute(own, AXES, [(i, (((i + 1) ^ 1) - 1) % peers) for i in range(peers)])
    pair = lax.ppermute(own, AXES, [(i, i ^ 1) for i in range(peers)])
    position, base, halo_map = call(
        functools.partial(route_kernel, peers, capacity),
        (
            shape((1, columns), jnp.int32),
            shape((rows, LANES), F32),
            shape((slots, columns), BF16),
        ),
        cost=(2e9, 2e6, 0),
        in_specs=[pl.BlockSpec(memory_space=pltpu.SMEM)] + [VMEM] * 6,
        out_specs=[VMEM] * 3,
    )(
        me.reshape(1),
        *from_hbm(routes.T, branch.reshape(1, -1), neighbours.T, gcm_state.T),
        own,
        pair,
    )
    outgoing = call(outgoing_kernel, shape((rows, LANES), F32), cost=(2e8, 1e6, 0))(base, halo_map, other)
    first, sums = cloud_before(crm_state)
    arrived = lax.all_to_all(outgoing.reshape(peers, capacity // 2, LANES), AXES, 0, 0, tiled=True)
    last, force, code, rain, reply = cloud_steps(capacity, arrived.reshape(rows, LANES), first, sums)
    returned = lax.all_to_all(reply.reshape(peers, capacity // 2, LANES), AXES, 0, 0, tiled=True)
    updated, rain = cloud_after(crm_state, last, force, code, rain)
    levels = features // NV
    tendency = call(
        functools.partial(tendency_kernel, crm_levels),
        shape((features, columns), F32),
        [pltpu.VMEM((NV, levels, columns), F32), pltpu.SemaphoreType.DMA((NV,))],
        (1e8, 1e6, 0),
        in_specs=[VMEM] * 2,
        out_specs=HBM,
    )(position, returned.reshape(rows, LANES))
    return (tendency.T, updated, rain.reshape(1, slots))


def solution(mesh):
    in_specs = (
        P(AXES, None),
        P(AXES, None, None),
        P(AXES, None),
        P(AXES),
        P(AXES, None),
        P(None, None, None, AXES),
    )
    out_specs = (
        P(AXES, None),
        P(None, None, None, AXES),
        P(AXES, None),
    )
    return jax.shard_map(
        on_device, mesh=mesh, in_specs=in_specs, out_specs=out_specs, check_vma=False
    )
```

```python
import functools

import jax
import jax.numpy as jnp
import numpy as np
from jax import lax
from jax.experimental import pallas as pl
from jax.experimental.pallas import tpu as pltpu
from jax.sharding import PartitionSpec as P

NV = 8
STEPS = 3
AXES = ("elem", "sub")
LANES = 128
HALF = 64
LOG2E = 1.4426950408889634
F32 = jnp.float32
BF16 = jnp.bfloat16
HIGHEST = lax.Precision.HIGHEST
SMALL_RAIN = 0.2


def mixing(k):
    return (0.8 + 0.05 * k) * (1.0 if k % 2 == 0 else -1.0) / float(np.sqrt(float(NV)))


def interp(z, level, crm_levels, levels):
    position = z.astype(F32) * ((levels - 1) / (crm_levels - 1))
    return jnp.maximum(0.0, 1.0 - jnp.abs(position - level.astype(F32)))


def dot(a, b, contract, precision=None):
    return lax.dot_general(
        a, b, ((contract[0:1], contract[1:2]), ((), ())),
        precision=precision, preferred_element_type=F32,
    )


def split(x):
    high = x.astype(BF16)
    return high, (x - high.astype(F32)).astype(BF16)


def both_halves(x):
    high, low = split(x)
    return jnp.concatenate([high, low], axis=0)


def slot_rows(onehot, fields):
    product = dot(onehot, both_halves(fields), (1, 1))
    product = product + pltpu.roll(product, HALF, 1)
    rows = product.shape[0] // 2
    return jnp.where(iota((rows, 2 * HALF), 1) < HALF, product[:rows], product[rows:])


def padded(fields):
    return jnp.concatenate([fields, jnp.zeros((HALF - fields.shape[0], fields.shape[1]), F32)], axis=0)


def iota(shape, dim):
    return lax.broadcasted_iota(jnp.int32, shape, dim)


def edges_kernel(edge_ref, out_ref):
    crm_levels = out_ref.shape[0]
    shape = (crm_levels, edge_ref.shape[2])
    levels = shape[1] // 2
    lane = iota(shape, 1)
    weight = jnp.where(
        lane < levels,
        mixing(0) * interp(iota(shape, 0), lane, crm_levels, levels),
        mixing(1) * interp(iota(shape, 0), lane - levels, crm_levels, levels),
    )
    out_ref[...] = dot(weight, edge_ref[...].reshape(-1, shape[1]), (1, 1), HIGHEST)


def route_kernel(peers, capacity, me_ref, routes_ref, branch_ref, neigh_ref, gcm_ref, own_ref,
                 pos_ref, base_ref, halo_map_ref):
    columns = routes_ref.shape[1]
    elems = columns // 4
    crm_levels = own_ref.shape[0]
    slots = peers * capacity
    half = capacity // 2
    me = me_ref[0]
    destination = routes_ref[...]
    named = iota((peers, columns), 0) == destination
    earlier = (iota((columns, columns), 0) < iota((columns, columns), 1)).astype(BF16)
    before = dot(named.astype(BF16), earlier, (1, 0))
    rank = jnp.sum(jnp.where(named, before, 0.0), axis=0, keepdims=True).astype(jnp.int32)
    upper = (rank >= half).astype(jnp.int32)
    position = upper * (slots // 2) + destination * half + rank - upper * half
    pos_ref[...] = position
    place = (iota((slots, columns), 0) == position).astype(BF16)

    target = jnp.concatenate([neigh_ref[j : j + 1, :] for j in range(4)], axis=1)
    owner = target // columns
    edge = target - owner * columns
    block = jnp.where(owner == me, 0, jnp.where(owner == (me ^ 1), 1, 2))
    source = block * columns + edge
    window = iota((3 * columns, columns), 0)
    local = iota((1, columns), 1)
    local = 4 * (local % elems) + local // elems
    chosen = (window == source).astype(F32) + (window == local).astype(F32)
    column = iota((columns, columns), 0)
    row = iota((columns, columns), 1)
    first = (column % 4) * elems + column // 4
    second = ((column + 1) % 4) * elems + column // 4
    pair = ((row == first) | (row == second)).astype(BF16)
    mapped = dot(pair, chosen.astype(BF16), (1, 1)).astype(BF16)
    halo_map_ref[...] = dot(place, mapped[:, columns:], (1, 0)).astype(BF16)

    levels = gcm_ref.shape[0] // NV
    mixed = mixing(0) * gcm_ref[:levels, :]
    for k in range(1, NV):
        mixed += mixing(k) * gcm_ref[pl.ds(k * levels, levels), :]
    shape = (crm_levels, levels)
    force = dot(interp(iota(shape, 0), iota(shape, 1), crm_levels, levels), mixed, (1, 0), HIGHEST)
    for part in split(own_ref[...]):
        force += 0.25 * dot(part, mapped[:, :columns], (1, 1))
    code = (branch_ref[...] + 1).astype(F32)
    base_ref[...] = slot_rows(place, padded(jnp.concatenate([force, code], axis=0)))


def outgoing_kernel(base_ref, map_ref, other_ref, pair_ref, _, out_ref):
    window = jnp.concatenate([pair_ref[...], other_ref[...]], axis=1)
    out_ref[...] = base_ref[...] + 0.25 * slot_rows(map_ref[...], padded(window))


class Field:
    def __init__(self, total):
        self.total, self.rows, self.diagonals = total, [], []

    def five(self, z):
        while len(self.diagonals) < z + 2:
            at = len(self.diagonals)
            below, here = self.rows[max(at - 1, 0)], self.rows[min(at, self.total - 1)]
            right = here[1:] + [pltpu.roll(here[0], 7, 0)]
            self.diagonals.append([a + b for a, b in zip(below, right)])
        low, high = self.diagonals[z], self.diagonals[z + 1]
        high = [pltpu.roll(high[-1], 1, 0)] + high[:-1]
        return [row + (a + b) for row, a, b in zip(self.rows[z], low, high)]


def five_points(row, up, down):
    left = [pltpu.roll(row[-1], 1, 0)] + row[:-1]
    right = row[1:] + [pltpu.roll(row[0], 7, 0)]
    return [(a + b + c) + (d + e) for a, b, c, d, e in zip(row, left, right, up, down)]


def add_up(values):
    while len(values) > 1:
        values = [a + b for a, b in zip(values[::2], values[1::2])]
    return values[0]


def rows_of_sums(ref, crm_levels):
    return add_up([ref[pl.ds(s, crm_levels, stride=8), :] for s in range(8)])


def saturation(z, crm_levels):
    return 1.0 - z * (2.0 / (crm_levels - 1))


def levels_of(crm_levels):
    return iota((crm_levels, LANES), 0)


def shifted(x):
    return jnp.concatenate([x[:1], x[:-1]], axis=0) + jnp.concatenate([x[1:], x[-1:]], axis=0)


def before_kernel(start, state_ref, first_ref, sums_ref, kept_ref, part_ref, kept_sums_ref, new_ref, sems, done_sems):
    blocks, _, crm_levels, width, _ = kept_ref.shape
    count = width // 8

    def copy(j):
        lanes = pl.ds(pl.multiple_of((start + j) * LANES, LANES), LANES)
        return pltpu.make_async_copy(state_ref.at[:, :, :, lanes], kept_ref.at[j], sems.at[j])

    def done(j):
        return pltpu.make_async_copy(new_ref.at[j], first_ref.at[j], done_sems.at[j])

    for j in range(blocks):
        copy(j).start()

    def block(j, _):
        copy(j).wait()
        dry = Field(crm_levels)
        for i in range(crm_levels + 1):
            if i < crm_levels:
                heat = [kept_ref[j, 0, i, pl.ds(k, 8, stride=count), :] for k in range(count)]
                moist = [kept_ref[j, 1, i, pl.ds(k, 8, stride=count), :] for k in range(count)]
                dry.rows.append([m - 0.3 * h for h, m in zip(heat, moist)])
                part_ref[0, pl.ds(8 * i, 8), :] = add_up(dry.rows[i])
                part_ref[1, pl.ds(8 * i, 8), :] = add_up(heat)
            if i:
                for k, total in enumerate(dry.five(i - 1)):
                    new_ref[j, i - 1, k] = (0.2 * LOG2E) * total
        done(j).start()
        level = saturation(levels_of(crm_levels).astype(F32), crm_levels)
        dry_mean = rows_of_sums(part_ref.at[0], crm_levels) * (1.0 / width)
        start = dry_mean + rows_of_sums(part_ref.at[1], crm_levels) * (2.3 / width)
        q = start
        for _ in range(STEPS):
            q = 0.6 * q + 0.2 * shifted(q)
        kept_sums_ref[j, 0] = LOG2E * (dry_mean - level)
        kept_sums_ref[j, 1] = q - start
        return 0

    lax.fori_loop(0, blocks, block, 0)
    sums = pltpu.make_async_copy(kept_sums_ref, sums_ref, done_sems.at[blocks])
    sums.start()
    for j in range(blocks):
        done(j).wait()
    sums.wait()


def lane_maps(rows, capacity):
    half = capacity // 2
    row = iota((rows, LANES), 0)
    slot = iota((rows, LANES), 1)
    rank = slot % capacity
    low = (row == (slot // capacity) * half + rank) & (rank < half)
    high = (row == (slot // capacity) * half + rank - half) & (rank >= half)
    return low.astype(BF16), high.astype(BF16)


def bounds(crm_levels):
    level = levels_of(crm_levels)
    edge = (0.4 / (crm_levels - 1)) * LOG2E
    return jnp.where(level == 0, -edge, 0.0) + jnp.where(level == crm_levels - 1, edge, 0.0)


def dried(crm_levels):
    return LOG2E * saturation(levels_of(crm_levels).astype(F32), crm_levels)


def respond(force):
    q = jnp.zeros_like(force)
    for _ in range(STEPS):
        q = 0.6 * q + 0.2 * shifted(q) + 0.5 * force
    return q


def rate_of(code):
    return 0.15 + 0.25 * (code == 2.0).astype(F32)


def cloud_kernel(capacity, arrived_ref, near_ref, near_sums_ref, far_ref, far_sums_ref, last_ref, force_ref, code_ref, rain_ref,
                 reply_ref, push_ref, part_ref, sums_ref, first_ref, sems):
    blocks, crm_levels, count = last_ref.shape[:3]
    near = near_ref.shape[0]
    width = count * 8
    part = arrived_ref.shape[0] // blocks

    def load(j):
        source = near_ref.at[j] if j < near else far_ref.at[j - near]
        return pltpu.make_async_copy(source, first_ref.at[j], sems.at[j])

    load_sums = [
        pltpu.make_async_copy(near_sums_ref, sums_ref.at[pl.ds(0, near)], sems.at[blocks]),
        pltpu.make_async_copy(far_sums_ref, sums_ref.at[pl.ds(near, blocks - near)], sems.at[blocks + 1]),
    ]
    for j in range(blocks):
        load(j).start()
    for copy in load_sums:
        copy.start()
    low, high = lane_maps(part, capacity)
    maps = jnp.concatenate([low, high], axis=1)
    maps = jnp.concatenate([maps, maps], axis=0)
    for j in range(blocks):
        got = dot(both_halves(arrived_ref[pl.ds(j * part, part), :]), maps, (0, 0))
        got = got[:HALF, :LANES] + got[HALF:, LANES:]
        push = (-0.65 * LOG2E) * got[:crm_levels]
        push_ref[j, 0] = push - dried(crm_levels)
        push_ref[j, 1] = push + bounds(crm_levels)
        force_ref[j] = got[:crm_levels]
        code_ref[j] = got[crm_levels : crm_levels + 1]

    def block(j, _):
        pltpu.make_async_copy(far_ref.at[0], first_ref.at[j], sems.at[j]).wait()
        lowered = jnp.broadcast_to((1.15 * LOG2E) * rate_of(code_ref[j]), (8, LANES))
        fields = [Field(crm_levels) for _ in range(STEPS)]
        for i in range(crm_levels + STEPS - 1):
            for t in range(STEPS):
                z = i - t
                if not 0 <= z < crm_levels:
                    continue
                push = jnp.broadcast_to(push_ref[j, min(t, 1), pl.ds(z, 1), :], (8, LANES))
                if t == 0:
                    values = [first_ref[j, z, k] + push for k in range(count)]
                else:
                    values = [0.2 * total + push for total in fields[t - 1].five(z)]
                values = [y - lowered * jnp.log(1.0 + jnp.exp2(y)) for y in values]
                fields[t].rows.append(values)
                if t == STEPS - 1:
                    for k in range(count):
                        last_ref[j, z, k] = values[k]
                    part_ref[j, pl.ds(8 * z, 8), :] = add_up(values)
        return 0

    lax.fori_loop(0, blocks, block, 0)
    for copy in load_sums:
        copy.wait()
    turned = jnp.concatenate([low, high], axis=0)
    for j in range(blocks):
        dg = rows_of_sums(part_ref.at[j], crm_levels) * (1.0 / width) - sums_ref[j, 0]
        answer = (0.7 / 2.3) * (sums_ref[j, 1] + respond(force_ref[j])) - (3.0 / (2.3 * LOG2E)) * dg
        reply_ref[pl.ds(j * part, part), :] = slot_rows(turned, padded(answer))
        budget = (-0.65 * LOG2E * STEPS) * force_ref[j] - dg
        rain = jnp.sum(budget, axis=0, keepdims=True) * (1.0 / (1.15 * LOG2E * crm_levels))
        rain_ref[j] = jnp.where(code_ref[j] > 0.0, rain, 0.0)


def after_kernel(state_ref, last_ref, force_ref, code_ref, guess_ref, out_ref, rain_ref,
                 kept_ref, new_ref, row_ref, push_ref, field_ref, sems, done_sems):
    blocks, _, crm_levels, width, _ = kept_ref.shape
    count = width // 8
    pieces = sems.shape[1]
    piece = crm_levels // pieces

    def lanes(j):
        return pl.ds(pl.multiple_of(j * LANES, LANES), LANES)

    def load(j, p):
        at = pl.ds(p * piece, piece)
        return pltpu.make_async_copy(
            state_ref.at[:, at, :, lanes(j)], kept_ref.at[j, :, at, :, :], sems.at[j, p]
        )

    def store(j, p):
        at = pl.ds(p * piece, piece)
        return pltpu.make_async_copy(
            new_ref.at[j, :, at, :, :], out_ref.at[:, at, :, lanes(j)], done_sems.at[j, p]
        )

    for j in range(blocks):
        for p in range(pieces):
            load(j, p).start()
    rain_ref[...] = guess_ref[...]
    for j in range(blocks):
        row_ref[j] = respond(force_ref[j])
    rows = [guess_ref[j] / rate_of(code_ref[j]) for j in range(blocks)]
    marks = [jnp.where(code_ref[j] > 0.0, row, -2.0) for j, row in enumerate(rows)]
    wettest = [jnp.max(mark, axis=1, keepdims=True) for mark in marks]
    dry = [((w > -1.0) & (w < SMALL_RAIN)).astype(jnp.int32) for w in wettest]
    some_dry = jnp.max(functools.reduce(jnp.maximum, dry)) > 0

    def block(j, _):
        occupied = jnp.broadcast_to(code_ref[j], (8, LANES)) > 0.0
        fields = [Field(crm_levels) for _ in range(STEPS + 1)]
        for i in range(crm_levels + STEPS):
            if i < crm_levels:
                if i % piece == 0:
                    load(j, i // piece).wait()
                heat = [kept_ref[j, 0, i, pl.ds(k, 8, stride=count), :] for k in range(count)]
                moist = [kept_ref[j, 1, i, pl.ds(k, 8, stride=count), :] for k in range(count)]
                fields[0].rows.append([(h + h) + m for h, m in zip(heat, moist)])
            for t in range(1, STEPS + 1):
                z = i - t
                if 0 <= z < crm_levels:
                    fields[t].rows.append(fields[t - 1].five(z))
            if not 0 <= z < crm_levels:
                continue
            row = jnp.broadcast_to(row_ref[j, pl.ds(z, 1), :], (8, LANES))
            for k, total in enumerate(fields[STEPS].rows[z]):
                at = pl.ds(k, 8, stride=count)
                linear = (1.0 / 125.0) * total + row
                dry = (1.0 / LOG2E) * last_ref[j, z, k] + saturation(z, crm_levels)
                heat = (1.0 / 2.3) * (linear - dry)
                moist = dry + 0.3 * heat
                new_ref[j, 0, z, at, :] = jnp.where(occupied, heat, kept_ref[j, 0, z, at, :])
                new_ref[j, 1, z, at, :] = jnp.where(occupied, moist, kept_ref[j, 1, z, at, :])
            if z % piece == piece - 1:
                store(j, z // piece).start()
        return 0

    lax.fori_loop(0, blocks, block, 0)

    def again(j, _):
        rate = rate_of(code_ref[j])
        lowered = jnp.broadcast_to((1.15 * LOG2E) * rate, (8, LANES))
        push = (-0.65 * LOG2E) * force_ref[j]
        push_ref[0] = push - dried(crm_levels)
        push_ref[1] = push + bounds(crm_levels)

        def condense(y, acc):
            e = jnp.exp2(y)
            amount = jnp.where(e < 2.0**-8, e * (1.0 - 0.5 * e), jnp.log(1.0 + e))
            return y - lowered * amount, acc + amount

        def start(z, _):
            for k in range(count):
                at = pl.ds(k, 8, stride=count)
                field_ref[0, z, k] = LOG2E * (kept_ref[j, 1, z, at, :] - 0.3 * kept_ref[j, 0, z, at, :])
            return 0

        def step(source, target, which):
            def body(z, acc):
                push = jnp.broadcast_to(push_ref[which, pl.ds(z, 1), :], (8, LANES))
                at = (z, jnp.maximum(z - 1, 0), jnp.minimum(z + 1, crm_levels - 1))
                totals = five_points(*[[field_ref[source, y, k] for k in range(count)] for y in at])
                new = []
                for k in range(count):
                    field_ref[target, z, k], total = condense(0.2 * totals[k] + push, acc[k])
                    new.append(total)
                return tuple(new)
            return body

        acc = tuple(jnp.zeros((8, LANES), F32) for _ in range(count))
        lax.fori_loop(0, crm_levels, start, 0)
        for t in range(STEPS):
            acc = lax.fori_loop(0, crm_levels, step(t % 2, (t + 1) % 2, min(t, 1)), acc)
        mean = jnp.sum(add_up(list(acc)), axis=0, keepdims=True) * (1.0 / (crm_levels * width))
        rain_ref[j] = jnp.where(code_ref[j] > 0.0, rate * mean, 0.0)
        return 0

    @pl.when(some_dry)
    def _():
        lax.fori_loop(0, blocks, again, 0)

    for j in range(blocks):
        for p in range(pieces):
            store(j, p).wait()


def tendency_kernel(crm_levels, pos_ref, returned_ref, out_ref, new_ref, sems):
    levels = out_ref.shape[0] // NV
    rows = returned_ref.shape[0]
    columns = pos_ref.shape[1]
    place = (iota((2 * rows, columns), 0) == pos_ref[...]).astype(BF16)
    high, low = split(returned_ref[...])
    lower = dot(high, place[:rows], (0, 0)) + dot(low, place[:rows], (0, 0))
    upper = dot(high, place[rows:], (0, 0)) + dot(low, place[rows:], (0, 0))
    answer = lower[:crm_levels] + upper[HALF : HALF + crm_levels]
    shape = (levels, crm_levels)
    spread = dot(interp(iota(shape, 1), iota(shape, 0), crm_levels, levels), answer, (1, 0), HIGHEST)
    copies = []
    for k in range(NV):
        new_ref[k] = mixing(k) * spread
        copies.append(
            pltpu.make_async_copy(new_ref.at[k], out_ref.at[pl.ds(k * levels, levels), :], sems.at[k])
        )
        copies[k].start()
    for copy in copies:
        copy.wait()


def call(kernel, out, scratch=(), cost=(0, 0, 0), vmem=32, **specs):
    return pl.pallas_call(
        kernel, out_shape=out, scratch_shapes=list(scratch),
        cost_estimate=pl.CostEstimate(flops=int(cost[0]), bytes_accessed=int(cost[1]), transcendentals=int(cost[2])),
        compiler_params=pltpu.CompilerParams(vmem_limit_bytes=vmem * 2**20), **specs,
    )


def from_hbm(*arrays):
    return [pltpu.with_memory_space_constraint(x, pltpu.HBM) for x in arrays]


HBM = pl.BlockSpec(memory_space=pltpu.HBM)
VMEM = pl.BlockSpec(memory_space=pltpu.VMEM)


def cloud_before(crm_state, start, blocks):
    _, crm_levels, width, _ = crm_state.shape
    cells = crm_levels * width * blocks * LANES
    field = (blocks, crm_levels, width // 8, 8, LANES)
    sums = (blocks, 2, crm_levels, LANES)
    return call(
        functools.partial(before_kernel, start),
        (pltpu.HBM(field, F32), pltpu.HBM(sums, F32)),
        [
            pltpu.VMEM((blocks, 2, crm_levels, width, LANES), F32),
            pltpu.VMEM((2, crm_levels * 8, LANES), F32),
            pltpu.VMEM(sums, F32),
            pltpu.VMEM(field, F32),
            pltpu.SemaphoreType.DMA((blocks,)),
            pltpu.SemaphoreType.DMA((blocks + 1,)),
        ],
        (cells * 25, cells * 8, 0),
        in_specs=[HBM],
        out_specs=[HBM] * 2,
    )(*from_hbm(crm_state))


def cloud_steps(capacity, arrived, near, near_sums, far, far_sums):
    blocks = near.shape[0] + far.shape[0]
    crm_levels, count = far.shape[1:3]
    cells = crm_levels * count * 8 * blocks * LANES
    sums = (blocks,) + far_sums.shape[1:]
    return call(
        functools.partial(cloud_kernel, capacity),
        (
            pltpu.VMEM((blocks,) + far.shape[1:], F32),
            pltpu.VMEM((blocks, crm_levels, LANES), F32),
            pltpu.VMEM((blocks, 1, LANES), F32),
            pltpu.VMEM((blocks, 1, LANES), F32),
            jax.ShapeDtypeStruct(arrived.shape, F32),
        ),
        [
            pltpu.VMEM(sums, F32),
            pltpu.VMEM((blocks, crm_levels * 8, LANES), F32),
            pltpu.VMEM(sums, F32),
            pltpu.VMEM((blocks,) + far.shape[1:], F32),
            pltpu.SemaphoreType.DMA((blocks + 2,)),
        ],
        (cells * 30, cells * 8, cells * 6),
        in_specs=[VMEM] + [HBM] * 4,
        out_specs=[VMEM] * 5,
    )(arrived, *from_hbm(near, near_sums, far, far_sums))


def cloud_after(crm_state, last, force, code, rain):
    _, crm_levels, width, slots = crm_state.shape
    blocks = slots // LANES
    pieces = 1
    cells = crm_levels * width * slots
    return call(
        after_kernel,
        (jax.ShapeDtypeStruct(crm_state.shape, F32), jax.ShapeDtypeStruct((blocks, 1, LANES), F32)),
        [pltpu.VMEM((blocks, 2, crm_levels, width, LANES), F32)] * 2
        + [
            pltpu.VMEM((blocks, crm_levels, LANES), F32),
            pltpu.VMEM((2, crm_levels, LANES), F32),
            pltpu.VMEM((2,) + last.shape[1:], F32),
        ]
        + [pltpu.SemaphoreType.DMA((blocks, pieces))] * 2,
        (cells * 10, cells * 8, 0),
        in_specs=[HBM] + [VMEM] * 4,
        out_specs=[HBM, VMEM],
    )(*from_hbm(crm_state), last, force, code, rain)


def on_device(gcm_state, edge_part, neighbours, branch, routes, crm_state):
    peers = lax.axis_size(AXES)
    me = lax.axis_index(AXES)
    columns, features = gcm_state.shape
    _, crm_levels, _, slots = crm_state.shape
    capacity = slots // peers
    rows = slots // 2
    shape = jax.ShapeDtypeStruct

    own = call(edges_kernel, shape((crm_levels, columns), F32), cost=(1e7, 4e5, 0))(
        *from_hbm(edge_part)
    )
    other = lax.ppermute(own, AXES, [(i, (((i + 1) ^ 1) - 1) % peers) for i in range(peers)])
    pair = lax.ppermute(own, AXES, [(i, i ^ 1) for i in range(peers)])
    position, base, halo_map = call(
        functools.partial(route_kernel, peers, capacity),
        (
            shape((1, columns), jnp.int32),
            shape((rows, LANES), F32),
            shape((slots, 2 * columns), BF16),
        ),
        cost=(2e9, 2e6, 0),
        in_specs=[pl.BlockSpec(memory_space=pltpu.SMEM)] + [VMEM] * 5,
        out_specs=[VMEM] * 3,
    )(
        me.reshape(1),
        *from_hbm(routes.T, branch.reshape(1, -1), neighbours.T, gcm_state.T),
        own,
    )
    near, near_sums = cloud_before(crm_state, 0, 1)
    outgoing = call(
        outgoing_kernel, shape((rows, LANES), F32), cost=(2e8, 1e6, 0),
        in_specs=[VMEM] * 4 + [HBM], out_specs=VMEM,
    )(base, halo_map, other, pair, *from_hbm(near))
    far, far_sums = cloud_before(crm_state, 1, slots // LANES - 1)
    arrived = lax.all_to_all(outgoing.reshape(peers, capacity // 2, LANES), AXES, 0, 0, tiled=True)
    last, force, code, rain, reply = cloud_steps(
        capacity, arrived.reshape(rows, LANES), near, near_sums, far, far_sums
    )
    returned = lax.all_to_all(reply.reshape(peers, capacity // 2, LANES), AXES, 0, 0, tiled=True)
    updated, rain = cloud_after(crm_state, last, force, code, rain)
    levels = features // NV
    tendency = call(
        functools.partial(tendency_kernel, crm_levels),
        shape((features, columns), F32),
        [pltpu.VMEM((NV, levels, columns), F32), pltpu.SemaphoreType.DMA((NV,))],
        (1e8, 1e6, 0),
        in_specs=[VMEM] * 2,
        out_specs=HBM,
    )(position, returned.reshape(rows, LANES))
    return (tendency.T, updated, rain.reshape(1, slots))


def solution(mesh):
    in_specs = (
        P(AXES, None),
        P(AXES, None, None),
        P(AXES, None),
        P(AXES),
        P(AXES, None),
        P(None, None, None, AXES),
    )
    out_specs = (
        P(AXES, None),
        P(None, None, None, AXES),
        P(AXES, None),
    )
    return jax.shard_map(
        on_device, mesh=mesh, in_specs=in_specs, out_specs=out_specs, check_vma=False
    )
```

```python
import functools

import jax
import jax.numpy as jnp
import numpy as np
from jax import lax
from jax.experimental import pallas as pl
from jax.experimental.pallas import tpu as pltpu
from jax.sharding import PartitionSpec as P

NV = 8
STEPS = 3
AXES = ("elem", "sub")
LANES = 128
HALF = 64
LOG2E = 1.4426950408889634
F32 = jnp.float32
BF16 = jnp.bfloat16
SMALL_RAIN = 0.2


def mixing(k):
    return (0.8 + 0.05 * k) * (1.0 if k % 2 == 0 else -1.0) / float(np.sqrt(float(NV)))


def interp(z, level, crm_levels, levels):
    position = z.astype(F32) * ((levels - 1) / (crm_levels - 1))
    return jnp.maximum(0.0, 1.0 - jnp.abs(position - level.astype(F32)))


def dot(a, b, contract):
    return lax.dot_general(
        a, b, ((contract[0:1], contract[1:2]), ((), ())),
        preferred_element_type=F32,
    )


def split(x):
    high = x.astype(BF16)
    return high, (x - high.astype(F32)).astype(BF16)


def dot_in_three(a, b, contract):
    high, low = split(b)
    parts = both_halves(a)
    rows = a.shape[0]
    first = dot(parts, high, contract)
    return first[:rows] + first[rows:] + dot(parts[:rows], low, contract)


def both_halves(x):
    high, low = split(x)
    return jnp.concatenate([high, low], axis=0)


def slot_rows(onehot, fields):
    product = dot(onehot, both_halves(fields), (1, 1))
    product = product + pltpu.roll(product, HALF, 1)
    rows = product.shape[0] // 2
    return jnp.where(iota((rows, 2 * HALF), 1) < HALF, product[:rows], product[rows:])


def padded(fields):
    return jnp.concatenate([fields, jnp.zeros((HALF - fields.shape[0], fields.shape[1]), F32)], axis=0)


def iota(shape, dim):
    return lax.broadcasted_iota(jnp.int32, shape, dim)


def edges_kernel(edge_ref, out_ref):
    crm_levels = out_ref.shape[0]
    shape = (crm_levels, edge_ref.shape[2])
    levels = shape[1] // 2
    lane = iota(shape, 1)
    weight = jnp.where(
        lane < levels,
        mixing(0) * interp(iota(shape, 0), lane, crm_levels, levels),
        mixing(1) * interp(iota(shape, 0), lane - levels, crm_levels, levels),
    )
    out_ref[...] = dot_in_three(weight, edge_ref[...].reshape(-1, shape[1]), (1, 1))


def route_kernel(peers, capacity, me_ref, routes_ref, branch_ref, neigh_ref, gcm_ref, own_ref,
                 pos_ref, base_ref, halo_map_ref):
    columns = routes_ref.shape[1]
    elems = columns // 4
    crm_levels = own_ref.shape[0]
    slots = peers * capacity
    half = capacity // 2
    me = me_ref[0]
    destination = routes_ref[...]
    named = iota((peers, columns), 0) == destination
    earlier = (iota((columns, columns), 0) < iota((columns, columns), 1)).astype(BF16)
    before = dot(named.astype(BF16), earlier, (1, 0))
    rank = jnp.sum(jnp.where(named, before, 0.0), axis=0, keepdims=True).astype(jnp.int32)
    upper = (rank >= half).astype(jnp.int32)
    position = upper * (slots // 2) + destination * half + rank - upper * half
    pos_ref[...] = position
    place = (iota((slots, columns), 0) == position).astype(BF16)

    target = jnp.concatenate([neigh_ref[j : j + 1, :] for j in range(4)], axis=1)
    owner = target // columns
    edge = target - owner * columns
    block = jnp.where(owner == me, 0, jnp.where(owner == (me ^ 1), 1, 2))
    source = block * columns + edge
    window = iota((3 * columns, columns), 0)
    local = iota((1, columns), 1)
    local = 4 * (local % elems) + local // elems
    chosen = (window == source).astype(F32) + (window == local).astype(F32)
    column = iota((columns, columns), 0)
    row = iota((columns, columns), 1)
    first = (column % 4) * elems + column // 4
    second = ((column + 1) % 4) * elems + column // 4
    pair = ((row == first) | (row == second)).astype(BF16)
    mapped = dot(pair, chosen.astype(BF16), (1, 1)).astype(BF16)
    halo_map_ref[...] = dot(place, mapped[:, columns:], (1, 0)).astype(BF16)

    levels = gcm_ref.shape[0] // NV
    mixed = mixing(0) * gcm_ref[:levels, :]
    for k in range(1, NV):
        mixed += mixing(k) * gcm_ref[pl.ds(k * levels, levels), :]
    shape = (crm_levels, levels)
    force = dot_in_three(interp(iota(shape, 0), iota(shape, 1), crm_levels, levels), mixed, (1, 0))
    for part in split(own_ref[...]):
        force += 0.25 * dot(part, mapped[:, :columns], (1, 1))
    code = (branch_ref[...] + 1).astype(F32)
    base_ref[...] = slot_rows(place, padded(jnp.concatenate([force, code], axis=0)))


def outgoing_kernel(base_ref, map_ref, other_ref, pair_ref, _, out_ref):
    window = jnp.concatenate([pair_ref[...], other_ref[...]], axis=1)
    out_ref[...] = base_ref[...] + 0.25 * slot_rows(map_ref[...], padded(window))


class Field:
    def __init__(self, total):
        self.total, self.rows, self.diagonals = total, [], []

    def five(self, z):
        while len(self.diagonals) < z + 2:
            at = len(self.diagonals)
            below, here = self.rows[max(at - 1, 0)], self.rows[min(at, self.total - 1)]
            right = here[1:] + [pltpu.roll(here[0], 7, 0)]
            self.diagonals.append([a + b for a, b in zip(below, right)])
        low, high = self.diagonals[z], self.diagonals[z + 1]
        high = [pltpu.roll(high[-1], 1, 0)] + high[:-1]
        return [row + (a + b) for row, a, b in zip(self.rows[z], low, high)]


def five_points(row, up, down):
    left = [pltpu.roll(row[-1], 1, 0)] + row[:-1]
    right = row[1:] + [pltpu.roll(row[0], 7, 0)]
    return [(a + b + c) + (d + e) for a, b, c, d, e in zip(row, left, right, up, down)]


def add_up(values):
    while len(values) > 1:
        values = [a + b for a, b in zip(values[::2], values[1::2])]
    return values[0]


def rows_of_sums(ref, crm_levels):
    return add_up([ref[pl.ds(s, crm_levels, stride=8), :] for s in range(8)])


def saturation(z, crm_levels):
    return 1.0 - z * (2.0 / (crm_levels - 1))


def levels_of(crm_levels):
    return iota((crm_levels, LANES), 0)


def shifted(x):
    return jnp.concatenate([x[:1], x[:-1]], axis=0) + jnp.concatenate([x[1:], x[-1:]], axis=0)


def before_kernel(start, state_ref, first_ref, sums_ref, kept_ref, part_ref, kept_sums_ref, new_ref, sems, done_sems):
    blocks, _, crm_levels, width, _ = kept_ref.shape
    count = width // 8

    def copy(j):
        lanes = pl.ds(pl.multiple_of((start + j) * LANES, LANES), LANES)
        return pltpu.make_async_copy(state_ref.at[:, :, :, lanes], kept_ref.at[j], sems.at[j])

    def done(j):
        return pltpu.make_async_copy(new_ref.at[j], first_ref.at[j], done_sems.at[j])

    for j in range(blocks):
        copy(j).start()

    def block(j, _):
        copy(j).wait()
        dry = Field(crm_levels)
        for i in range(crm_levels + 1):
            if i < crm_levels:
                heat = [kept_ref[j, 0, i, pl.ds(k, 8, stride=count), :] for k in range(count)]
                moist = [kept_ref[j, 1, i, pl.ds(k, 8, stride=count), :] for k in range(count)]
                dry.rows.append([m - 0.3 * h for h, m in zip(heat, moist)])
                part_ref[0, pl.ds(8 * i, 8), :] = add_up(dry.rows[i])
                part_ref[1, pl.ds(8 * i, 8), :] = add_up(heat)
            if i:
                for k, total in enumerate(dry.five(i - 1)):
                    new_ref[j, i - 1, k] = (0.2 * LOG2E) * total
        done(j).start()
        level = saturation(levels_of(crm_levels).astype(F32), crm_levels)
        dry_mean = rows_of_sums(part_ref.at[0], crm_levels) * (1.0 / width)
        start = dry_mean + rows_of_sums(part_ref.at[1], crm_levels) * (2.3 / width)
        q = start
        for _ in range(STEPS):
            q = 0.6 * q + 0.2 * shifted(q)
        kept_sums_ref[j, 0] = LOG2E * (dry_mean - level)
        kept_sums_ref[j, 1] = q - start
        return 0

    lax.fori_loop(0, blocks, block, 0)
    sums = pltpu.make_async_copy(kept_sums_ref, sums_ref, done_sems.at[blocks])
    sums.start()
    for j in range(blocks):
        done(j).wait()
    sums.wait()


def lane_maps(rows, capacity):
    half = capacity // 2
    row = iota((rows, LANES), 0)
    slot = iota((rows, LANES), 1)
    rank = slot % capacity
    low = (row == (slot // capacity) * half + rank) & (rank < half)
    high = (row == (slot // capacity) * half + rank - half) & (rank >= half)
    return low.astype(BF16), high.astype(BF16)


def bounds(crm_levels):
    level = levels_of(crm_levels)
    edge = (0.4 / (crm_levels - 1)) * LOG2E
    return jnp.where(level == 0, -edge, 0.0) + jnp.where(level == crm_levels - 1, edge, 0.0)


def dried(crm_levels):
    return LOG2E * saturation(levels_of(crm_levels).astype(F32), crm_levels)


def respond(force):
    q = jnp.zeros_like(force)
    for _ in range(STEPS):
        q = 0.6 * q + 0.2 * shifted(q) + 0.5 * force
    return q


def rate_of(code):
    return 0.15 + 0.25 * (code == 2.0).astype(F32)


def cloud_kernel(capacity, arrived_ref, near_ref, near_sums_ref, far_ref, far_sums_ref, last_ref, force_ref, code_ref, rain_ref,
                 reply_ref, push_ref, part_ref, sums_ref, first_ref, sems):
    blocks, crm_levels, count = last_ref.shape[:3]
    near = near_ref.shape[0]
    width = count * 8
    part = arrived_ref.shape[0] // blocks

    def load(j):
        source = near_ref.at[j] if j < near else far_ref.at[j - near]
        return pltpu.make_async_copy(source, first_ref.at[j], sems.at[j])

    load_sums = [
        pltpu.make_async_copy(near_sums_ref, sums_ref.at[pl.ds(0, near)], sems.at[blocks]),
        pltpu.make_async_copy(far_sums_ref, sums_ref.at[pl.ds(near, blocks - near)], sems.at[blocks + 1]),
    ]
    for j in range(blocks):
        load(j).start()
    for copy in load_sums:
        copy.start()
    low, high = lane_maps(part, capacity)
    maps = jnp.concatenate([low, high], axis=1)
    maps = jnp.concatenate([maps, maps], axis=0)
    for j in range(blocks):
        got = dot(both_halves(arrived_ref[pl.ds(j * part, part), :]), maps, (0, 0))
        got = got[:HALF, :LANES] + got[HALF:, LANES:]
        push = (-0.65 * LOG2E) * got[:crm_levels]
        push_ref[j, 0] = push - dried(crm_levels)
        push_ref[j, 1] = push + bounds(crm_levels)
        force_ref[j] = got[:crm_levels]
        code_ref[j] = got[crm_levels : crm_levels + 1]

    def block(j, _):
        pltpu.make_async_copy(far_ref.at[0], first_ref.at[j], sems.at[j]).wait()
        lowered = jnp.broadcast_to((1.15 * LOG2E) * rate_of(code_ref[j]), (8, LANES))
        fields = [Field(crm_levels) for _ in range(STEPS)]
        for i in range(crm_levels + STEPS - 1):
            for t in range(STEPS):
                z = i - t
                if not 0 <= z < crm_levels:
                    continue
                push = jnp.broadcast_to(push_ref[j, min(t, 1), pl.ds(z, 1), :], (8, LANES))
                if t == 0:
                    values = [first_ref[j, z, k] + push for k in range(count)]
                else:
                    values = [0.2 * total + push for total in fields[t - 1].five(z)]
                values = [y - lowered * jnp.log(1.0 + jnp.exp2(y)) for y in values]
                fields[t].rows.append(values)
                if t == STEPS - 1:
                    for k in range(count):
                        last_ref[j, z, k] = values[k]
                    part_ref[j, pl.ds(8 * z, 8), :] = add_up(values)
        return 0

    lax.fori_loop(0, blocks, block, 0)
    for copy in load_sums:
        copy.wait()
    turned = jnp.concatenate([low, high], axis=0)
    for j in range(blocks):
        dg = rows_of_sums(part_ref.at[j], crm_levels) * (1.0 / width) - sums_ref[j, 0]
        answer = (0.7 / 2.3) * (sums_ref[j, 1] + respond(force_ref[j])) - (3.0 / (2.3 * LOG2E)) * dg
        reply_ref[pl.ds(j * part, part), :] = slot_rows(turned, padded(answer))
        budget = (-0.65 * LOG2E * STEPS) * force_ref[j] - dg
        rain = jnp.sum(budget, axis=0, keepdims=True) * (1.0 / (1.15 * LOG2E * crm_levels))
        rain_ref[j] = jnp.where(code_ref[j] > 0.0, rain, 0.0)


def after_kernel(state_ref, last_ref, force_ref, code_ref, guess_ref, out_ref, rain_ref,
                 kept_ref, new_ref, row_ref, push_ref, field_ref, sems, done_sems):
    blocks, _, crm_levels, width, _ = kept_ref.shape
    count = width // 8
    pieces = sems.shape[1]
    piece = crm_levels // pieces

    def lanes(j):
        return pl.ds(pl.multiple_of(j * LANES, LANES), LANES)

    def load(j, p):
        at = pl.ds(p * piece, piece)
        return pltpu.make_async_copy(
            state_ref.at[:, at, :, lanes(j)], kept_ref.at[j, :, at, :, :], sems.at[j, p]
        )

    def store(j, p):
        at = pl.ds(p * piece, piece)
        return pltpu.make_async_copy(
            new_ref.at[j, :, at, :, :], out_ref.at[:, at, :, lanes(j)], done_sems.at[j, p]
        )

    for j in range(blocks):
        for p in range(pieces):
            load(j, p).start()
    rain_ref[...] = guess_ref[...]
    for j in range(blocks):
        row_ref[j] = respond(force_ref[j])
    rows = [guess_ref[j] / rate_of(code_ref[j]) for j in range(blocks)]
    marks = [jnp.where(code_ref[j] > 0.0, row, -2.0) for j, row in enumerate(rows)]
    wettest = [jnp.max(mark, axis=1, keepdims=True) for mark in marks]
    dry = [((w > -1.0) & (w < SMALL_RAIN)).astype(jnp.int32) for w in wettest]
    some_dry = jnp.max(functools.reduce(jnp.maximum, dry)) > 0

    def block(j, _):
        occupied = jnp.broadcast_to(code_ref[j], (8, LANES)) > 0.0
        fields = [Field(crm_levels) for _ in range(STEPS + 1)]
        for i in range(crm_levels + STEPS):
            if i < crm_levels:
                if i % piece == 0:
                    load(j, i // piece).wait()
                heat = [kept_ref[j, 0, i, pl.ds(k, 8, stride=count), :] for k in range(count)]
                moist = [kept_ref[j, 1, i, pl.ds(k, 8, stride=count), :] for k in range(count)]
                fields[0].rows.append([(h + h) + m for h, m in zip(heat, moist)])
            for t in range(1, STEPS + 1):
                z = i - t
                if 0 <= z < crm_levels:
                    fields[t].rows.append(fields[t - 1].five(z))
            if not 0 <= z < crm_levels:
                continue
            row = jnp.broadcast_to(row_ref[j, pl.ds(z, 1), :], (8, LANES))
            for k, total in enumerate(fields[STEPS].rows[z]):
                at = pl.ds(k, 8, stride=count)
                linear = (1.0 / 125.0) * total + row
                dry = (1.0 / LOG2E) * last_ref[j, z, k] + saturation(z, crm_levels)
                heat = (1.0 / 2.3) * (linear - dry)
                moist = dry + 0.3 * heat
                new_ref[j, 0, z, at, :] = jnp.where(occupied, heat, kept_ref[j, 0, z, at, :])
                new_ref[j, 1, z, at, :] = jnp.where(occupied, moist, kept_ref[j, 1, z, at, :])
            if z % piece == piece - 1:
                store(j, z // piece).start()
        return 0

    lax.fori_loop(0, blocks, block, 0)

    def again(j, _):
        rate = rate_of(code_ref[j])
        lowered = jnp.broadcast_to((1.15 * LOG2E) * rate, (8, LANES))
        push = (-0.65 * LOG2E) * force_ref[j]
        push_ref[0] = push - dried(crm_levels)
        push_ref[1] = push + bounds(crm_levels)

        def condense(y, acc):
            e = jnp.exp2(y)
            amount = jnp.where(e < 2.0**-8, e * (1.0 - 0.5 * e), jnp.log(1.0 + e))
            return y - lowered * amount, acc + amount

        def start(z, _):
            for k in range(count):
                at = pl.ds(k, 8, stride=count)
                field_ref[0, z, k] = LOG2E * (kept_ref[j, 1, z, at, :] - 0.3 * kept_ref[j, 0, z, at, :])
            return 0

        def step(source, target, which):
            def body(z, acc):
                push = jnp.broadcast_to(push_ref[which, pl.ds(z, 1), :], (8, LANES))
                at = (z, jnp.maximum(z - 1, 0), jnp.minimum(z + 1, crm_levels - 1))
                totals = five_points(*[[field_ref[source, y, k] for k in range(count)] for y in at])
                new = []
                for k in range(count):
                    field_ref[target, z, k], total = condense(0.2 * totals[k] + push, acc[k])
                    new.append(total)
                return tuple(new)
            return body

        acc = tuple(jnp.zeros((8, LANES), F32) for _ in range(count))
        lax.fori_loop(0, crm_levels, start, 0)
        for t in range(STEPS):
            acc = lax.fori_loop(0, crm_levels, step(t % 2, (t + 1) % 2, min(t, 1)), acc)
        mean = jnp.sum(add_up(list(acc)), axis=0, keepdims=True) * (1.0 / (crm_levels * width))
        rain_ref[j] = jnp.where(code_ref[j] > 0.0, rate * mean, 0.0)
        return 0

    @pl.when(some_dry)
    def _():
        lax.fori_loop(0, blocks, again, 0)

    for j in range(blocks):
        for p in range(pieces):
            store(j, p).wait()


def tendency_kernel(crm_levels, pos_ref, returned_ref, out_ref, new_ref, sems):
    levels = out_ref.shape[0] // NV
    rows = returned_ref.shape[0]
    columns = pos_ref.shape[1]
    place = (iota((2 * rows, columns), 0) == pos_ref[...]).astype(BF16)
    shape = (levels, 2 * HALF)
    lane, level = iota(shape, 1), iota(shape, 0)
    table = [
        jnp.where((lane >= at) & (lane < at + crm_levels), interp(lane - at, level, crm_levels, levels), 0.0)
        for at in (0, HALF)
    ]
    spread = dot_in_three(jnp.concatenate(table, axis=0), returned_ref[...], (1, 1))
    parts = both_halves(jnp.concatenate([spread[:levels], spread[levels:]], axis=1))
    answer = dot(parts, place, (1, 0))
    answer = answer[:levels] + answer[levels:]
    copies = []
    for k in range(NV):
        new_ref[k] = mixing(k) * answer
        copies.append(
            pltpu.make_async_copy(new_ref.at[k], out_ref.at[pl.ds(k * levels, levels), :], sems.at[k])
        )
        copies[k].start()
    for copy in copies:
        copy.wait()


def call(kernel, out, scratch=(), cost=(0, 0, 0), vmem=32, **specs):
    return pl.pallas_call(
        kernel, out_shape=out, scratch_shapes=list(scratch),
        cost_estimate=pl.CostEstimate(flops=int(cost[0]), bytes_accessed=int(cost[1]), transcendentals=int(cost[2])),
        compiler_params=pltpu.CompilerParams(vmem_limit_bytes=vmem * 2**20), **specs,
    )


def from_hbm(*arrays):
    return [pltpu.with_memory_space_constraint(x, pltpu.HBM) for x in arrays]


HBM = pl.BlockSpec(memory_space=pltpu.HBM)
VMEM = pl.BlockSpec(memory_space=pltpu.VMEM)


def cloud_before(crm_state, start, blocks):
    _, crm_levels, width, _ = crm_state.shape
    cells = crm_levels * width * blocks * LANES
    field = (blocks, crm_levels, width // 8, 8, LANES)
    sums = (blocks, 2, crm_levels, LANES)
    return call(
        functools.partial(before_kernel, start),
        (pltpu.HBM(field, F32), pltpu.HBM(sums, F32)),
        [
            pltpu.VMEM((blocks, 2, crm_levels, width, LANES), F32),
            pltpu.VMEM((2, crm_levels * 8, LANES), F32),
            pltpu.VMEM(sums, F32),
            pltpu.VMEM(field, F32),
            pltpu.SemaphoreType.DMA((blocks,)),
            pltpu.SemaphoreType.DMA((blocks + 1,)),
        ],
        (cells * 25, cells * 8, 0),
        in_specs=[HBM],
        out_specs=[HBM] * 2,
    )(*from_hbm(crm_state))


def cloud_steps(capacity, arrived, near, near_sums, far, far_sums):
    blocks = near.shape[0] + far.shape[0]
    crm_levels, count = far.shape[1:3]
    cells = crm_levels * count * 8 * blocks * LANES
    sums = (blocks,) + far_sums.shape[1:]
    return call(
        functools.partial(cloud_kernel, capacity),
        (
            pltpu.VMEM((blocks,) + far.shape[1:], F32),
            pltpu.VMEM((blocks, crm_levels, LANES), F32),
            pltpu.VMEM((blocks, 1, LANES), F32),
            pltpu.VMEM((blocks, 1, LANES), F32),
            jax.ShapeDtypeStruct(arrived.shape, F32),
        ),
        [
            pltpu.VMEM(sums, F32),
            pltpu.VMEM((blocks, crm_levels * 8, LANES), F32),
            pltpu.VMEM(sums, F32),
            pltpu.VMEM((blocks,) + far.shape[1:], F32),
            pltpu.SemaphoreType.DMA((blocks + 2,)),
        ],
        (cells * 30, cells * 8, cells * 6),
        in_specs=[VMEM] + [HBM] * 4,
        out_specs=[VMEM] * 5,
    )(arrived, *from_hbm(near, near_sums, far, far_sums))


def cloud_after(crm_state, last, force, code, rain):
    _, crm_levels, width, slots = crm_state.shape
    blocks = slots // LANES
    pieces = 1
    cells = crm_levels * width * slots
    return call(
        after_kernel,
        (jax.ShapeDtypeStruct(crm_state.shape, F32), jax.ShapeDtypeStruct((blocks, 1, LANES), F32)),
        [pltpu.VMEM((blocks, 2, crm_levels, width, LANES), F32)] * 2
        + [
            pltpu.VMEM((blocks, crm_levels, LANES), F32),
            pltpu.VMEM((2, crm_levels, LANES), F32),
            pltpu.VMEM((2,) + last.shape[1:], F32),
        ]
        + [pltpu.SemaphoreType.DMA((blocks, pieces))] * 2,
        (cells * 10, cells * 8, 0),
        in_specs=[HBM] + [VMEM] * 4,
        out_specs=[HBM, VMEM],
    )(*from_hbm(crm_state), last, force, code, rain)


def on_device(gcm_state, edge_part, neighbours, branch, routes, crm_state):
    peers = lax.axis_size(AXES)
    me = lax.axis_index(AXES)
    columns, features = gcm_state.shape
    _, crm_levels, _, slots = crm_state.shape
    capacity = slots // peers
    rows = slots // 2
    shape = jax.ShapeDtypeStruct

    own = call(edges_kernel, shape((crm_levels, columns), F32), cost=(1e7, 4e5, 0))(
        *from_hbm(edge_part)
    )
    other = lax.ppermute(own, AXES, [(i, (((i + 1) ^ 1) - 1) % peers) for i in range(peers)])
    pair = lax.ppermute(own, AXES, [(i, i ^ 1) for i in range(peers)])
    position, base, halo_map = call(
        functools.partial(route_kernel, peers, capacity),
        (
            shape((1, columns), jnp.int32),
            shape((rows, LANES), F32),
            shape((slots, 2 * columns), BF16),
        ),
        cost=(2e9, 2e6, 0),
        in_specs=[pl.BlockSpec(memory_space=pltpu.SMEM)] + [VMEM] * 5,
        out_specs=[VMEM] * 3,
    )(
        me.reshape(1),
        *from_hbm(routes.T, branch.reshape(1, -1), neighbours.T, gcm_state.T),
        own,
    )
    near, near_sums = cloud_before(crm_state, 0, 1)
    outgoing = call(
        outgoing_kernel, shape((rows, LANES), F32), cost=(2e8, 1e6, 0),
        in_specs=[VMEM] * 4 + [HBM], out_specs=VMEM,
    )(base, halo_map, other, pair, *from_hbm(near))
    far, far_sums = cloud_before(crm_state, 1, slots // LANES - 1)
    arrived = lax.all_to_all(outgoing.reshape(peers, capacity // 2, LANES), AXES, 0, 0, tiled=True)
    last, force, code, rain, reply = cloud_steps(
        capacity, arrived.reshape(rows, LANES), near, near_sums, far, far_sums
    )
    returned = lax.all_to_all(reply.reshape(peers, capacity // 2, LANES), AXES, 0, 0, tiled=True)
    updated, rain = cloud_after(crm_state, last, force, code, rain)
    levels = features // NV
    tendency = call(
        functools.partial(tendency_kernel, crm_levels),
        shape((features, columns), F32),
        [pltpu.VMEM((NV, levels, columns), F32), pltpu.SemaphoreType.DMA((NV,))],
        (1e8, 1e6, 0),
        in_specs=[VMEM] * 2,
        out_specs=HBM,
    )(position, returned.reshape(rows, LANES))
    return (tendency.T, updated, rain.reshape(1, slots))


def solution(mesh):
    in_specs = (
        P(AXES, None),
        P(AXES, None, None),
        P(AXES, None),
        P(AXES),
        P(AXES, None),
        P(None, None, None, AXES),
    )
    out_specs = (
        P(AXES, None),
        P(None, None, None, AXES),
        P(AXES, None),
    )
    return jax.shard_map(
        on_device, mesh=mesh, in_specs=in_specs, out_specs=out_specs, check_vma=False
    )
```

```python
import functools

import jax
import jax.numpy as jnp
import numpy as np
from jax import lax
from jax.experimental import pallas as pl
from jax.experimental.pallas import tpu as pltpu
from jax.sharding import PartitionSpec as P

NV = 8
STEPS = 3
AXES = ("elem", "sub")
LANES = 128
HALF = 64
LOG2E = 1.4426950408889634
F32 = jnp.float32
BF16 = jnp.bfloat16
SMALL_RAIN = 0.2


def mixing(k):
    return (0.8 + 0.05 * k) * (1.0 if k % 2 == 0 else -1.0) / float(np.sqrt(float(NV)))


def interp(z, level, crm_levels, levels):
    position = z.astype(F32) * ((levels - 1) / (crm_levels - 1))
    return jnp.maximum(0.0, 1.0 - jnp.abs(position - level.astype(F32)))


def dot(a, b, contract):
    return lax.dot_general(
        a, b, ((contract[0:1], contract[1:2]), ((), ())),
        preferred_element_type=F32,
    )


def split(x):
    high = x.astype(BF16)
    return high, (x - high.astype(F32)).astype(BF16)


def dot_in_three(a, b, contract):
    high, low = split(b)
    parts = both_halves(a)
    rows = a.shape[0]
    first = dot(parts, high, contract)
    return first[:rows] + first[rows:] + dot(parts[:rows], low, contract)


def both_halves(x):
    high, low = split(x)
    return jnp.concatenate([high, low], axis=0)


def slot_rows(onehot, fields):
    product = dot(onehot, both_halves(fields), (1, 1))
    product = product + pltpu.roll(product, HALF, 1)
    rows = product.shape[0] // 2
    return jnp.where(iota((rows, 2 * HALF), 1) < HALF, product[:rows], product[rows:])


def padded(fields):
    return jnp.concatenate([fields, jnp.zeros((HALF - fields.shape[0], fields.shape[1]), F32)], axis=0)


def iota(shape, dim):
    return lax.broadcasted_iota(jnp.int32, shape, dim)


def edges_kernel(edge_ref, out_ref):
    crm_levels = out_ref.shape[0]
    shape = (crm_levels, edge_ref.shape[2])
    levels = shape[1] // 2
    lane = iota(shape, 1)
    weight = jnp.where(
        lane < levels,
        mixing(0) * interp(iota(shape, 0), lane, crm_levels, levels),
        mixing(1) * interp(iota(shape, 0), lane - levels, crm_levels, levels),
    )
    out_ref[...] = dot_in_three(weight, edge_ref[...].reshape(-1, shape[1]), (1, 1))


def outgoing_kernel(base_ref, map_ref, other_ref, pair_ref, out_ref):
    window = jnp.concatenate([pair_ref[...], other_ref[...]], axis=1)
    out_ref[...] = base_ref[...] + 0.25 * slot_rows(map_ref[...], padded(window))


class Field:
    def __init__(self, total):
        self.total, self.rows, self.diagonals = total, [], []

    def five(self, z):
        while len(self.diagonals) < z + 2:
            at = len(self.diagonals)
            below, here = self.rows[max(at - 1, 0)], self.rows[min(at, self.total - 1)]
            right = here[1:] + [pltpu.roll(here[0], 7, 0)]
            self.diagonals.append([a + b for a, b in zip(below, right)])
        low, high = self.diagonals[z], self.diagonals[z + 1]
        high = [pltpu.roll(high[-1], 1, 0)] + high[:-1]
        return [row + (a + b) for row, a, b in zip(self.rows[z], low, high)]


def five_points(row, up, down):
    left = [pltpu.roll(row[-1], 1, 0)] + row[:-1]
    right = row[1:] + [pltpu.roll(row[0], 7, 0)]
    return [(a + b + c) + (d + e) for a, b, c, d, e in zip(row, left, right, up, down)]


def add_up(values):
    while len(values) > 1:
        values = [a + b for a, b in zip(values[::2], values[1::2])]
    return values[0]


def rows_of_sums(ref, crm_levels):
    return add_up([ref[pl.ds(s, crm_levels, stride=8), :] for s in range(8)])


def saturation(z, crm_levels):
    return 1.0 - z * (2.0 / (crm_levels - 1))


def levels_of(crm_levels):
    return iota((crm_levels, LANES), 0)


def shifted(x):
    return jnp.concatenate([x[:1], x[:-1]], axis=0) + jnp.concatenate([x[1:], x[-1:]], axis=0)


def route(peers, capacity, me_ref, routes_ref, branch_ref, neigh_ref, gcm_ref, own_ref,
          pos_ref, base_ref, halo_map_ref):
    columns = routes_ref.shape[1]
    elems = columns // 4
    crm_levels = own_ref.shape[0]
    slots = peers * capacity
    half = capacity // 2
    me = me_ref[0]
    destination = routes_ref[...]
    named = iota((peers, columns), 0) == destination
    earlier = (iota((columns, columns), 0) < iota((columns, columns), 1)).astype(BF16)
    before = dot(named.astype(BF16), earlier, (1, 0))
    rank = jnp.sum(jnp.where(named, before, 0.0), axis=0, keepdims=True).astype(jnp.int32)
    upper = (rank >= half).astype(jnp.int32)
    position = upper * (slots // 2) + destination * half + rank - upper * half
    pos_ref[...] = position
    place = (iota((slots, columns), 0) == position).astype(BF16)

    target = jnp.concatenate([neigh_ref[j : j + 1, :] for j in range(4)], axis=1)
    owner = target // columns
    edge = target - owner * columns
    block = jnp.where(owner == me, 0, jnp.where(owner == (me ^ 1), 1, 2))
    source = block * columns + edge
    window = iota((3 * columns, columns), 0)
    local = iota((1, columns), 1)
    local = 4 * (local % elems) + local // elems
    chosen = (window == source).astype(F32) + (window == local).astype(F32)
    column = iota((columns, columns), 0)
    row = iota((columns, columns), 1)
    first = (column % 4) * elems + column // 4
    second = ((column + 1) % 4) * elems + column // 4
    pair = ((row == first) | (row == second)).astype(BF16)
    mapped = dot(pair, chosen.astype(BF16), (1, 1)).astype(BF16)
    halo_map_ref[...] = dot(place, mapped[:, columns:], (1, 0)).astype(BF16)

    levels = gcm_ref.shape[0] // NV
    mixed = mixing(0) * gcm_ref[:levels, :]
    for k in range(1, NV):
        mixed += mixing(k) * gcm_ref[pl.ds(k * levels, levels), :]
    shape = (crm_levels, levels)
    force = dot_in_three(interp(iota(shape, 0), iota(shape, 1), crm_levels, levels), mixed, (1, 0))
    for part in split(own_ref[...]):
        force += 0.25 * dot(part, mapped[:, :columns], (1, 1))
    code = (branch_ref[...] + 1).astype(F32)
    base_ref[...] = slot_rows(place, padded(jnp.concatenate([force, code], axis=0)))


def before_kernel(peers, capacity, me_ref, routes_ref, branch_ref, neigh_ref, gcm_ref, own_ref, state_ref,
                  pos_ref, base_ref, halo_map_ref, first_ref, sums_ref,
                  near_routes_ref, near_branch_ref, near_neigh_ref, near_gcm_ref, kept_ref, part_ref, sems):
    blocks, _, crm_levels, width, _ = kept_ref.shape
    count = width // 8

    def copy(j):
        lanes = pl.ds(pl.multiple_of(j * LANES, LANES), LANES)
        return pltpu.make_async_copy(state_ref.at[:, :, :, lanes], kept_ref.at[j], sems.at[j])

    near = (near_routes_ref, near_branch_ref, near_neigh_ref, near_gcm_ref)
    loads = [
        pltpu.make_async_copy(far_ref, near_ref, sems.at[blocks + i])
        for i, (far_ref, near_ref) in enumerate(zip((routes_ref, branch_ref, neigh_ref, gcm_ref), near))
    ]
    for load in loads:
        load.start()
    for j in range(blocks):
        copy(j).start()
    for load in loads:
        load.wait()
    route(peers, capacity, me_ref, *near, own_ref, pos_ref, base_ref, halo_map_ref)

    def block(j, _):
        copy(j).wait()
        dry = Field(crm_levels)
        for i in range(crm_levels + 1):
            if i < crm_levels:
                heat = [kept_ref[j, 0, i, pl.ds(k, 8, stride=count), :] for k in range(count)]
                moist = [kept_ref[j, 1, i, pl.ds(k, 8, stride=count), :] for k in range(count)]
                dry.rows.append([m - 0.3 * h for h, m in zip(heat, moist)])
                part_ref[0, pl.ds(8 * i, 8), :] = add_up(dry.rows[i])
                part_ref[1, pl.ds(8 * i, 8), :] = add_up(heat)
            if i:
                for k, total in enumerate(dry.five(i - 1)):
                    first_ref[j, i - 1, k] = (0.2 * LOG2E) * total
        level = saturation(levels_of(crm_levels).astype(F32), crm_levels)
        dry_mean = rows_of_sums(part_ref.at[0], crm_levels) * (1.0 / width)
        start = dry_mean + rows_of_sums(part_ref.at[1], crm_levels) * (2.3 / width)
        q = start
        for _ in range(STEPS):
            q = 0.6 * q + 0.2 * shifted(q)
        sums_ref[j, 0] = LOG2E * (dry_mean - level)
        sums_ref[j, 1] = q - start
        return 0

    lax.fori_loop(0, blocks, block, 0)


def lane_maps(rows, capacity):
    half = capacity // 2
    row = iota((rows, LANES), 0)
    slot = iota((rows, LANES), 1)
    rank = slot % capacity
    low = (row == (slot // capacity) * half + rank) & (rank < half)
    high = (row == (slot // capacity) * half + rank - half) & (rank >= half)
    return low.astype(BF16), high.astype(BF16)


def bounds(crm_levels):
    level = levels_of(crm_levels)
    edge = (0.4 / (crm_levels - 1)) * LOG2E
    return jnp.where(level == 0, -edge, 0.0) + jnp.where(level == crm_levels - 1, edge, 0.0)


def dried(crm_levels):
    return LOG2E * saturation(levels_of(crm_levels).astype(F32), crm_levels)


def respond(force):
    q = jnp.zeros_like(force)
    for _ in range(STEPS):
        q = 0.6 * q + 0.2 * shifted(q) + 0.5 * force
    return q


def rate_of(code):
    return 0.15 + 0.25 * (code == 2.0).astype(F32)


def cloud_kernel(capacity, arrived_ref, first_ref, sums_ref, last_ref, force_ref, code_ref, rain_ref,
                 reply_ref, push_ref, part_ref):
    blocks, crm_levels, count = last_ref.shape[:3]
    width = count * 8
    part = arrived_ref.shape[0] // blocks
    low, high = lane_maps(part, capacity)
    maps = jnp.concatenate([low, high], axis=1)
    maps = jnp.concatenate([maps, maps], axis=0)
    for j in range(blocks):
        got = dot(both_halves(arrived_ref[pl.ds(j * part, part), :]), maps, (0, 0))
        got = got[:HALF, :LANES] + got[HALF:, LANES:]
        push = (-0.65 * LOG2E) * got[:crm_levels]
        push_ref[j, 0] = push - dried(crm_levels)
        push_ref[j, 1] = push + bounds(crm_levels)
        force_ref[j] = got[:crm_levels]
        code_ref[j] = got[crm_levels : crm_levels + 1]

    def block(j, _):
        lowered = jnp.broadcast_to((1.15 * LOG2E) * rate_of(code_ref[j]), (8, LANES))
        fields = [Field(crm_levels) for _ in range(STEPS)]
        for i in range(crm_levels + STEPS - 1):
            for t in range(STEPS):
                z = i - t
                if not 0 <= z < crm_levels:
                    continue
                push = jnp.broadcast_to(push_ref[j, min(t, 1), pl.ds(z, 1), :], (8, LANES))
                if t == 0:
                    values = [first_ref[j, z, k] + push for k in range(count)]
                else:
                    values = [0.2 * total + push for total in fields[t - 1].five(z)]
                values = [y - lowered * jnp.log(1.0 + jnp.exp2(y)) for y in values]
                fields[t].rows.append(values)
                if t == STEPS - 1:
                    for k in range(count):
                        last_ref[j, z, k] = values[k]
                    part_ref[j, pl.ds(8 * z, 8), :] = add_up(values)
        return 0

    lax.fori_loop(0, blocks, block, 0)
    turned = jnp.concatenate([low, high], axis=0)
    for j in range(blocks):
        dg = rows_of_sums(part_ref.at[j], crm_levels) * (1.0 / width) - sums_ref[j, 0]
        answer = (0.7 / 2.3) * (sums_ref[j, 1] + respond(force_ref[j])) - (3.0 / (2.3 * LOG2E)) * dg
        reply_ref[pl.ds(j * part, part), :] = slot_rows(turned, padded(answer))
        budget = (-0.65 * LOG2E * STEPS) * force_ref[j] - dg
        rain = jnp.sum(budget, axis=0, keepdims=True) * (1.0 / (1.15 * LOG2E * crm_levels))
        rain_ref[j] = jnp.where(code_ref[j] > 0.0, rain, 0.0)


def after_kernel(state_ref, last_ref, force_ref, code_ref, guess_ref, out_ref, rain_ref,
                 kept_ref, new_ref, row_ref, push_ref, field_ref, sems, done_sems):
    blocks, _, crm_levels, width, _ = kept_ref.shape
    count = width // 8
    pieces = sems.shape[1]
    piece = crm_levels // pieces

    def lanes(j):
        return pl.ds(pl.multiple_of(j * LANES, LANES), LANES)

    def load(j, p):
        at = pl.ds(p * piece, piece)
        return pltpu.make_async_copy(
            state_ref.at[:, at, :, lanes(j)], kept_ref.at[j, :, at, :, :], sems.at[j, p]
        )

    def store(j, p):
        at = pl.ds(p * piece, piece)
        return pltpu.make_async_copy(
            new_ref.at[j, :, at, :, :], out_ref.at[:, at, :, lanes(j)], done_sems.at[j, p]
        )

    for j in range(blocks):
        for p in range(pieces):
            load(j, p).start()
    rain_ref[...] = guess_ref[...]
    for j in range(blocks):
        row_ref[j] = respond(force_ref[j])
    rows = [guess_ref[j] / rate_of(code_ref[j]) for j in range(blocks)]
    marks = [jnp.where(code_ref[j] > 0.0, row, -2.0) for j, row in enumerate(rows)]
    wettest = [jnp.max(mark, axis=1, keepdims=True) for mark in marks]
    dry = [((w > -1.0) & (w < SMALL_RAIN)).astype(jnp.int32) for w in wettest]
    some_dry = jnp.max(functools.reduce(jnp.maximum, dry)) > 0

    def block(j, _):
        occupied = jnp.broadcast_to(code_ref[j], (8, LANES)) > 0.0
        fields = [Field(crm_levels) for _ in range(STEPS + 1)]
        for i in range(crm_levels + STEPS):
            if i < crm_levels:
                if i % piece == 0:
                    load(j, i // piece).wait()
                heat = [kept_ref[j, 0, i, pl.ds(k, 8, stride=count), :] for k in range(count)]
                moist = [kept_ref[j, 1, i, pl.ds(k, 8, stride=count), :] for k in range(count)]
                fields[0].rows.append([(h + h) + m for h, m in zip(heat, moist)])
            for t in range(1, STEPS + 1):
                z = i - t
                if 0 <= z < crm_levels:
                    fields[t].rows.append(fields[t - 1].five(z))
            if not 0 <= z < crm_levels:
                continue
            row = jnp.broadcast_to(row_ref[j, pl.ds(z, 1), :], (8, LANES))
            for k, total in enumerate(fields[STEPS].rows[z]):
                at = pl.ds(k, 8, stride=count)
                linear = (1.0 / 125.0) * total + row
                dry = (1.0 / LOG2E) * last_ref[j, z, k] + saturation(z, crm_levels)
                heat = (1.0 / 2.3) * (linear - dry)
                moist = dry + 0.3 * heat
                new_ref[j, 0, z, at, :] = jnp.where(occupied, heat, kept_ref[j, 0, z, at, :])
                new_ref[j, 1, z, at, :] = jnp.where(occupied, moist, kept_ref[j, 1, z, at, :])
            if z % piece == piece - 1:
                store(j, z // piece).start()
        return 0

    lax.fori_loop(0, blocks, block, 0)

    def again(j, _):
        rate = rate_of(code_ref[j])
        lowered = jnp.broadcast_to((1.15 * LOG2E) * rate, (8, LANES))
        push = (-0.65 * LOG2E) * force_ref[j]
        push_ref[0] = push - dried(crm_levels)
        push_ref[1] = push + bounds(crm_levels)

        def condense(y, acc):
            e = jnp.exp2(y)
            amount = jnp.where(e < 2.0**-8, e * (1.0 - 0.5 * e), jnp.log(1.0 + e))
            return y - lowered * amount, acc + amount

        def start(z, _):
            for k in range(count):
                at = pl.ds(k, 8, stride=count)
                field_ref[0, z, k] = LOG2E * (kept_ref[j, 1, z, at, :] - 0.3 * kept_ref[j, 0, z, at, :])
            return 0

        def step(source, target, which):
            def body(z, acc):
                push = jnp.broadcast_to(push_ref[which, pl.ds(z, 1), :], (8, LANES))
                at = (z, jnp.maximum(z - 1, 0), jnp.minimum(z + 1, crm_levels - 1))
                totals = five_points(*[[field_ref[source, y, k] for k in range(count)] for y in at])
                new = []
                for k in range(count):
                    field_ref[target, z, k], total = condense(0.2 * totals[k] + push, acc[k])
                    new.append(total)
                return tuple(new)
            return body

        acc = tuple(jnp.zeros((8, LANES), F32) for _ in range(count))
        lax.fori_loop(0, crm_levels, start, 0)
        for t in range(STEPS):
            acc = lax.fori_loop(0, crm_levels, step(t % 2, (t + 1) % 2, min(t, 1)), acc)
        mean = jnp.sum(add_up(list(acc)), axis=0, keepdims=True) * (1.0 / (crm_levels * width))
        rain_ref[j] = jnp.where(code_ref[j] > 0.0, rate * mean, 0.0)
        return 0

    @pl.when(some_dry)
    def _():
        lax.fori_loop(0, blocks, again, 0)

    for j in range(blocks):
        for p in range(pieces):
            store(j, p).wait()


def tendency_kernel(crm_levels, pos_ref, returned_ref, out_ref, new_ref, sems):
    levels = out_ref.shape[0] // NV
    rows = returned_ref.shape[0]
    columns = pos_ref.shape[1]
    place = (iota((2 * rows, columns), 0) == pos_ref[...]).astype(BF16)
    shape = (levels, 2 * HALF)
    lane, level = iota(shape, 1), iota(shape, 0)
    table = [
        jnp.where((lane >= at) & (lane < at + crm_levels), interp(lane - at, level, crm_levels, levels), 0.0)
        for at in (0, HALF)
    ]
    spread = dot_in_three(jnp.concatenate(table, axis=0), returned_ref[...], (1, 1))
    parts = both_halves(jnp.concatenate([spread[:levels], spread[levels:]], axis=1))
    answer = dot(parts, place, (1, 0))
    answer = answer[:levels] + answer[levels:]
    copies = []
    for k in range(NV):
        new_ref[k] = mixing(k) * answer
        copies.append(
            pltpu.make_async_copy(new_ref.at[k], out_ref.at[pl.ds(k * levels, levels), :], sems.at[k])
        )
        copies[k].start()
    for copy in copies:
        copy.wait()


def call(kernel, out, scratch=(), cost=(0, 0, 0), vmem=32, **specs):
    return pl.pallas_call(
        kernel, out_shape=out, scratch_shapes=list(scratch),
        cost_estimate=pl.CostEstimate(flops=int(cost[0]), bytes_accessed=int(cost[1]), transcendentals=int(cost[2])),
        compiler_params=pltpu.CompilerParams(vmem_limit_bytes=vmem * 2**20), **specs,
    )


def from_hbm(*arrays):
    return [pltpu.with_memory_space_constraint(x, pltpu.HBM) for x in arrays]


HBM = pl.BlockSpec(memory_space=pltpu.HBM)
VMEM = pl.BlockSpec(memory_space=pltpu.VMEM)


def before(peers, capacity, me, routes, branch, neighbours, gcm_state, own, crm_state):
    _, crm_levels, width, slots = crm_state.shape
    columns = routes.shape[0]
    blocks = slots // LANES
    cells = crm_levels * width * slots
    return call(
        functools.partial(before_kernel, peers, capacity),
        (
            pltpu.VMEM((1, columns), jnp.int32),
            pltpu.VMEM((slots // 2, LANES), F32),
            pltpu.VMEM((slots, 2 * columns), BF16),
            pltpu.VMEM((blocks, crm_levels, width // 8, 8, LANES), F32),
            pltpu.VMEM((blocks, 2, crm_levels, LANES), F32),
        ),
        [
            pltpu.VMEM((1, columns), jnp.int32),
            pltpu.VMEM((1, columns), jnp.int32),
            pltpu.VMEM((4, columns // 4), jnp.int32),
            pltpu.VMEM(gcm_state.shape[::-1], F32),
            pltpu.VMEM((blocks, 2, crm_levels, width, LANES), F32),
            pltpu.VMEM((2, crm_levels * 8, LANES), F32),
            pltpu.SemaphoreType.DMA((blocks + 4,)),
        ],
        (cells * 25 + 2e9, cells * 8 + 2e6, 0),
        in_specs=[pl.BlockSpec(memory_space=pltpu.SMEM)] + [HBM] * 4 + [VMEM, HBM],
        out_specs=[VMEM] * 5,
    )(
        me.reshape(1),
        *from_hbm(routes.T, branch.reshape(1, -1), neighbours.T, gcm_state.T),
        own,
        *from_hbm(crm_state),
    )


def cloud_steps(capacity, arrived, first, sums):
    blocks, crm_levels, count = first.shape[:3]
    cells = crm_levels * count * 8 * blocks * LANES
    return call(
        functools.partial(cloud_kernel, capacity),
        (
            pltpu.VMEM(first.shape, F32),
            pltpu.VMEM((blocks, crm_levels, LANES), F32),
            pltpu.VMEM((blocks, 1, LANES), F32),
            pltpu.VMEM((blocks, 1, LANES), F32),
            jax.ShapeDtypeStruct(arrived.shape, F32),
        ),
        [pltpu.VMEM(sums.shape, F32), pltpu.VMEM((blocks, crm_levels * 8, LANES), F32)],
        (cells * 30, cells * 8, cells * 6),
        in_specs=[VMEM] * 3,
        out_specs=[VMEM] * 5,
    )(arrived, first, sums)


def cloud_after(crm_state, last, force, code, rain):
    _, crm_levels, width, slots = crm_state.shape
    blocks = slots // LANES
    pieces = 1
    cells = crm_levels * width * slots
    return call(
        after_kernel,
        (jax.ShapeDtypeStruct(crm_state.shape, F32), jax.ShapeDtypeStruct((blocks, 1, LANES), F32)),
        [pltpu.VMEM((blocks, 2, crm_levels, width, LANES), F32)] * 2
        + [
            pltpu.VMEM((blocks, crm_levels, LANES), F32),
            pltpu.VMEM((2, crm_levels, LANES), F32),
            pltpu.VMEM((2,) + last.shape[1:], F32),
        ]
        + [pltpu.SemaphoreType.DMA((blocks, pieces))] * 2,
        (cells * 10, cells * 8, 0),
        in_specs=[HBM] + [VMEM] * 4,
        out_specs=[HBM, VMEM],
    )(*from_hbm(crm_state), last, force, code, rain)


def on_device(gcm_state, edge_part, neighbours, branch, routes, crm_state):
    peers = lax.axis_size(AXES)
    me = lax.axis_index(AXES)
    columns, features = gcm_state.shape
    _, crm_levels, _, slots = crm_state.shape
    capacity = slots // peers
    rows = slots // 2
    shape = jax.ShapeDtypeStruct

    own = call(edges_kernel, shape((crm_levels, columns), F32), cost=(1e7, 4e5, 0))(
        *from_hbm(edge_part)
    )
    other = lax.ppermute(own, AXES, [(i, (((i + 1) ^ 1) - 1) % peers) for i in range(peers)])
    pair = lax.ppermute(own, AXES, [(i, i ^ 1) for i in range(peers)])
    position, base, halo_map, first, sums = before(
        peers, capacity, me, routes, branch, neighbours, gcm_state, own, crm_state
    )
    outgoing = call(outgoing_kernel, shape((rows, LANES), F32), cost=(2e8, 1e6, 0))(base, halo_map, other, pair)
    arrived = lax.all_to_all(outgoing.reshape(peers, capacity // 2, LANES), AXES, 0, 0, tiled=True)
    last, force, code, rain, reply = cloud_steps(capacity, arrived.reshape(rows, LANES), first, sums)
    returned = lax.all_to_all(reply.reshape(peers, capacity // 2, LANES), AXES, 0, 0, tiled=True)
    updated, rain = cloud_after(crm_state, last, force, code, rain)
    levels = features // NV
    tendency = call(
        functools.partial(tendency_kernel, crm_levels),
        shape((features, columns), F32),
        [pltpu.VMEM((NV, levels, columns), F32), pltpu.SemaphoreType.DMA((NV,))],
        (1e8, 1e6, 0),
        in_specs=[VMEM] * 2,
        out_specs=HBM,
    )(position, returned.reshape(rows, LANES))
    return (tendency.T, updated, rain.reshape(1, slots))


def solution(mesh):
    in_specs = (
        P(AXES, None),
        P(AXES, None, None),
        P(AXES, None),
        P(AXES),
        P(AXES, None),
        P(None, None, None, AXES),
    )
    out_specs = (
        P(AXES, None),
        P(None, None, None, AXES),
        P(AXES, None),
    )
    return jax.shard_map(
        on_device, mesh=mesh, in_specs=in_specs, out_specs=out_specs, check_vma=False
    )
```

```python
import functools

import jax
import jax.numpy as jnp
import numpy as np
from jax import lax
from jax.experimental import pallas as pl
from jax.experimental.pallas import tpu as pltpu
from jax.sharding import PartitionSpec as P

NV = 8
STEPS = 3
AXES = ("elem", "sub")
LANES = 128
HALF = 64
LOG2E = 1.4426950408889634
F32 = jnp.float32
BF16 = jnp.bfloat16
SMALL_RAIN = 0.2


def mixing(k):
    return (0.8 + 0.05 * k) * (1.0 if k % 2 == 0 else -1.0) / float(np.sqrt(float(NV)))


def interp(z, level, crm_levels, levels):
    position = z.astype(F32) * ((levels - 1) / (crm_levels - 1))
    return jnp.maximum(0.0, 1.0 - jnp.abs(position - level.astype(F32)))


def dot(a, b, contract):
    return lax.dot_general(
        a, b, ((contract[0:1], contract[1:2]), ((), ())),
        preferred_element_type=F32,
    )


def split(x):
    high = x.astype(BF16)
    return high, (x - high.astype(F32)).astype(BF16)


def dot_in_three(a, b, contract):
    high, low = split(b)
    parts = both_halves(a)
    rows = a.shape[0]
    first = dot(parts, high, contract)
    return first[:rows] + first[rows:] + dot(parts[:rows], low, contract)


def both_halves(x):
    high = x.astype(BF16).astype(F32)
    return jnp.concatenate([high, x - high], axis=0).astype(BF16)


def slot_rows(onehot, fields):
    product = dot(onehot, both_halves(fields), (1, 1))
    product = product + pltpu.roll(product, HALF, 1)
    rows = product.shape[0] // 2
    return jnp.where(iota((rows, 2 * HALF), 1) < HALF, product[:rows], product[rows:])


def padded(fields):
    return jnp.concatenate([fields, jnp.zeros((HALF - fields.shape[0], fields.shape[1]), F32)], axis=0)


def iota(shape, dim):
    return lax.broadcasted_iota(jnp.int32, shape, dim)


def edges_kernel(edge_ref, out_ref):
    crm_levels = out_ref.shape[0]
    shape = (crm_levels, edge_ref.shape[2])
    levels = shape[1] // 2
    lane = iota(shape, 1)
    weight = jnp.where(
        lane < levels,
        mixing(0) * interp(iota(shape, 0), lane, crm_levels, levels),
        mixing(1) * interp(iota(shape, 0), lane - levels, crm_levels, levels),
    )
    out_ref[...] = dot_in_three(weight, edge_ref[...].reshape(-1, shape[1]), (1, 1))


def outgoing_kernel(base_ref, map_ref, other_ref, pair_ref, out_ref):
    window = jnp.concatenate([pair_ref[...], other_ref[...]], axis=1)
    out_ref[...] = base_ref[...] + 0.25 * slot_rows(map_ref[...], padded(window))


class Field:
    def __init__(self, total):
        self.total, self.rows, self.diagonals = total, [], []

    def five(self, z):
        while len(self.diagonals) < z + 2:
            at = len(self.diagonals)
            below, here = self.rows[max(at - 1, 0)], self.rows[min(at, self.total - 1)]
            right = here[1:] + [pltpu.roll(here[0], 7, 0)]
            self.diagonals.append([a + b for a, b in zip(below, right)])
        low, high = self.diagonals[z], self.diagonals[z + 1]
        high = [pltpu.roll(high[-1], 1, 0)] + high[:-1]
        return [row + (a + b) for row, a, b in zip(self.rows[z], low, high)]


def five_points(row, up, down):
    left = [pltpu.roll(row[-1], 1, 0)] + row[:-1]
    right = row[1:] + [pltpu.roll(row[0], 7, 0)]
    return [(a + b + c) + (d + e) for a, b, c, d, e in zip(row, left, right, up, down)]


def add_up(values):
    while len(values) > 1:
        values = [a + b for a, b in zip(values[::2], values[1::2])]
    return values[0]


def rows_of_sums(ref, crm_levels):
    return add_up([ref[pl.ds(s, crm_levels, stride=8), :] for s in range(8)])


def saturation(z, crm_levels):
    return 1.0 - z * (2.0 / (crm_levels - 1))


def levels_of(crm_levels):
    return iota((crm_levels, LANES), 0)


def shifted(x):
    return jnp.concatenate([x[:1], x[:-1]], axis=0) + jnp.concatenate([x[1:], x[-1:]], axis=0)


def route(peers, capacity, me_ref, routes_ref, branch_ref, neigh_ref, gcm_ref, own_ref,
          pos_ref, base_ref, halo_map_ref):
    columns = routes_ref.shape[1]
    elems = columns // 4
    crm_levels = own_ref.shape[0]
    slots = peers * capacity
    half = capacity // 2
    me = me_ref[0]
    destination = routes_ref[...]
    named = iota((peers, columns), 0) == destination
    earlier = (iota((columns, columns), 0) < iota((columns, columns), 1)).astype(BF16)
    before = dot(named.astype(BF16), earlier, (1, 0))
    rank = jnp.sum(jnp.where(named, before, 0.0), axis=0, keepdims=True).astype(jnp.int32)
    upper = (rank >= half).astype(jnp.int32)
    position = upper * (slots // 2) + destination * half + rank - upper * half
    pos_ref[...] = position
    place = (iota((slots, columns), 0) == position).astype(BF16)

    target = jnp.concatenate([neigh_ref[j : j + 1, :] for j in range(4)], axis=1)
    owner = target // columns
    edge = target - owner * columns
    block = jnp.where(owner == me, 0, jnp.where(owner == (me ^ 1), 1, 2))
    source = block * columns + edge
    window = iota((3 * columns, columns), 0)
    local = iota((1, columns), 1)
    local = 4 * (local % elems) + local // elems
    chosen = (window == source).astype(F32) + (window == local).astype(F32)
    column = iota((columns, columns), 0)
    row = iota((columns, columns), 1)
    first = (column % 4) * elems + column // 4
    second = ((column + 1) % 4) * elems + column // 4
    pair = ((row == first) | (row == second)).astype(BF16)
    mapped = dot(pair, chosen.astype(BF16), (1, 1)).astype(BF16)
    halo_map_ref[...] = dot(place, mapped[:, columns:], (1, 0)).astype(BF16)

    levels = gcm_ref.shape[0] // NV
    mixed = mixing(0) * gcm_ref[:levels, :]
    for k in range(1, NV):
        mixed += mixing(k) * gcm_ref[pl.ds(k * levels, levels), :]
    shape = (crm_levels, levels)
    force = dot_in_three(interp(iota(shape, 0), iota(shape, 1), crm_levels, levels), mixed, (1, 0))
    for part in split(own_ref[...]):
        force += 0.25 * dot(part, mapped[:, :columns], (1, 1))
    code = (branch_ref[...] + 1).astype(F32)
    base_ref[...] = slot_rows(place, padded(jnp.concatenate([force, code], axis=0)))


def before_kernel(peers, capacity, me_ref, routes_ref, branch_ref, neigh_ref, gcm_ref, own_ref, state_ref,
                  pos_ref, base_ref, halo_map_ref, first_ref, sums_ref,
                  near_routes_ref, near_branch_ref, near_neigh_ref, near_gcm_ref, kept_ref, part_ref, sems):
    blocks, _, crm_levels, width, _ = kept_ref.shape
    count = width // 8

    def copy(j):
        lanes = pl.ds(pl.multiple_of(j * LANES, LANES), LANES)
        return pltpu.make_async_copy(state_ref.at[:, :, :, lanes], kept_ref.at[j], sems.at[j])

    near = (near_routes_ref, near_branch_ref, near_neigh_ref, near_gcm_ref)
    loads = [
        pltpu.make_async_copy(far_ref, near_ref, sems.at[blocks + i])
        for i, (far_ref, near_ref) in enumerate(zip((routes_ref, branch_ref, neigh_ref, gcm_ref), near))
    ]
    for load in loads:
        load.start()
    for j in range(blocks):
        copy(j).start()
    for load in loads:
        load.wait()
    route(peers, capacity, me_ref, *near, own_ref, pos_ref, base_ref, halo_map_ref)

    def block(j, _):
        copy(j).wait()
        dry = Field(crm_levels)
        for i in range(crm_levels + 1):
            if i < crm_levels:
                heat = [kept_ref[j, 0, i, pl.ds(k, 8, stride=count), :] for k in range(count)]
                moist = [kept_ref[j, 1, i, pl.ds(k, 8, stride=count), :] for k in range(count)]
                dry.rows.append([m - 0.3 * h for h, m in zip(heat, moist)])
                part_ref[0, pl.ds(8 * i, 8), :] = add_up(dry.rows[i])
                part_ref[1, pl.ds(8 * i, 8), :] = add_up(heat)
            if i:
                for k, total in enumerate(dry.five(i - 1)):
                    first_ref[j, i - 1, k] = (0.2 * LOG2E) * total
        level = saturation(levels_of(crm_levels).astype(F32), crm_levels)
        dry_mean = rows_of_sums(part_ref.at[0], crm_levels) * (1.0 / width)
        start = dry_mean + rows_of_sums(part_ref.at[1], crm_levels) * (2.3 / width)
        q = start
        for _ in range(STEPS):
            q = 0.6 * q + 0.2 * shifted(q)
        sums_ref[j, 0] = LOG2E * (dry_mean - level)
        sums_ref[j, 1] = q - start
        return 0

    lax.fori_loop(0, blocks, block, 0)


def lane_maps(rows, capacity):
    half = capacity // 2
    row = iota((rows, LANES), 0)
    slot = iota((rows, LANES), 1)
    rank = slot % capacity
    low = (row == (slot // capacity) * half + rank) & (rank < half)
    high = (row == (slot // capacity) * half + rank - half) & (rank >= half)
    return low.astype(BF16), high.astype(BF16)


def bounds(crm_levels):
    level = levels_of(crm_levels)
    edge = (0.4 / (crm_levels - 1)) * LOG2E
    return jnp.where(level == 0, -edge, 0.0) + jnp.where(level == crm_levels - 1, edge, 0.0)


def dried(crm_levels):
    return LOG2E * saturation(levels_of(crm_levels).astype(F32), crm_levels)


def respond(force):
    q = jnp.zeros_like(force)
    for _ in range(STEPS):
        q = 0.6 * q + 0.2 * shifted(q) + 0.5 * force
    return q


def rate_of(code):
    return 0.15 + 0.25 * (code == 2.0).astype(F32)


def cloud_kernel(capacity, arrived_ref, first_ref, sums_ref, last_ref, force_ref, code_ref, rain_ref,
                 reply_ref, push_ref, part_ref):
    blocks, crm_levels, count = last_ref.shape[:3]
    width = count * 8
    part = arrived_ref.shape[0] // blocks
    low, high = lane_maps(part, capacity)
    maps = jnp.concatenate([low, high], axis=1)
    maps = jnp.concatenate([maps, maps], axis=0)
    for j in range(blocks):
        got = dot(both_halves(arrived_ref[pl.ds(j * part, part), :]), maps, (0, 0))
        got = got[:HALF, :LANES] + got[HALF:, LANES:]
        push = (-0.65 * LOG2E) * got[:crm_levels]
        push_ref[j, 0] = push - dried(crm_levels)
        push_ref[j, 1] = push + bounds(crm_levels)
        force_ref[j] = got[:crm_levels]
        code_ref[j] = got[crm_levels : crm_levels + 1]

    def block(j, _):
        lowered = jnp.broadcast_to((1.15 * LOG2E) * rate_of(code_ref[j]), (8, LANES))
        fields = [Field(crm_levels) for _ in range(STEPS)]
        for i in range(crm_levels + STEPS - 1):
            for t in range(STEPS):
                z = i - t
                if not 0 <= z < crm_levels:
                    continue
                push = jnp.broadcast_to(push_ref[j, min(t, 1), pl.ds(z, 1), :], (8, LANES))
                if t == 0:
                    values = [first_ref[j, z, k] + push for k in range(count)]
                else:
                    values = [0.2 * total + push for total in fields[t - 1].five(z)]
                values = [y - lowered * jnp.log(1.0 + jnp.exp2(y)) for y in values]
                fields[t].rows.append(values)
                if t == STEPS - 1:
                    for k in range(count):
                        last_ref[j, z, k] = values[k]
                    part_ref[j, pl.ds(8 * z, 8), :] = add_up(values)
        return 0

    lax.fori_loop(0, blocks, block, 0)
    turned = jnp.concatenate([low, high], axis=0)
    for j in range(blocks):
        dg = rows_of_sums(part_ref.at[j], crm_levels) * (1.0 / width) - sums_ref[j, 0]
        answer = (0.7 / 2.3) * (sums_ref[j, 1] + respond(force_ref[j])) - (3.0 / (2.3 * LOG2E)) * dg
        reply_ref[pl.ds(j * part, part), :] = slot_rows(turned, padded(answer))
        budget = (-0.65 * LOG2E * STEPS) * force_ref[j] - dg
        rain = jnp.sum(budget, axis=0, keepdims=True) * (1.0 / (1.15 * LOG2E * crm_levels))
        rain_ref[j] = jnp.where(code_ref[j] > 0.0, rain, 0.0)


def after_kernel(state_ref, last_ref, force_ref, code_ref, guess_ref, out_ref, rain_ref,
                 kept_ref, new_ref, row_ref, push_ref, field_ref, sems, done_sems):
    blocks, _, crm_levels, width, _ = kept_ref.shape
    count = width // 8
    pieces = sems.shape[1]
    piece = crm_levels // pieces

    def lanes(j):
        return pl.ds(pl.multiple_of(j * LANES, LANES), LANES)

    def load(j, p):
        at = pl.ds(p * piece, piece)
        return pltpu.make_async_copy(
            state_ref.at[:, at, :, lanes(j)], kept_ref.at[j, :, at, :, :], sems.at[j, p]
        )

    def store(j, p):
        at = pl.ds(p * piece, piece)
        return pltpu.make_async_copy(
            new_ref.at[j, :, at, :, :], out_ref.at[:, at, :, lanes(j)], done_sems.at[j, p]
        )

    for j in range(blocks):
        for p in range(pieces):
            load(j, p).start()
    rain_ref[...] = guess_ref[...]
    for j in range(blocks):
        row_ref[j] = respond(force_ref[j])
    rows = [guess_ref[j] / rate_of(code_ref[j]) for j in range(blocks)]
    marks = [jnp.where(code_ref[j] > 0.0, row, -2.0) for j, row in enumerate(rows)]
    wettest = [jnp.max(mark, axis=1, keepdims=True) for mark in marks]
    dry = [((w > -1.0) & (w < SMALL_RAIN)).astype(jnp.int32) for w in wettest]
    some_dry = jnp.max(functools.reduce(jnp.maximum, dry)) > 0

    def block(j, _):
        occupied = jnp.broadcast_to(code_ref[j], (8, LANES)) > 0.0
        fields = [Field(crm_levels) for _ in range(STEPS + 1)]
        for i in range(crm_levels + STEPS):
            if i < crm_levels:
                if i % piece == 0:
                    load(j, i // piece).wait()
                heat = [kept_ref[j, 0, i, pl.ds(k, 8, stride=count), :] for k in range(count)]
                moist = [kept_ref[j, 1, i, pl.ds(k, 8, stride=count), :] for k in range(count)]
                fields[0].rows.append([(h + h) + m for h, m in zip(heat, moist)])
            for t in range(1, STEPS + 1):
                z = i - t
                if 0 <= z < crm_levels:
                    fields[t].rows.append(fields[t - 1].five(z))
            if not 0 <= z < crm_levels:
                continue
            row = jnp.broadcast_to(row_ref[j, pl.ds(z, 1), :], (8, LANES))
            for k, total in enumerate(fields[STEPS].rows[z]):
                at = pl.ds(k, 8, stride=count)
                linear = (1.0 / 125.0) * total + row
                dry = (1.0 / LOG2E) * last_ref[j, z, k] + saturation(z, crm_levels)
                heat = (1.0 / 2.3) * (linear - dry)
                moist = dry + 0.3 * heat
                new_ref[j, 0, z, at, :] = jnp.where(occupied, heat, kept_ref[j, 0, z, at, :])
                new_ref[j, 1, z, at, :] = jnp.where(occupied, moist, kept_ref[j, 1, z, at, :])
            if z % piece == piece - 1:
                store(j, z // piece).start()
        return 0

    lax.fori_loop(0, blocks, block, 0)

    def again(j, _):
        rate = rate_of(code_ref[j])
        lowered = jnp.broadcast_to((1.15 * LOG2E) * rate, (8, LANES))
        push = (-0.65 * LOG2E) * force_ref[j]
        push_ref[0] = push - dried(crm_levels)
        push_ref[1] = push + bounds(crm_levels)

        def condense(y, acc):
            e = jnp.exp2(y)
            amount = jnp.where(e < 2.0**-8, e * (1.0 - 0.5 * e), jnp.log(1.0 + e))
            return y - lowered * amount, acc + amount

        def start(z, _):
            for k in range(count):
                at = pl.ds(k, 8, stride=count)
                field_ref[0, z, k] = LOG2E * (kept_ref[j, 1, z, at, :] - 0.3 * kept_ref[j, 0, z, at, :])
            return 0

        def step(source, target, which):
            def body(z, acc):
                push = jnp.broadcast_to(push_ref[which, pl.ds(z, 1), :], (8, LANES))
                at = (z, jnp.maximum(z - 1, 0), jnp.minimum(z + 1, crm_levels - 1))
                totals = five_points(*[[field_ref[source, y, k] for k in range(count)] for y in at])
                new = []
                for k in range(count):
                    field_ref[target, z, k], total = condense(0.2 * totals[k] + push, acc[k])
                    new.append(total)
                return tuple(new)
            return body

        acc = tuple(jnp.zeros((8, LANES), F32) for _ in range(count))
        lax.fori_loop(0, crm_levels, start, 0)
        for t in range(STEPS):
            acc = lax.fori_loop(0, crm_levels, step(t % 2, (t + 1) % 2, min(t, 1)), acc)
        mean = jnp.sum(add_up(list(acc)), axis=0, keepdims=True) * (1.0 / (crm_levels * width))
        rain_ref[j] = jnp.where(code_ref[j] > 0.0, rate * mean, 0.0)
        return 0

    @pl.when(some_dry)
    def _():
        lax.fori_loop(0, blocks, again, 0)

    for j in range(blocks):
        for p in range(pieces):
            store(j, p).wait()


def tendency_kernel(crm_levels, pos_ref, returned_ref, out_ref, new_ref, sems):
    levels = out_ref.shape[0] // NV
    rows = returned_ref.shape[0]
    columns = pos_ref.shape[1]
    place = (iota((2 * rows, columns), 0) == pos_ref[...]).astype(BF16)
    shape = (levels, 2 * HALF)
    lane, level = iota(shape, 1), iota(shape, 0)
    table = [
        jnp.where((lane >= at) & (lane < at + crm_levels), interp(lane - at, level, crm_levels, levels), 0.0)
        for at in (0, HALF)
    ]
    spread = dot_in_three(jnp.concatenate(table, axis=0), returned_ref[...], (1, 1))
    parts = both_halves(jnp.concatenate([spread[:levels], spread[levels:]], axis=1))
    answer = dot(parts, place, (1, 0))
    answer = answer[:levels] + answer[levels:]
    copies = []
    for k in range(NV):
        new_ref[k] = mixing(k) * answer
        copies.append(
            pltpu.make_async_copy(new_ref.at[k], out_ref.at[pl.ds(k * levels, levels), :], sems.at[k])
        )
        copies[k].start()
    for copy in copies:
        copy.wait()


def call(kernel, out, scratch=(), cost=(0, 0, 0), vmem=32, **specs):
    return pl.pallas_call(
        kernel, out_shape=out, scratch_shapes=list(scratch),
        cost_estimate=pl.CostEstimate(flops=int(cost[0]), bytes_accessed=int(cost[1]), transcendentals=int(cost[2])),
        compiler_params=pltpu.CompilerParams(vmem_limit_bytes=vmem * 2**20), **specs,
    )


def from_hbm(*arrays):
    return [pltpu.with_memory_space_constraint(x, pltpu.HBM) for x in arrays]


HBM = pl.BlockSpec(memory_space=pltpu.HBM)
VMEM = pl.BlockSpec(memory_space=pltpu.VMEM)


def before(peers, capacity, me, routes, branch, neighbours, gcm_state, own, crm_state):
    _, crm_levels, width, slots = crm_state.shape
    columns = routes.shape[0]
    blocks = slots // LANES
    cells = crm_levels * width * slots
    return call(
        functools.partial(before_kernel, peers, capacity),
        (
            pltpu.VMEM((1, columns), jnp.int32),
            pltpu.VMEM((slots // 2, LANES), F32),
            pltpu.VMEM((slots, 2 * columns), BF16),
            pltpu.VMEM((blocks, crm_levels, width // 8, 8, LANES), F32),
            pltpu.VMEM((blocks, 2, crm_levels, LANES), F32),
        ),
        [
            pltpu.VMEM((1, columns), jnp.int32),
            pltpu.VMEM((1, columns), jnp.int32),
            pltpu.VMEM((4, columns // 4), jnp.int32),
            pltpu.VMEM(gcm_state.shape[::-1], F32),
            pltpu.VMEM((blocks, 2, crm_levels, width, LANES), F32),
            pltpu.VMEM((2, crm_levels * 8, LANES), F32),
            pltpu.SemaphoreType.DMA((blocks + 4,)),
        ],
        (cells * 25 + 2e9, cells * 8 + 2e6, 0),
        in_specs=[pl.BlockSpec(memory_space=pltpu.SMEM)] + [HBM] * 4 + [VMEM, HBM],
        out_specs=[VMEM] * 5,
    )(
        me.reshape(1),
        *from_hbm(routes.T, branch.reshape(1, -1), neighbours.T, gcm_state.T),
        own,
        *from_hbm(crm_state),
    )


def cloud_steps(capacity, arrived, first, sums):
    blocks, crm_levels, count = first.shape[:3]
    cells = crm_levels * count * 8 * blocks * LANES
    return call(
        functools.partial(cloud_kernel, capacity),
        (
            pltpu.VMEM(first.shape, F32),
            pltpu.VMEM((blocks, crm_levels, LANES), F32),
            pltpu.VMEM((blocks, 1, LANES), F32),
            pltpu.VMEM((blocks, 1, LANES), F32),
            jax.ShapeDtypeStruct(arrived.shape, F32),
        ),
        [pltpu.VMEM(sums.shape, F32), pltpu.VMEM((blocks, crm_levels * 8, LANES), F32)],
        (cells * 30, cells * 8, cells * 6),
        in_specs=[VMEM] * 3,
        out_specs=[VMEM] * 5,
    )(arrived, first, sums)


def cloud_after(crm_state, last, force, code, rain):
    _, crm_levels, width, slots = crm_state.shape
    blocks = slots // LANES
    pieces = 1
    cells = crm_levels * width * slots
    return call(
        after_kernel,
        (jax.ShapeDtypeStruct(crm_state.shape, F32), jax.ShapeDtypeStruct((blocks, 1, LANES), F32)),
        [pltpu.VMEM((blocks, 2, crm_levels, width, LANES), F32)] * 2
        + [
            pltpu.VMEM((blocks, crm_levels, LANES), F32),
            pltpu.VMEM((2, crm_levels, LANES), F32),
            pltpu.VMEM((2,) + last.shape[1:], F32),
        ]
        + [pltpu.SemaphoreType.DMA((blocks, pieces))] * 2,
        (cells * 10, cells * 8, 0),
        in_specs=[HBM] + [VMEM] * 4,
        out_specs=[HBM, VMEM],
    )(*from_hbm(crm_state), last, force, code, rain)


def on_device(gcm_state, edge_part, neighbours, branch, routes, crm_state):
    peers = lax.axis_size(AXES)
    me = lax.axis_index(AXES)
    columns, features = gcm_state.shape
    _, crm_levels, _, slots = crm_state.shape
    capacity = slots // peers
    rows = slots // 2
    shape = jax.ShapeDtypeStruct

    own = call(edges_kernel, shape((crm_levels, columns), F32), cost=(1e7, 4e5, 0))(
        *from_hbm(edge_part)
    )
    other = lax.ppermute(own, AXES, [(i, (((i + 1) ^ 1) - 1) % peers) for i in range(peers)])
    pair = lax.ppermute(own, AXES, [(i, i ^ 1) for i in range(peers)])
    position, base, halo_map, first, sums = before(
        peers, capacity, me, routes, branch, neighbours, gcm_state, own, crm_state
    )
    outgoing = call(outgoing_kernel, shape((rows, LANES), F32), cost=(2e8, 1e6, 0))(base, halo_map, other, pair)
    arrived = lax.all_to_all(outgoing.reshape(peers, capacity // 2, LANES), AXES, 0, 0, tiled=True)
    last, force, code, rain, reply = cloud_steps(capacity, arrived.reshape(rows, LANES), first, sums)
    returned = lax.all_to_all(reply.reshape(peers, capacity // 2, LANES), AXES, 0, 0, tiled=True)
    updated, rain = cloud_after(crm_state, last, force, code, rain)
    levels = features // NV
    tendency = call(
        functools.partial(tendency_kernel, crm_levels),
        shape((features, columns), F32),
        [pltpu.VMEM((NV, levels, columns), F32), pltpu.SemaphoreType.DMA((NV,))],
        (1e8, 1e6, 0),
        in_specs=[VMEM] * 2,
        out_specs=HBM,
    )(position, returned.reshape(rows, LANES))
    return (tendency.T, updated, rain.reshape(1, slots))


def solution(mesh):
    in_specs = (
        P(AXES, None),
        P(AXES, None, None),
        P(AXES, None),
        P(AXES),
        P(AXES, None),
        P(None, None, None, AXES),
    )
    out_specs = (
        P(AXES, None),
        P(None, None, None, AXES),
        P(AXES, None),
    )
    return jax.shard_map(
        on_device, mesh=mesh, in_specs=in_specs, out_specs=out_specs, check_vma=False
    )
```

```python
import functools

import jax
import jax.numpy as jnp
import numpy as np
from jax import lax
from jax.experimental import pallas as pl
from jax.experimental.pallas import tpu as pltpu
from jax.sharding import PartitionSpec as P

NV = 8
STEPS = 3
AXES = ("elem", "sub")
LANES = 128
HALF = 64
LOG2E = 1.4426950408889634
F32 = jnp.float32
BF16 = jnp.bfloat16
SMALL_RAIN = 0.2


def mixing(k):
    return (0.8 + 0.05 * k) * (1.0 if k % 2 == 0 else -1.0) / float(np.sqrt(float(NV)))


def interp(z, level, crm_levels, levels):
    position = z.astype(F32) * ((levels - 1) / (crm_levels - 1))
    return jnp.maximum(0.0, 1.0 - jnp.abs(position - level.astype(F32)))


def dot(a, b, contract):
    return lax.dot_general(
        a, b, ((contract[0:1], contract[1:2]), ((), ())),
        preferred_element_type=F32,
    )


def split(x):
    high = x.astype(BF16)
    return high, (x - high.astype(F32)).astype(BF16)


def dot_in_three(a, b, contract):
    high, low = split(b)
    parts = both_halves(a)
    rows = a.shape[0]
    first = dot(parts, high, contract)
    return first[:rows] + first[rows:] + dot(parts[:rows], low, contract)


def both_halves(x):
    high = x.astype(BF16).astype(F32)
    return jnp.concatenate([high, x - high], axis=0).astype(BF16)


def slot_rows(onehot, fields):
    product = dot(onehot, both_halves(fields), (1, 1))
    product = product + pltpu.roll(product, HALF, 1)
    rows = product.shape[0] // 2
    return jnp.where(iota((rows, 2 * HALF), 1) < HALF, product[:rows], product[rows:])


def padded(fields):
    return jnp.concatenate([fields, jnp.zeros((HALF - fields.shape[0], fields.shape[1]), F32)], axis=0)


def iota(shape, dim):
    return lax.broadcasted_iota(jnp.int32, shape, dim)


def edges_kernel(edge_ref, out_ref):
    crm_levels = out_ref.shape[0]
    shape = (crm_levels, edge_ref.shape[2])
    levels = shape[1] // 2
    lane = iota(shape, 1)
    weight = jnp.where(
        lane < levels,
        mixing(0) * interp(iota(shape, 0), lane, crm_levels, levels),
        mixing(1) * interp(iota(shape, 0), lane - levels, crm_levels, levels),
    )
    out_ref[...] = dot_in_three(weight, edge_ref[...].reshape(-1, shape[1]), (1, 1))


def outgoing_kernel(base_ref, map_ref, other_ref, pair_ref, out_ref):
    window = jnp.concatenate([pair_ref[...], other_ref[...]], axis=1)
    out_ref[...] = base_ref[...] + 0.25 * slot_rows(map_ref[...], padded(window))


class Field:
    def __init__(self, total):
        self.total, self.rows, self.diagonals = total, [], []

    def five(self, z):
        while len(self.diagonals) < z + 2:
            at = len(self.diagonals)
            below, here = self.rows[max(at - 1, 0)], self.rows[min(at, self.total - 1)]
            right = here[1:] + [pltpu.roll(here[0], 7, 0)]
            self.diagonals.append([a + b for a, b in zip(below, right)])
        low, high = self.diagonals[z], self.diagonals[z + 1]
        high = [pltpu.roll(high[-1], 1, 0)] + high[:-1]
        return [row + (a + b) for row, a, b in zip(self.rows[z], low, high)]


def five_points(row, up, down):
    left = [pltpu.roll(row[-1], 1, 0)] + row[:-1]
    right = row[1:] + [pltpu.roll(row[0], 7, 0)]
    return [(a + b + c) + (d + e) for a, b, c, d, e in zip(row, left, right, up, down)]


def add_up(values):
    while len(values) > 1:
        values = [a + b for a, b in zip(values[::2], values[1::2])]
    return values[0]


def rows_of_sums(ref, crm_levels):
    return add_up([ref[pl.ds(s, crm_levels, stride=8), :] for s in range(8)])


def saturation(z, crm_levels):
    return 1.0 - z * (2.0 / (crm_levels - 1))


def levels_of(crm_levels):
    return iota((crm_levels, LANES), 0)


def shifted(x):
    return jnp.concatenate([x[:1], x[:-1]], axis=0) + jnp.concatenate([x[1:], x[-1:]], axis=0)


def route(peers, capacity, me_ref, routes_ref, branch_ref, neigh_ref, gcm_ref, own_ref,
          pos_ref, base_ref, halo_map_ref):
    columns = routes_ref.shape[1]
    elems = columns // 4
    crm_levels = own_ref.shape[0]
    slots = peers * capacity
    half = capacity // 2
    me = me_ref[0]
    destination = routes_ref[...]
    named = iota((peers, columns), 0) == destination
    earlier = (iota((columns, columns), 0) < iota((columns, columns), 1)).astype(BF16)
    before = dot(named.astype(BF16), earlier, (1, 0))
    rank = jnp.sum(jnp.where(named, before, 0.0), axis=0, keepdims=True).astype(jnp.int32)
    upper = (rank >= half).astype(jnp.int32)
    position = upper * (slots // 2) + destination * half + rank - upper * half
    pos_ref[...] = position
    place = (iota((slots, columns), 0) == position).astype(BF16)

    target = jnp.concatenate([neigh_ref[j : j + 1, :] for j in range(4)], axis=1)
    owner = target // columns
    edge = target - owner * columns
    block = jnp.where(owner == me, 0, jnp.where(owner == (me ^ 1), 1, 2))
    source = block * columns + edge
    window = iota((3 * columns, columns), 0)
    local = iota((1, columns), 1)
    local = 4 * (local % elems) + local // elems
    chosen = (window == source).astype(F32) + (window == local).astype(F32)
    column = iota((columns, columns), 0)
    row = iota((columns, columns), 1)
    first = (column % 4) * elems + column // 4
    second = ((column + 1) % 4) * elems + column // 4
    pair = ((row == first) | (row == second)).astype(BF16)
    mapped = dot(pair, chosen.astype(BF16), (1, 1)).astype(BF16)
    halo_map_ref[...] = dot(place, mapped[:, columns:], (1, 0)).astype(BF16)

    levels = gcm_ref.shape[0] // NV
    mixed = mixing(0) * gcm_ref[:levels, :]
    for k in range(1, NV):
        mixed += mixing(k) * gcm_ref[pl.ds(k * levels, levels), :]
    shape = (crm_levels, levels)
    force = dot_in_three(interp(iota(shape, 0), iota(shape, 1), crm_levels, levels), mixed, (1, 0))
    for part in split(own_ref[...]):
        force += 0.25 * dot(part, mapped[:, :columns], (1, 1))
    code = (branch_ref[...] + 1).astype(F32)
    base_ref[...] = slot_rows(place, padded(jnp.concatenate([force, code], axis=0)))


def before_kernel(peers, capacity, me_ref, routes_ref, branch_ref, neigh_ref, gcm_ref, own_ref, state_ref,
                  pos_ref, base_ref, halo_map_ref, first_ref, grown_ref, sums_ref,
                  near_routes_ref, near_branch_ref, near_neigh_ref, near_gcm_ref, kept_ref, part_ref, sems):
    blocks, _, crm_levels, width, _ = kept_ref.shape
    count = width // 8

    def copy(j):
        lanes = pl.ds(pl.multiple_of(j * LANES, LANES), LANES)
        return pltpu.make_async_copy(state_ref.at[:, :, :, lanes], kept_ref.at[j], sems.at[j])

    near = (near_routes_ref, near_branch_ref, near_neigh_ref, near_gcm_ref)
    loads = [
        pltpu.make_async_copy(far_ref, near_ref, sems.at[blocks + i])
        for i, (far_ref, near_ref) in enumerate(zip((routes_ref, branch_ref, neigh_ref, gcm_ref), near))
    ]
    for load in loads:
        load.start()
    for j in range(blocks):
        copy(j).start()
    for load in loads:
        load.wait()
    route(peers, capacity, me_ref, *near, own_ref, pos_ref, base_ref, halo_map_ref)

    def block(j, _):
        copy(j).wait()
        dry = Field(crm_levels)
        for i in range(crm_levels + 1):
            if i < crm_levels:
                heat = [kept_ref[j, 0, i, pl.ds(k, 8, stride=count), :] for k in range(count)]
                moist = [kept_ref[j, 1, i, pl.ds(k, 8, stride=count), :] for k in range(count)]
                dry.rows.append([m - 0.3 * h for h, m in zip(heat, moist)])
                part_ref[0, pl.ds(8 * i, 8), :] = add_up(dry.rows[i])
                part_ref[1, pl.ds(8 * i, 8), :] = add_up(heat)
            if i:
                for k, total in enumerate(dry.five(i - 1)):
                    first_ref[j, i - 1, k] = (0.2 * LOG2E) * total
                    grown_ref[j, i - 1, k] = jnp.exp2((0.2 * LOG2E) * total)
        level = saturation(levels_of(crm_levels).astype(F32), crm_levels)
        dry_mean = rows_of_sums(part_ref.at[0], crm_levels) * (1.0 / width)
        start = dry_mean + rows_of_sums(part_ref.at[1], crm_levels) * (2.3 / width)
        q = start
        for _ in range(STEPS):
            q = 0.6 * q + 0.2 * shifted(q)
        sums_ref[j, 0] = LOG2E * (dry_mean - level)
        sums_ref[j, 1] = q - start
        return 0

    lax.fori_loop(0, blocks, block, 0)


def lane_maps(rows, capacity):
    half = capacity // 2
    row = iota((rows, LANES), 0)
    slot = iota((rows, LANES), 1)
    rank = slot % capacity
    low = (row == (slot // capacity) * half + rank) & (rank < half)
    high = (row == (slot // capacity) * half + rank - half) & (rank >= half)
    return low.astype(BF16), high.astype(BF16)


def bounds(crm_levels):
    level = levels_of(crm_levels)
    edge = (0.4 / (crm_levels - 1)) * LOG2E
    return jnp.where(level == 0, -edge, 0.0) + jnp.where(level == crm_levels - 1, edge, 0.0)


def dried(crm_levels):
    return LOG2E * saturation(levels_of(crm_levels).astype(F32), crm_levels)


def respond(force):
    q = jnp.zeros_like(force)
    for _ in range(STEPS):
        q = 0.6 * q + 0.2 * shifted(q) + 0.5 * force
    return q


def rate_of(code):
    return 0.15 + 0.25 * (code == 2.0).astype(F32)


def cloud_kernel(capacity, arrived_ref, first_ref, grown_ref, sums_ref, last_ref, force_ref, code_ref, rain_ref,
                 reply_ref, push_ref, part_ref):
    blocks, crm_levels, count = last_ref.shape[:3]
    width = count * 8
    part = arrived_ref.shape[0] // blocks
    low, high = lane_maps(part, capacity)
    maps = jnp.concatenate([low, high], axis=1)
    maps = jnp.concatenate([maps, maps], axis=0)
    for j in range(blocks):
        got = dot(both_halves(arrived_ref[pl.ds(j * part, part), :]), maps, (0, 0))
        got = got[:HALF, :LANES] + got[HALF:, LANES:]
        push = (-0.65 * LOG2E) * got[:crm_levels]
        push_ref[j, 0] = push - dried(crm_levels)
        push_ref[j, 1] = push + bounds(crm_levels)
        force_ref[j] = got[:crm_levels]
        code_ref[j] = got[crm_levels : crm_levels + 1]

    def block(j, _):
        lowered = jnp.broadcast_to((1.15 * LOG2E) * rate_of(code_ref[j]), (8, LANES))
        fields = [Field(crm_levels) for _ in range(STEPS)]
        for i in range(crm_levels + 2 * (STEPS - 1)):
            for t in range(STEPS):
                z = i - 2 * t
                if not 0 <= z < crm_levels:
                    continue
                push = jnp.broadcast_to(push_ref[j, min(t, 1), pl.ds(z, 1), :], (8, LANES))
                if t == 0:
                    values = [first_ref[j, z, k] + push for k in range(count)]
                else:
                    values = [0.2 * total + push for total in fields[t - 1].five(z)]
                if t == 0:
                    factor = jnp.exp2(push)
                    powers = [factor * grown_ref[j, z, k] for k in range(count)]
                else:
                    powers = [jnp.exp2(y) for y in values]
                values = [y - lowered * jnp.log(1.0 + e) for y, e in zip(values, powers)]
                fields[t].rows.append(values)
                if t == STEPS - 1:
                    for k in range(count):
                        last_ref[j, z, k] = values[k]
                    part_ref[j, pl.ds(8 * z, 8), :] = add_up(values)
        return 0

    lax.fori_loop(0, blocks, block, 0)
    turned = jnp.concatenate([low, high], axis=0)
    for j in range(blocks):
        dg = rows_of_sums(part_ref.at[j], crm_levels) * (1.0 / width) - sums_ref[j, 0]
        answer = (0.7 / 2.3) * (sums_ref[j, 1] + respond(force_ref[j])) - (3.0 / (2.3 * LOG2E)) * dg
        reply_ref[pl.ds(j * part, part), :] = slot_rows(turned, padded(answer))
        budget = (-0.65 * LOG2E * STEPS) * force_ref[j] - dg
        rain = jnp.sum(budget, axis=0, keepdims=True) * (1.0 / (1.15 * LOG2E * crm_levels))
        rain_ref[j] = jnp.where(code_ref[j] > 0.0, rain, 0.0)


def after_kernel(state_ref, last_ref, force_ref, code_ref, guess_ref, out_ref, rain_ref,
                 kept_ref, new_ref, row_ref, push_ref, field_ref, sems, done_sems):
    blocks, _, crm_levels, width, _ = kept_ref.shape
    count = width // 8
    pieces = sems.shape[1]
    piece = crm_levels // pieces

    def lanes(j):
        return pl.ds(pl.multiple_of(j * LANES, LANES), LANES)

    def load(j, p):
        at = pl.ds(p * piece, piece)
        return pltpu.make_async_copy(
            state_ref.at[:, at, :, lanes(j)], kept_ref.at[j, :, at, :, :], sems.at[j, p]
        )

    def store(j, p):
        at = pl.ds(p * piece, piece)
        return pltpu.make_async_copy(
            new_ref.at[j, :, at, :, :], out_ref.at[:, at, :, lanes(j)], done_sems.at[j, p]
        )

    for j in range(blocks):
        for p in range(pieces):
            load(j, p).start()
    rain_ref[...] = guess_ref[...]
    for j in range(blocks):
        row_ref[j] = respond(force_ref[j])
    rows = [guess_ref[j] / rate_of(code_ref[j]) for j in range(blocks)]
    marks = [jnp.where(code_ref[j] > 0.0, row, -2.0) for j, row in enumerate(rows)]
    wettest = [jnp.max(mark, axis=1, keepdims=True) for mark in marks]
    dry = [((w > -1.0) & (w < SMALL_RAIN)).astype(jnp.int32) for w in wettest]
    some_dry = jnp.max(functools.reduce(jnp.maximum, dry)) > 0

    def block(j, _):
        occupied = jnp.broadcast_to(code_ref[j], (8, LANES)) > 0.0
        fields = [Field(crm_levels) for _ in range(STEPS + 1)]
        for i in range(crm_levels + STEPS):
            if i < crm_levels:
                if i % piece == 0:
                    load(j, i // piece).wait()
                heat = [kept_ref[j, 0, i, pl.ds(k, 8, stride=count), :] for k in range(count)]
                moist = [kept_ref[j, 1, i, pl.ds(k, 8, stride=count), :] for k in range(count)]
                fields[0].rows.append([(h + h) + m for h, m in zip(heat, moist)])
            for t in range(1, STEPS + 1):
                z = i - t
                if 0 <= z < crm_levels:
                    fields[t].rows.append(fields[t - 1].five(z))
            if not 0 <= z < crm_levels:
                continue
            row = jnp.broadcast_to(row_ref[j, pl.ds(z, 1), :], (8, LANES))
            for k, total in enumerate(fields[STEPS].rows[z]):
                at = pl.ds(k, 8, stride=count)
                linear = (1.0 / 125.0) * total + row
                dry = (1.0 / LOG2E) * last_ref[j, z, k] + saturation(z, crm_levels)
                heat = (1.0 / 2.3) * (linear - dry)
                moist = dry + 0.3 * heat
                new_ref[j, 0, z, at, :] = jnp.where(occupied, heat, kept_ref[j, 0, z, at, :])
                new_ref[j, 1, z, at, :] = jnp.where(occupied, moist, kept_ref[j, 1, z, at, :])
            if z % piece == piece - 1:
                store(j, z // piece).start()
        return 0

    lax.fori_loop(0, blocks, block, 0)

    def again(j, _):
        rate = rate_of(code_ref[j])
        lowered = jnp.broadcast_to((1.15 * LOG2E) * rate, (8, LANES))
        push = (-0.65 * LOG2E) * force_ref[j]
        push_ref[0] = push - dried(crm_levels)
        push_ref[1] = push + bounds(crm_levels)

        def condense(y, acc):
            e = jnp.exp2(y)
            amount = jnp.where(e < 2.0**-8, e * (1.0 - 0.5 * e), jnp.log(1.0 + e))
            return y - lowered * amount, acc + amount

        def start(z, _):
            for k in range(count):
                at = pl.ds(k, 8, stride=count)
                field_ref[0, z, k] = LOG2E * (kept_ref[j, 1, z, at, :] - 0.3 * kept_ref[j, 0, z, at, :])
            return 0

        def step(source, target, which):
            def body(z, acc):
                push = jnp.broadcast_to(push_ref[which, pl.ds(z, 1), :], (8, LANES))
                at = (z, jnp.maximum(z - 1, 0), jnp.minimum(z + 1, crm_levels - 1))
                totals = five_points(*[[field_ref[source, y, k] for k in range(count)] for y in at])
                new = []
                for k in range(count):
                    field_ref[target, z, k], total = condense(0.2 * totals[k] + push, acc[k])
                    new.append(total)
                return tuple(new)
            return body

        acc = tuple(jnp.zeros((8, LANES), F32) for _ in range(count))
        lax.fori_loop(0, crm_levels, start, 0)
        for t in range(STEPS):
            acc = lax.fori_loop(0, crm_levels, step(t % 2, (t + 1) % 2, min(t, 1)), acc)
        mean = jnp.sum(add_up(list(acc)), axis=0, keepdims=True) * (1.0 / (crm_levels * width))
        rain_ref[j] = jnp.where(code_ref[j] > 0.0, rate * mean, 0.0)
        return 0

    @pl.when(some_dry)
    def _():
        lax.fori_loop(0, blocks, again, 0)

    for j in range(blocks):
        for p in range(pieces):
            store(j, p).wait()


def tendency_kernel(crm_levels, pos_ref, returned_ref, out_ref, new_ref, sems):
    levels = out_ref.shape[0] // NV
    rows = returned_ref.shape[0]
    columns = pos_ref.shape[1]
    place = (iota((2 * rows, columns), 0) == pos_ref[...]).astype(BF16)
    shape = (levels, 2 * HALF)
    lane, level = iota(shape, 1), iota(shape, 0)
    table = [
        jnp.where((lane >= at) & (lane < at + crm_levels), interp(lane - at, level, crm_levels, levels), 0.0)
        for at in (0, HALF)
    ]
    spread = dot_in_three(jnp.concatenate(table, axis=0), returned_ref[...], (1, 1))
    parts = both_halves(jnp.concatenate([spread[:levels], spread[levels:]], axis=1))
    answer = dot(parts, place, (1, 0))
    answer = answer[:levels] + answer[levels:]
    copies = []
    for k in range(NV):
        new_ref[k] = mixing(k) * answer
        copies.append(
            pltpu.make_async_copy(new_ref.at[k], out_ref.at[pl.ds(k * levels, levels), :], sems.at[k])
        )
        copies[k].start()
    for copy in copies:
        copy.wait()


def call(kernel, out, scratch=(), cost=(0, 0, 0), vmem=32, **specs):
    return pl.pallas_call(
        kernel, out_shape=out, scratch_shapes=list(scratch),
        cost_estimate=pl.CostEstimate(flops=int(cost[0]), bytes_accessed=int(cost[1]), transcendentals=int(cost[2])),
        compiler_params=pltpu.CompilerParams(vmem_limit_bytes=vmem * 2**20), **specs,
    )


def from_hbm(*arrays):
    return [pltpu.with_memory_space_constraint(x, pltpu.HBM) for x in arrays]


HBM = pl.BlockSpec(memory_space=pltpu.HBM)
VMEM = pl.BlockSpec(memory_space=pltpu.VMEM)


def before(peers, capacity, me, routes, branch, neighbours, gcm_state, own, crm_state):
    _, crm_levels, width, slots = crm_state.shape
    columns = routes.shape[0]
    blocks = slots // LANES
    cells = crm_levels * width * slots
    return call(
        functools.partial(before_kernel, peers, capacity),
        (
            pltpu.VMEM((1, columns), jnp.int32),
            pltpu.VMEM((slots // 2, LANES), F32),
            pltpu.VMEM((slots, 2 * columns), BF16),
            pltpu.VMEM((blocks, crm_levels, width // 8, 8, LANES), F32),
            pltpu.VMEM((blocks, crm_levels, width // 8, 8, LANES), F32),
            pltpu.VMEM((blocks, 2, crm_levels, LANES), F32),
        ),
        [
            pltpu.VMEM((1, columns), jnp.int32),
            pltpu.VMEM((1, columns), jnp.int32),
            pltpu.VMEM((4, columns // 4), jnp.int32),
            pltpu.VMEM(gcm_state.shape[::-1], F32),
            pltpu.VMEM((blocks, 2, crm_levels, width, LANES), F32),
            pltpu.VMEM((2, crm_levels * 8, LANES), F32),
            pltpu.SemaphoreType.DMA((blocks + 4,)),
        ],
        (cells * 25 + 2e9, cells * 8 + 2e6, 0),
        in_specs=[pl.BlockSpec(memory_space=pltpu.SMEM)] + [HBM] * 4 + [VMEM, HBM],
        out_specs=[VMEM] * 6,
    )(
        me.reshape(1),
        *from_hbm(routes.T, branch.reshape(1, -1), neighbours.T, gcm_state.T),
        own,
        *from_hbm(crm_state),
    )


def cloud_steps(capacity, arrived, first, grown, sums):
    blocks, crm_levels, count = first.shape[:3]
    cells = crm_levels * count * 8 * blocks * LANES
    return call(
        functools.partial(cloud_kernel, capacity),
        (
            pltpu.VMEM(first.shape, F32),
            pltpu.VMEM((blocks, crm_levels, LANES), F32),
            pltpu.VMEM((blocks, 1, LANES), F32),
            pltpu.VMEM((blocks, 1, LANES), F32),
            jax.ShapeDtypeStruct(arrived.shape, F32),
        ),
        [pltpu.VMEM(sums.shape, F32), pltpu.VMEM((blocks, crm_levels * 8, LANES), F32)],
        (cells * 30, cells * 8, cells * 6),
        in_specs=[VMEM] * 4,
        out_specs=[VMEM] * 5,
    )(arrived, first, grown, sums)


def cloud_after(crm_state, last, force, code, rain):
    _, crm_levels, width, slots = crm_state.shape
    blocks = slots // LANES
    pieces = 1
    cells = crm_levels * width * slots
    return call(
        after_kernel,
        (jax.ShapeDtypeStruct(crm_state.shape, F32), jax.ShapeDtypeStruct((blocks, 1, LANES), F32)),
        [pltpu.VMEM((blocks, 2, crm_levels, width, LANES), F32)] * 2
        + [
            pltpu.VMEM((blocks, crm_levels, LANES), F32),
            pltpu.VMEM((2, crm_levels, LANES), F32),
            pltpu.VMEM((2,) + last.shape[1:], F32),
        ]
        + [pltpu.SemaphoreType.DMA((blocks, pieces))] * 2,
        (cells * 10, cells * 8, 0),
        in_specs=[HBM] + [VMEM] * 4,
        out_specs=[HBM, VMEM],
    )(*from_hbm(crm_state), last, force, code, rain)


def on_device(gcm_state, edge_part, neighbours, branch, routes, crm_state):
    peers = lax.axis_size(AXES)
    me = lax.axis_index(AXES)
    columns, features = gcm_state.shape
    _, crm_levels, _, slots = crm_state.shape
    capacity = slots // peers
    rows = slots // 2
    shape = jax.ShapeDtypeStruct

    own = call(edges_kernel, shape((crm_levels, columns), F32), cost=(1e7, 4e5, 0))(
        *from_hbm(edge_part)
    )
    other = lax.ppermute(own, AXES, [(i, (((i + 1) ^ 1) - 1) % peers) for i in range(peers)])
    pair = lax.ppermute(own, AXES, [(i, i ^ 1) for i in range(peers)])
    position, base, halo_map, first, grown, sums = before(
        peers, capacity, me, routes, branch, neighbours, gcm_state, own, crm_state
    )
    outgoing = call(outgoing_kernel, shape((rows, LANES), F32), cost=(2e8, 1e6, 0))(base, halo_map, other, pair)
    arrived = lax.all_to_all(outgoing.reshape(peers, capacity // 2, LANES), AXES, 0, 0, tiled=True)
    last, force, code, rain, reply = cloud_steps(capacity, arrived.reshape(rows, LANES), first, grown, sums)
    returned = lax.all_to_all(reply.reshape(peers, capacity // 2, LANES), AXES, 0, 0, tiled=True)
    updated, rain = cloud_after(crm_state, last, force, code, rain)
    levels = features // NV
    tendency = call(
        functools.partial(tendency_kernel, crm_levels),
        shape((features, columns), F32),
        [pltpu.VMEM((NV, levels, columns), F32), pltpu.SemaphoreType.DMA((NV,))],
        (1e8, 1e6, 0),
        in_specs=[VMEM] * 2,
        out_specs=HBM,
    )(position, returned.reshape(rows, LANES))
    return (tendency.T, updated, rain.reshape(1, slots))


def solution(mesh):
    in_specs = (
        P(AXES, None),
        P(AXES, None, None),
        P(AXES, None),
        P(AXES),
        P(AXES, None),
        P(None, None, None, AXES),
    )
    out_specs = (
        P(AXES, None),
        P(None, None, None, AXES),
        P(AXES, None),
    )
    return jax.shard_map(
        on_device, mesh=mesh, in_specs=in_specs, out_specs=out_specs, check_vma=False
    )
```

```python
import functools

import jax
import jax.numpy as jnp
import numpy as np
from jax import lax
from jax.experimental import pallas as pl
from jax.experimental.pallas import tpu as pltpu
from jax.sharding import PartitionSpec as P

NV = 8
STEPS = 3
AXES = ("elem", "sub")
LANES = 128
HALF = 64
LOG2E = 1.4426950408889634
F32 = jnp.float32
BF16 = jnp.bfloat16
SMALL_RAIN = 0.2


def mixing(k):
    return (0.8 + 0.05 * k) * (1.0 if k % 2 == 0 else -1.0) / float(np.sqrt(float(NV)))


def interp(z, level, crm_levels, levels):
    position = z.astype(F32) * ((levels - 1) / (crm_levels - 1))
    return jnp.maximum(0.0, 1.0 - jnp.abs(position - level.astype(F32)))


def dot(a, b, contract):
    return lax.dot_general(
        a, b, ((contract[0:1], contract[1:2]), ((), ())),
        preferred_element_type=F32,
    )


def split(x):
    high = x.astype(BF16)
    return high, (x - high.astype(F32)).astype(BF16)


def dot_in_three(a, b, contract):
    high, low = split(b)
    parts = both_halves(a)
    rows = a.shape[0]
    first = dot(parts, high, contract)
    return first[:rows] + first[rows:] + dot(parts[:rows], low, contract)


def both_halves(x):
    high = x.astype(BF16).astype(F32)
    return jnp.concatenate([high, x - high], axis=0).astype(BF16)


def slot_rows(onehot, fields):
    product = dot(onehot, both_halves(fields), (1, 1))
    product = product + pltpu.roll(product, HALF, 1)
    rows = product.shape[0] // 2
    return jnp.where(iota((rows, 2 * HALF), 1) < HALF, product[:rows], product[rows:])


def padded(fields):
    return jnp.concatenate([fields, jnp.zeros((HALF - fields.shape[0], fields.shape[1]), F32)], axis=0)


def iota(shape, dim):
    return lax.broadcasted_iota(jnp.int32, shape, dim)


def edges_kernel(edge_ref, out_ref):
    crm_levels = out_ref.shape[0]
    shape = (crm_levels, edge_ref.shape[2])
    levels = shape[1] // 2
    lane = iota(shape, 1)
    weight = jnp.where(
        lane < levels,
        mixing(0) * interp(iota(shape, 0), lane, crm_levels, levels),
        mixing(1) * interp(iota(shape, 0), lane - levels, crm_levels, levels),
    )
    out_ref[...] = dot_in_three(weight, edge_ref[...].reshape(-1, shape[1]), (1, 1))


def outgoing_kernel(base_ref, map_ref, other_ref, pair_ref, out_ref):
    window = jnp.concatenate([pair_ref[...], other_ref[...]], axis=1)
    out_ref[...] = base_ref[...] + slot_rows(map_ref[...], padded(window))


class Field:
    def __init__(self, total):
        self.total, self.rows, self.diagonals = total, [], []

    def five(self, z):
        while len(self.diagonals) < z + 2:
            at = len(self.diagonals)
            below, here = self.rows[max(at - 1, 0)], self.rows[min(at, self.total - 1)]
            right = here[1:] + [pltpu.roll(here[0], 7, 0)]
            self.diagonals.append([a + b for a, b in zip(below, right)])
        low, high = self.diagonals[z], self.diagonals[z + 1]
        high = [pltpu.roll(high[-1], 1, 0)] + high[:-1]
        return [row + (a + b) for row, a, b in zip(self.rows[z], low, high)]


def five_points(row, up, down):
    left = [pltpu.roll(row[-1], 1, 0)] + row[:-1]
    right = row[1:] + [pltpu.roll(row[0], 7, 0)]
    return [(a + b + c) + (d + e) for a, b, c, d, e in zip(row, left, right, up, down)]


def add_up(values):
    while len(values) > 1:
        values = [a + b for a, b in zip(values[::2], values[1::2])]
    return values[0]


def rows_of_sums(ref, crm_levels):
    return add_up([ref[pl.ds(s, crm_levels, stride=8), :] for s in range(8)])


def saturation(z, crm_levels):
    return 1.0 - z * (2.0 / (crm_levels - 1))


def levels_of(crm_levels):
    return iota((crm_levels, LANES), 0)


def shifted(x):
    return jnp.concatenate([x[:1], x[:-1]], axis=0) + jnp.concatenate([x[1:], x[-1:]], axis=0)


def route(peers, capacity, me_ref, routes_ref, branch_ref, neigh_ref, gcm_ref, own_ref,
          pos_ref, base_ref, halo_map_ref):
    columns = routes_ref.shape[1]
    elems = columns // 4
    crm_levels = own_ref.shape[0]
    slots = peers * capacity
    half = capacity // 2
    me = me_ref[0]
    destination = routes_ref[...]
    named = iota((peers, columns), 0) == destination
    earlier = (iota((columns, columns), 0) < iota((columns, columns), 1)).astype(BF16)
    before = dot(named.astype(BF16), earlier, (1, 0))
    rank = jnp.sum(jnp.where(named, before, 0.0), axis=0, keepdims=True).astype(jnp.int32)
    upper = (rank >= half).astype(jnp.int32)
    position = upper * (slots // 2) + destination * half + rank - upper * half
    pos_ref[...] = position
    place = (iota((slots, columns), 0) == position).astype(BF16)

    target = jnp.concatenate([neigh_ref[j : j + 1, :] for j in range(4)], axis=1)
    owner = target // columns
    edge = target - owner * columns
    block = jnp.where(owner == me, 0, jnp.where(owner == (me ^ 1), 1, 2))
    source = block * columns + edge
    window = iota((3 * columns, columns), 0)
    local = iota((1, columns), 1)
    local = 4 * (local % elems) + local // elems
    chosen = (window == source).astype(F32) + (window == local).astype(F32)
    column = iota((columns, columns), 0)
    row = iota((columns, columns), 1)
    first = (column % 4) * elems + column // 4
    second = ((column + 1) % 4) * elems + column // 4
    pair = ((row == first) | (row == second)).astype(BF16)
    mapped = dot(pair, chosen.astype(BF16), (1, 1)).astype(BF16)
    halo_map_ref[...] = (0.25 * dot(place, mapped[:, columns:], (1, 0))).astype(BF16)

    levels = gcm_ref.shape[0] // NV
    mixed = mixing(0) * gcm_ref[:levels, :]
    for k in range(1, NV):
        mixed += mixing(k) * gcm_ref[pl.ds(k * levels, levels), :]
    shape = (crm_levels, levels)
    force = dot_in_three(interp(iota(shape, 0), iota(shape, 1), crm_levels, levels), mixed, (1, 0))
    for part in split(own_ref[...]):
        force += 0.25 * dot(part, mapped[:, :columns], (1, 1))
    code = (branch_ref[...] + 1).astype(F32)
    base_ref[...] = slot_rows(place, padded(jnp.concatenate([force, code], axis=0)))


def before_kernel(peers, capacity, me_ref, routes_ref, branch_ref, neigh_ref, gcm_ref, own_ref, state_ref,
                  pos_ref, base_ref, halo_map_ref, first_ref, grown_ref, sums_ref,
                  near_routes_ref, near_branch_ref, near_neigh_ref, near_gcm_ref, kept_ref, part_ref, sems):
    blocks, _, crm_levels, width, _ = kept_ref.shape
    count = width // 8

    def copy(j):
        lanes = pl.ds(pl.multiple_of(j * LANES, LANES), LANES)
        return pltpu.make_async_copy(state_ref.at[:, :, :, lanes], kept_ref.at[j], sems.at[j])

    near = (near_routes_ref, near_branch_ref, near_neigh_ref, near_gcm_ref)
    loads = [
        pltpu.make_async_copy(far_ref, near_ref, sems.at[blocks + i])
        for i, (far_ref, near_ref) in enumerate(zip((routes_ref, branch_ref, neigh_ref, gcm_ref), near))
    ]
    for load in loads:
        load.start()
    for j in range(blocks):
        copy(j).start()
    for load in loads:
        load.wait()
    route(peers, capacity, me_ref, *near, own_ref, pos_ref, base_ref, halo_map_ref)

    def block(j, _):
        copy(j).wait()
        dry = Field(crm_levels)
        for i in range(crm_levels + 1):
            if i < crm_levels:
                heat = [kept_ref[j, 0, i, pl.ds(k, 8, stride=count), :] for k in range(count)]
                moist = [kept_ref[j, 1, i, pl.ds(k, 8, stride=count), :] for k in range(count)]
                dry.rows.append([m - 0.3 * h for h, m in zip(heat, moist)])
                part_ref[0, pl.ds(8 * i, 8), :] = add_up(dry.rows[i])
                part_ref[1, pl.ds(8 * i, 8), :] = add_up(heat)
            if i:
                for k, total in enumerate(dry.five(i - 1)):
                    first_ref[j, i - 1, k] = (0.2 * LOG2E) * total
                    grown_ref[j, i - 1, k] = jnp.exp2((0.2 * LOG2E) * total)
        level = saturation(levels_of(crm_levels).astype(F32), crm_levels)
        dry_mean = rows_of_sums(part_ref.at[0], crm_levels) * (1.0 / width)
        start = dry_mean + rows_of_sums(part_ref.at[1], crm_levels) * (2.3 / width)
        q = start
        for _ in range(STEPS):
            q = 0.6 * q + 0.2 * shifted(q)
        sums_ref[j, 0] = LOG2E * (dry_mean - level)
        sums_ref[j, 1] = q - start
        return 0

    lax.fori_loop(0, blocks, block, 0)


def lane_maps(rows, capacity):
    half = capacity // 2
    row = iota((rows, LANES), 0)
    slot = iota((rows, LANES), 1)
    rank = slot % capacity
    low = (row == (slot // capacity) * half + rank) & (rank < half)
    high = (row == (slot // capacity) * half + rank - half) & (rank >= half)
    return low.astype(BF16), high.astype(BF16)


def bounds(crm_levels):
    level = levels_of(crm_levels)
    edge = (0.4 / (crm_levels - 1)) * LOG2E
    return jnp.where(level == 0, -edge, 0.0) + jnp.where(level == crm_levels - 1, edge, 0.0)


def dried(crm_levels):
    return LOG2E * saturation(levels_of(crm_levels).astype(F32), crm_levels)


def respond(force):
    q = 0.5 * force
    for _ in range(STEPS - 1):
        q = 0.6 * q + 0.2 * shifted(q) + 0.5 * force
    return q


def rate_of(code):
    return 0.15 + 0.25 * (code == 2.0).astype(F32)


def cloud_kernel(capacity, arrived_ref, first_ref, grown_ref, sums_ref, last_ref, force_ref, code_ref, rain_ref,
                 reply_ref, push_ref, part_ref):
    blocks, crm_levels, count = last_ref.shape[:3]
    width = count * 8
    part = arrived_ref.shape[0] // blocks
    low, high = lane_maps(part, capacity)
    dry_end, wall = dried(crm_levels), bounds(crm_levels)
    maps = jnp.concatenate([low, high], axis=1)
    maps = jnp.concatenate([maps, maps], axis=0)
    for j in range(blocks):
        got = dot(both_halves(arrived_ref[pl.ds(j * part, part), :]), maps, (0, 0))
        got = got[:HALF, :LANES] + got[HALF:, LANES:]
        push = (-0.65 * LOG2E) * got[:crm_levels]
        push_ref[j, 0] = push - dry_end
        push_ref[j, 1] = push + wall
        force_ref[j] = got[:crm_levels]
        code_ref[j] = got[crm_levels : crm_levels + 1]

    def block(j, _):
        lowered = jnp.broadcast_to((1.15 * LOG2E) * rate_of(code_ref[j]), (8, LANES))
        fields = [Field(crm_levels) for _ in range(STEPS)]
        for i in range(crm_levels + 2 * (STEPS - 1)):
            for t in range(STEPS):
                z = i - 2 * t
                if not 0 <= z < crm_levels:
                    continue
                push = jnp.broadcast_to(push_ref[j, min(t, 1), pl.ds(z, 1), :], (8, LANES))
                if t == 0:
                    values = [first_ref[j, z, k] + push for k in range(count)]
                else:
                    values = [0.2 * total + push for total in fields[t - 1].five(z)]
                if t == 0:
                    factor = jnp.exp2(push)
                    powers = [factor * grown_ref[j, z, k] for k in range(count)]
                else:
                    powers = [jnp.exp2(y) for y in values]
                values = [y - lowered * jnp.log(1.0 + e) for y, e in zip(values, powers)]
                fields[t].rows.append(values)
                if t == STEPS - 1:
                    for k in range(count):
                        last_ref[j, z, k] = values[k]
                    part_ref[j, pl.ds(8 * z, 8), :] = add_up(values)
        return 0

    lax.fori_loop(0, blocks, block, 0)
    turned = jnp.concatenate([low, high], axis=0)
    for j in range(blocks):
        dg = rows_of_sums(part_ref.at[j], crm_levels) * (1.0 / width) - sums_ref[j, 0]
        answer = (0.7 / 2.3) * (sums_ref[j, 1] + respond(force_ref[j])) - (3.0 / (2.3 * LOG2E)) * dg
        reply_ref[pl.ds(j * part, part), :] = slot_rows(turned, padded(answer))
        budget = (-0.65 * LOG2E * STEPS) * force_ref[j] - dg
        rain = jnp.sum(budget, axis=0, keepdims=True) * (1.0 / (1.15 * LOG2E * crm_levels))
        rain_ref[j] = jnp.where(code_ref[j] > 0.0, rain, 0.0)


def after_kernel(state_ref, last_ref, force_ref, code_ref, guess_ref, out_ref, rain_ref,
                 kept_ref, new_ref, row_ref, push_ref, field_ref, sems, done_sems):
    blocks, _, crm_levels, width, _ = kept_ref.shape
    count = width // 8
    pieces = sems.shape[1]
    piece = crm_levels // pieces

    def lanes(j):
        return pl.ds(pl.multiple_of(j * LANES, LANES), LANES)

    def load(j, p):
        at = pl.ds(p * piece, piece)
        return pltpu.make_async_copy(
            state_ref.at[:, at, :, lanes(j)], kept_ref.at[j, :, at, :, :], sems.at[j, p]
        )

    def store(j, p):
        at = pl.ds(p * piece, piece)
        return pltpu.make_async_copy(
            new_ref.at[j, :, at, :, :], out_ref.at[:, at, :, lanes(j)], done_sems.at[j, p]
        )

    for j in range(blocks):
        for p in range(pieces):
            load(j, p).start()
    rain_ref[...] = guess_ref[...]
    for j in range(blocks):
        row_ref[j] = respond(force_ref[j])
    rows = [guess_ref[j] / rate_of(code_ref[j]) for j in range(blocks)]
    marks = [jnp.where(code_ref[j] > 0.0, row, -2.0) for j, row in enumerate(rows)]
    wettest = [jnp.max(mark, axis=1, keepdims=True) for mark in marks]
    dry = [((w > -1.0) & (w < SMALL_RAIN)).astype(jnp.int32) for w in wettest]
    some_dry = jnp.max(functools.reduce(jnp.maximum, dry)) > 0

    def block(j, _):
        occupied = jnp.broadcast_to(code_ref[j], (8, LANES)) > 0.0
        fields = [Field(crm_levels) for _ in range(STEPS + 1)]
        for i in range(crm_levels + STEPS):
            if i < crm_levels:
                if i % piece == 0:
                    load(j, i // piece).wait()
                heat = [kept_ref[j, 0, i, pl.ds(k, 8, stride=count), :] for k in range(count)]
                moist = [kept_ref[j, 1, i, pl.ds(k, 8, stride=count), :] for k in range(count)]
                fields[0].rows.append([(h + h) + m for h, m in zip(heat, moist)])
            for t in range(1, STEPS + 1):
                z = i - t
                if 0 <= z < crm_levels:
                    fields[t].rows.append(fields[t - 1].five(z))
            if not 0 <= z < crm_levels:
                continue
            row = jnp.broadcast_to(row_ref[j, pl.ds(z, 1), :], (8, LANES))
            for k, total in enumerate(fields[STEPS].rows[z]):
                at = pl.ds(k, 8, stride=count)
                linear = (1.0 / 125.0) * total + row
                dry = (1.0 / LOG2E) * last_ref[j, z, k] + saturation(z, crm_levels)
                heat = (1.0 / 2.3) * (linear - dry)
                moist = dry + 0.3 * heat
                new_ref[j, 0, z, at, :] = jnp.where(occupied, heat, kept_ref[j, 0, z, at, :])
                new_ref[j, 1, z, at, :] = jnp.where(occupied, moist, kept_ref[j, 1, z, at, :])
            if z % piece == piece - 1:
                store(j, z // piece).start()
        return 0

    lax.fori_loop(0, blocks, block, 0)

    def again(j, _):
        rate = rate_of(code_ref[j])
        lowered = jnp.broadcast_to((1.15 * LOG2E) * rate, (8, LANES))
        push = (-0.65 * LOG2E) * force_ref[j]
        push_ref[0] = push - dried(crm_levels)
        push_ref[1] = push + bounds(crm_levels)

        def condense(y, acc):
            e = jnp.exp2(y)
            amount = jnp.where(e < 2.0**-8, e * (1.0 - 0.5 * e), jnp.log(1.0 + e))
            return y - lowered * amount, acc + amount

        def start(z, _):
            for k in range(count):
                at = pl.ds(k, 8, stride=count)
                field_ref[0, z, k] = LOG2E * (kept_ref[j, 1, z, at, :] - 0.3 * kept_ref[j, 0, z, at, :])
            return 0

        def step(source, target, which):
            def body(z, acc):
                push = jnp.broadcast_to(push_ref[which, pl.ds(z, 1), :], (8, LANES))
                at = (z, jnp.maximum(z - 1, 0), jnp.minimum(z + 1, crm_levels - 1))
                totals = five_points(*[[field_ref[source, y, k] for k in range(count)] for y in at])
                new = []
                for k in range(count):
                    field_ref[target, z, k], total = condense(0.2 * totals[k] + push, acc[k])
                    new.append(total)
                return tuple(new)
            return body

        acc = tuple(jnp.zeros((8, LANES), F32) for _ in range(count))
        lax.fori_loop(0, crm_levels, start, 0)
        for t in range(STEPS):
            acc = lax.fori_loop(0, crm_levels, step(t % 2, (t + 1) % 2, min(t, 1)), acc)
        mean = jnp.sum(add_up(list(acc)), axis=0, keepdims=True) * (1.0 / (crm_levels * width))
        rain_ref[j] = jnp.where(code_ref[j] > 0.0, rate * mean, 0.0)
        return 0

    @pl.when(some_dry)
    def _():
        lax.fori_loop(0, blocks, again, 0)

    for j in range(blocks):
        for p in range(pieces):
            store(j, p).wait()


def tendency_kernel(crm_levels, pos_ref, returned_ref, out_ref, new_ref, sems):
    levels = out_ref.shape[0] // NV
    rows = returned_ref.shape[0]
    columns = pos_ref.shape[1]
    place = (iota((2 * rows, columns), 0) == pos_ref[...]).astype(BF16)
    shape = (levels, 2 * HALF)
    lane, level = iota(shape, 1), iota(shape, 0)
    table = [
        jnp.where((lane >= at) & (lane < at + crm_levels), interp(lane - at, level, crm_levels, levels), 0.0)
        for at in (0, HALF)
    ]
    spread = dot_in_three(jnp.concatenate(table, axis=0), returned_ref[...], (1, 1))
    parts = both_halves(jnp.concatenate([spread[:levels], spread[levels:]], axis=1))
    answer = dot(parts, place, (1, 0))
    answer = answer[:levels] + answer[levels:]
    copies = []
    for k in range(NV):
        new_ref[k] = mixing(k) * answer
        copies.append(
            pltpu.make_async_copy(new_ref.at[k], out_ref.at[pl.ds(k * levels, levels), :], sems.at[k])
        )
        copies[k].start()
    for copy in copies:
        copy.wait()


def call(kernel, out, scratch=(), cost=(0, 0, 0), vmem=32, **specs):
    return pl.pallas_call(
        kernel, out_shape=out, scratch_shapes=list(scratch),
        cost_estimate=pl.CostEstimate(flops=int(cost[0]), bytes_accessed=int(cost[1]), transcendentals=int(cost[2])),
        compiler_params=pltpu.CompilerParams(vmem_limit_bytes=vmem * 2**20), **specs,
    )


def from_hbm(*arrays):
    return [pltpu.with_memory_space_constraint(x, pltpu.HBM) for x in arrays]


HBM = pl.BlockSpec(memory_space=pltpu.HBM)
VMEM = pl.BlockSpec(memory_space=pltpu.VMEM)


def before(peers, capacity, me, routes, branch, neighbours, gcm_state, own, crm_state):
    _, crm_levels, width, slots = crm_state.shape
    columns = routes.shape[0]
    blocks = slots // LANES
    cells = crm_levels * width * slots
    return call(
        functools.partial(before_kernel, peers, capacity),
        (
            pltpu.VMEM((1, columns), jnp.int32),
            pltpu.VMEM((slots // 2, LANES), F32),
            pltpu.VMEM((slots, 2 * columns), BF16),
            pltpu.VMEM((blocks, crm_levels, width // 8, 8, LANES), F32),
            pltpu.VMEM((blocks, crm_levels, width // 8, 8, LANES), F32),
            pltpu.VMEM((blocks, 2, crm_levels, LANES), F32),
        ),
        [
            pltpu.VMEM((1, columns), jnp.int32),
            pltpu.VMEM((1, columns), jnp.int32),
            pltpu.VMEM((4, columns // 4), jnp.int32),
            pltpu.VMEM(gcm_state.shape[::-1], F32),
            pltpu.VMEM((blocks, 2, crm_levels, width, LANES), F32),
            pltpu.VMEM((2, crm_levels * 8, LANES), F32),
            pltpu.SemaphoreType.DMA((blocks + 4,)),
        ],
        (cells * 25 + 2e9, cells * 8 + 2e6, 0),
        in_specs=[pl.BlockSpec(memory_space=pltpu.SMEM)] + [HBM] * 4 + [VMEM, HBM],
        out_specs=[VMEM] * 6,
    )(
        me.reshape(1),
        *from_hbm(routes.T, branch.reshape(1, -1), neighbours.T, gcm_state.T),
        own,
        *from_hbm(crm_state),
    )


def cloud_steps(capacity, arrived, first, grown, sums):
    blocks, crm_levels, count = first.shape[:3]
    cells = crm_levels * count * 8 * blocks * LANES
    return call(
        functools.partial(cloud_kernel, capacity),
        (
            pltpu.VMEM(first.shape, F32),
            pltpu.VMEM((blocks, crm_levels, LANES), F32),
            pltpu.VMEM((blocks, 1, LANES), F32),
            pltpu.VMEM((blocks, 1, LANES), F32),
            jax.ShapeDtypeStruct(arrived.shape, F32),
        ),
        [pltpu.VMEM(sums.shape, F32), pltpu.VMEM((blocks, crm_levels * 8, LANES), F32)],
        (cells * 30, cells * 8, cells * 6),
        in_specs=[VMEM] * 4,
        out_specs=[VMEM] * 5,
    )(arrived, first, grown, sums)


def cloud_after(crm_state, last, force, code, rain):
    _, crm_levels, width, slots = crm_state.shape
    blocks = slots // LANES
    pieces = 1
    cells = crm_levels * width * slots
    return call(
        after_kernel,
        (jax.ShapeDtypeStruct(crm_state.shape, F32), jax.ShapeDtypeStruct((blocks, 1, LANES), F32)),
        [pltpu.VMEM((blocks, 2, crm_levels, width, LANES), F32)] * 2
        + [
            pltpu.VMEM((blocks, crm_levels, LANES), F32),
            pltpu.VMEM((2, crm_levels, LANES), F32),
            pltpu.VMEM((2,) + last.shape[1:], F32),
        ]
        + [pltpu.SemaphoreType.DMA((blocks, pieces))] * 2,
        (cells * 10, cells * 8, 0),
        in_specs=[HBM] + [VMEM] * 4,
        out_specs=[HBM, VMEM],
    )(*from_hbm(crm_state), last, force, code, rain)


def on_device(gcm_state, edge_part, neighbours, branch, routes, crm_state):
    peers = lax.axis_size(AXES)
    me = lax.axis_index(AXES)
    columns, features = gcm_state.shape
    _, crm_levels, _, slots = crm_state.shape
    capacity = slots // peers
    rows = slots // 2
    shape = jax.ShapeDtypeStruct

    own = call(edges_kernel, shape((crm_levels, columns), F32), cost=(1e7, 4e5, 0))(
        *from_hbm(edge_part)
    )
    other = lax.ppermute(own, AXES, [(i, (((i + 1) ^ 1) - 1) % peers) for i in range(peers)])
    pair = lax.ppermute(own, AXES, [(i, i ^ 1) for i in range(peers)])
    position, base, halo_map, first, grown, sums = before(
        peers, capacity, me, routes, branch, neighbours, gcm_state, own, crm_state
    )
    outgoing = call(outgoing_kernel, shape((rows, LANES), F32), cost=(2e8, 1e6, 0))(base, halo_map, other, pair)
    arrived = lax.all_to_all(outgoing.reshape(peers, capacity // 2, LANES), AXES, 0, 0, tiled=True)
    last, force, code, rain, reply = cloud_steps(capacity, arrived.reshape(rows, LANES), first, grown, sums)
    returned = lax.all_to_all(reply.reshape(peers, capacity // 2, LANES), AXES, 0, 0, tiled=True)
    updated, rain = cloud_after(crm_state, last, force, code, rain)
    levels = features // NV
    tendency = call(
        functools.partial(tendency_kernel, crm_levels),
        shape((features, columns), F32),
        [pltpu.VMEM((NV, levels, columns), F32), pltpu.SemaphoreType.DMA((NV,))],
        (1e8, 1e6, 0),
        in_specs=[VMEM] * 2,
        out_specs=HBM,
    )(position, returned.reshape(rows, LANES))
    return (tendency.T, updated, rain.reshape(1, slots))


def solution(mesh):
    in_specs = (
        P(AXES, None),
        P(AXES, None, None),
        P(AXES, None),
        P(AXES),
        P(AXES, None),
        P(None, None, None, AXES),
    )
    out_specs = (
        P(AXES, None),
        P(None, None, None, AXES),
        P(AXES, None),
    )
    return jax.shard_map(
        on_device, mesh=mesh, in_specs=in_specs, out_specs=out_specs, check_vma=False
    )
```
